256 devices in a mesh: dp: 2 (over core), ctx: 16 (over y, x), tensor: 8 (over z).
Axes of the slice: x: 4, y: 4, z: 8, core: 2. Of those that a mesh axis runs over, the one named last changes fastest.
Arguments:
- values: bfloat16 [2, 16, 3, 256, 8192], P('dp', 'ctx', None, None, 'tensor'), may hold values from -6 to 6
- step_sizes: bfloat16 [2, 16, 3, 128, 256], P('dp', 'ctx', None, 'tensor'), may hold values from 0 to 0.4, as said below
- write_map: bfloat16 [2, 16, 3, 256, 1024], P('dp', 'ctx', None, None, 'tensor'), may hold values from -6 to 6
- read_map: bfloat16 [2, 16, 3, 256, 1024], P('dp', 'ctx', None, None, 'tensor'), may hold values from -6 to 6
- decay_rates: float32 [128], P('tensor'), may hold values from 0.5 to 2
- skip_gain: float32 [128], P('tensor'), may hold values from 0.5 to 1.5
- routes: int32 [2, 16, 3], P('dp', 'ctx'), may hold values from -1 to 3, as said below
- segment_ids: int32 [2, 8192], P('dp', 'ctx'), may hold values from 0 to 2, never falling along the last dimension, each value on 1 to 4096 neighbouring positions
- grad_out: bfloat16 [2, 16, 2, 256, 8192], P('dp', 'ctx', None, None, 'tensor'), may hold values from -6 to 6
Outputs:
- output: bfloat16 [2, 16, 2, 256, 8192], P('dp', 'ctx', None, None, 'tensor')
- grad_values: bfloat16 [2, 16, 3, 256, 8192], P('dp', 'ctx', None, None, 'tensor')
- grad_steps: bfloat16 [2, 16, 3, 128, 256], P('dp', 'ctx', None, 'tensor')
- grad_write: bfloat16 [2, 16, 3, 256, 1024], P('dp', 'ctx', None, None, 'tensor')
- grad_read: bfloat16 [2, 16, 3, 256, 1024], P('dp', 'ctx', None, None, 'tensor')
The draws below stay inside these ranges and needn't reach their ends.
Inputs may be any that keep to these rules, and one draw needn't show every extreme that they name: `routes`: -1 marks an empty slot; every owner slot (j, c, s) is named by exactly one loader block of the same ctx index c; one loader device sends at most 2 blocks to one dp index, and some device of each ctx index has all 3 slots live. `segment_ids`: ids never fall along a stream; each document is a run of tokens, one of them exactly 4096 long. `step_sizes`: positive.
All inputs are finite; a program needn't handle non-finite values.
Results may differ from the reference program's by a relative error of at most 0.022.
Values may be sent and summed in bfloat16 or wider, within the bound.
No kernel may reach another device: no remote copies, remote signals or barrier semaphores. Data moves between devices by JAX's collectives and lax.ppermute only.
A program may use at most 128 MiB of HBM per device.

```python
import math
import jax
import jax.numpy as jnp
import numpy as np
from jax import lax

HEADS = 128
HEAD_DIM = 64
STATE = 128
GROUPS = 8
STRETCH = 256
DOCS = 3
OWN = 2
SRC = 3
WORDS_PER_SHARD = 8192
N_DP = 2
N_CTX = 16
N_TENSOR = 8


def draw_routes(key, part):
    key = jax.random.fold_in(key, 11)

    def per_context(subkey):
        split_seed_sequence = jax.random.split(subkey, 5)
        ranking = jax.random.permutation(split_seed_sequence[0], N_DP)
        shifts = jax.random.randint(split_seed_sequence[1], (N_DP // 2,), 0, OWN // 2 + 1)
        shifts = shifts.at[0].set(SRC - OWN)
        burden = jnp.full((N_DP,), OWN, jnp.int32)
        burden = burden.at[ranking[0::2]].add(shifts).at[ranking[1::2]].add(-shifts)
        offsets = jnp.cumsum(burden) - burden
        indices = jnp.arange(N_DP * OWN, dtype=jnp.int32)
        sender = jnp.sum((indices[:, None] >= offsets[None, :]).astype(jnp.int32), axis=1) - 1
        within = indices - offsets[sender]
        shuffle = jax.random.permutation(split_seed_sequence[2], N_DP)
        target = shuffle[indices % N_DP]
        slot_orders = jax.vmap(lambda inner_key: jax.random.permutation(inner_key, OWN))(jax.random.split(split_seed_sequence[3], N_DP))
        owner_slot = slot_orders[target, indices // N_DP]
        positions = jax.vmap(lambda inner_key: jax.random.permutation(inner_key, SRC))(jax.random.split(split_seed_sequence[4], N_DP))
        where_put = positions[sender, within]
        layout = jnp.full((N_DP, SRC), -1, jnp.int32)
        return layout.at[sender, where_put].set((target * OWN + owner_slot).astype(jnp.int32))
    tables = jax.vmap(per_context)(jax.random.split(key, N_CTX))
    return jnp.moveaxis(tables, 0, 1).astype(jnp.int32)


def draw_step_sizes(key, part):
    key = jax.random.fold_in(key, 5)
    split_seed_sequence = jax.random.split(key, 6)
    tensor_dimensions = (N_DP, N_CTX, SRC, HEADS, STRETCH)
    quick_share = 0.5
    rough_guess = jnp.exp(jax.random.uniform(split_seed_sequence[2], tensor_dimensions, jnp.float32, math.log(0.5), math.log(2.0)))
    quick = jax.random.bernoulli(split_seed_sequence[0], quick_share, (HEADS,))
    quick_base = jnp.exp(jax.random.uniform(split_seed_sequence[1], (HEADS,), jnp.float32, math.log(0.02), math.log(0.06)))
    slow_base = 0.25 / WORDS_PER_SHARD * jnp.exp(jax.random.uniform(split_seed_sequence[3], (HEADS,), jnp.float32, math.log(0.5), math.log(2.0)))
    baseline_amount = jnp.where(quick, quick_base, slow_base)
    sudden_spikes = jax.random.bernoulli(split_seed_sequence[4], 3.0 / WORDS_PER_SHARD, tensor_dimensions)
    abrupt_changes = jax.random.uniform(split_seed_sequence[5], tensor_dimensions, jnp.float32, 0.2, 0.38)
    return jnp.where(sudden_spikes, abrupt_changes, baseline_amount[:, None] * rough_guess).astype(jnp.bfloat16)


def level_of(own_key, extent, pieces, low, largest):
    def one(position, shards_of):
        heights = jax.random.uniform(jax.random.fold_in(jax.random.fold_in(own_key, 6), position), (shards_of,), jnp.float32, low / len(pieces), largest / len(pieces))
        return jnp.repeat(jnp.exp(heights), extent[position] // shards_of).reshape((-1,) + (1,) * (len(extent) - position - 1))

    loudness = one(*pieces[0])
    for cut in pieces[1:]:
        loudness = loudness * one(*cut)
    return loudness


def length_profile(amount, total, limit, slope):
    loads = [(1 << 20) // math.isqrt(grade ** slope) + 1 for grade in range(2, amount + 1)]
    spare, counts = total - limit - (amount - 1), [1] * (amount - 1)
    while spare > 0:
        free = [i for i in range(amount - 1) if counts[i] < limit]
        pool, left = sum([loads[i] for i in free]), spare
        for i in free:
            extra = min(limit - counts[i], max(1, left * loads[i] // pool), spare)
            counts[i] = counts[i] + extra
            spare = spare - extra
    return np.array([limit] + counts)


def uneven_parts(stream_key, number_of, total, limit, skew):
    if number_of == 2:
        one = jax.random.randint(stream_key, (), max(1, total - limit), min(limit, total - 1) + 1)
        return jnp.stack([one, total - one])
    tallies = jnp.asarray(length_profile(number_of, total, limit, skew), jnp.int32)
    pairs = (number_of - 1) // 2
    donor, taker = tallies[1:1 + 2 * pairs:2], tallies[2:2 + 2 * pairs:2]
    slack = jnp.minimum(donor - 1, limit - taker)
    passed = jax.random.randint(jax.random.fold_in(stream_key, 1), (pairs,), 0, 1 << 20) % (slack + 1)
    tallies = tallies.at[1:1 + 2 * pairs:2].set(donor - passed).at[2:2 + 2 * pairs:2].set(taker + passed)
    return tallies[jax.random.permutation(jax.random.fold_in(stream_key, 2), number_of)]


def centred(stream_key, extent, width, limit, pieces=(), kind=jnp.bfloat16):
    values = jax.random.normal(stream_key, extent, jnp.float32) * width
    if len(pieces) > 0:
        values = level_of(stream_key, extent, pieces, -0.22, 0.18) * values
    return jnp.clip(values, min=-limit, max=limit).astype(kind)


def setup_inputs(seed: int = 0) -> dict:
    arg_keys = jax.random.split(jax.random.key(seed), 10)
    values = centred(arg_keys[0], (N_DP, N_CTX, SRC, STRETCH, HEADS * HEAD_DIM), 1.0, 6.0, ((0, 2), (1, 16), (4, 8)))
    step_sizes = draw_step_sizes(jax.random.fold_in(arg_keys[9], 71), 0)
    write_map = centred(arg_keys[2], (N_DP, N_CTX, SRC, STRETCH, GROUPS * STATE), 1.0, 6.0, ((0, 2), (1, 16), (4, 8)))
    read_map = centred(arg_keys[3], (N_DP, N_CTX, SRC, STRETCH, GROUPS * STATE), 1.0, 6.0, ((0, 2), (1, 16), (4, 8)))
    decay_rates = jnp.clip(jnp.exp(math.log(2.0) - 1.3862944 * jax.random.uniform(arg_keys[4], (HEADS,), jnp.float32) ** level_of(arg_keys[4], (HEADS,), ((0, 8),), -0.2, 0.2)), 0.5, 2.0)
    skip_gain = jnp.clip(0.5 + 1.0 * jax.random.uniform(arg_keys[5], (HEADS,), jnp.float32) ** level_of(arg_keys[5], (HEADS,), ((0, 8),), -0.2, 0.2), 0.5, 1.5)
    routes = draw_routes(jax.random.fold_in(arg_keys[9], 71), 0)
    segment_ids = jax.vmap(lambda own: jnp.searchsorted(jnp.cumsum(uneven_parts(own, DOCS, WORDS_PER_SHARD, WORDS_PER_SHARD // 2, 0)), jnp.arange(WORDS_PER_SHARD), side="right"))(jax.random.split(arg_keys[7], N_DP)).reshape((N_DP, WORDS_PER_SHARD)).astype(jnp.int32)
    grad_out = centred(arg_keys[8], (N_DP, N_CTX, OWN, STRETCH, HEADS * HEAD_DIM), 1.0, 6.0, ((0, 2), (1, 16), (4, 8)))
    return {"values": values, "step_sizes": step_sizes, "write_map": write_map, "read_map": read_map, "decay_rates": decay_rates, "skip_gain": skip_gain, "routes": routes, "segment_ids": segment_ids, "grad_out": grad_out}


def decays(sizes, rates):
    return jnp.cumsum(-rates[None, :, :, None] * sizes.astype(jnp.float32), axis=-1)

def within_blocks(values, sizes, write_map, read_map, cumulative, segments, skip_grid):
    length = values.shape[1]
    places = jnp.arange(length)
    allowed = (segments[:, :, None] == segments[:, None, :]) & (places[:, None] >= places[None, :])[None]
    spread = cumulative[..., :, None] - cumulative[..., None, :]
    falloff = jnp.exp(jnp.where(allowed[:, None, None], spread, -jnp.inf))
    step_float = sizes.astype(jnp.float32)
    scores = jnp.einsum('kign,kjgn->kgij', read_map.astype(jnp.float32), write_map.astype(jnp.float32))
    weights = lax.optimization_barrier((falloff * scores[:, None] * step_float[..., None, :]).astype(jnp.bfloat16))
    inside = jnp.einsum('kqgij,kjqgp->kiqgp', weights.astype(jnp.float32), values.astype(jnp.float32))
    tail_mask = (segments == segments[:, -1:]).astype(jnp.float32)
    ending = jnp.exp(cumulative[..., -1:] - cumulative) * step_float * tail_mask[:, None, None, :]
    scaled = lax.optimization_barrier((values.astype(jnp.float32) * jnp.moveaxis(ending, -1, 1)[..., None]).astype(jnp.bfloat16))
    local_state = jnp.einsum('kjqgp,kjgn->kqgpn', scaled.astype(jnp.float32), write_map.astype(jnp.float32))
    carry_on = (segments[:, -1] == segments[:, 0]).astype(jnp.float32)[:, None, None] * jnp.exp(cumulative[..., -1])
    result = inside + skip_grid[None, None, :, :, None] * values.astype(jnp.float32)
    return (result, local_state, carry_on)

def across_blocks(read_map, cumulative, segments, state_used):
    head_mask = (segments == segments[:, :1]).astype(jnp.float32)
    entering = jnp.exp(cumulative) * head_mask[:, None, None, :]
    rounded = lax.optimization_barrier(state_used.astype(jnp.bfloat16))
    produced = jnp.einsum('kign,kqgpn->kiqgp', read_map.astype(jnp.float32), rounded.astype(jnp.float32))
    return produced * jnp.moveaxis(entering, -1, 1)[..., None]

def reference(values, step_sizes, write_map, read_map, decay_rates, skip_gain, routes, segment_ids, grad_out):
    stretches = N_CTX * OWN
    per_group = HEADS // (N_TENSOR * GROUPS)
    quarter = per_group * GROUPS
    owner_slots = N_DP * OWN
    source_lanes = jnp.moveaxis(routes, 1, 0).reshape(N_CTX, N_DP * SRC)
    target = jnp.where(source_lanes >= 0, source_lanes, owner_slots)
    sources = jnp.broadcast_to(jnp.arange(N_DP * SRC, dtype=jnp.int32)[None, :], (N_CTX, N_DP * SRC))
    context_rows = jnp.broadcast_to(jnp.arange(N_CTX, dtype=jnp.int32)[:, None], (N_CTX, N_DP * SRC))
    owner_of = jnp.zeros((N_CTX, owner_slots), jnp.int32).at[context_rows, target].set(sources, mode='drop')
    context_grid = jnp.broadcast_to(jnp.arange(N_CTX, dtype=jnp.int32)[:, None], (N_CTX, OWN))
    rate_parts = decay_rates.reshape(N_TENSOR, per_group, GROUPS)
    skip_parts = skip_gain.reshape(N_TENSOR, per_group, GROUPS)

    def stream(index):
        chosen = lax.dynamic_slice_in_dim(owner_of, index * OWN, OWN, 1)
        from_dp = chosen // SRC
        from_slot = chosen % SRC
        stream_values = values[from_dp, context_grid, from_slot].reshape(stretches, STRETCH, N_TENSOR, quarter * HEAD_DIM)
        stream_steps = step_sizes[from_dp, context_grid, from_slot].reshape(stretches, N_TENSOR, quarter, STRETCH)
        stream_writes = write_map[from_dp, context_grid, from_slot].reshape(stretches, STRETCH, GROUPS, STATE)
        stream_reads = read_map[from_dp, context_grid, from_slot].reshape(stretches, STRETCH, GROUPS, STATE)
        stream_marks = segment_ids[index].reshape(stretches, STRETCH)
        cotangent = grad_out[index].reshape(stretches, STRETCH, N_TENSOR, quarter * HEAD_DIM)

        def quarter_pass(member):
            block_values = stream_values[:, :, member].reshape(stretches, STRETCH, per_group, GROUPS, HEAD_DIM)
            block_steps = stream_steps[:, member].reshape(stretches, per_group, GROUPS, STRETCH)
            block_grad = cotangent[:, :, member].reshape(stretches, STRETCH, per_group, GROUPS, HEAD_DIM).astype(jnp.float32)
            rate_grid = rate_parts[member]
            skip_grid = skip_parts[member]

            def stretch_step(carry, element):
                state_in, previous = carry
                stretch_values, stretch_steps, stretch_writes, stretch_reads, stretch_marks = element
                linked = (stretch_marks[0] == previous).astype(jnp.float32)
                cumulative = decays(stretch_steps[None], rate_grid)
                local_out, local_state, carry_on = within_blocks(stretch_values[None], stretch_steps[None], stretch_writes[None], stretch_reads[None], cumulative, stretch_marks[None], skip_grid)
                state_used = linked * state_in
                total = local_out + across_blocks(stretch_reads[None], cumulative, stretch_marks[None], state_used[None])
                state_out = carry_on[0][..., None, None] * state_used + local_state[0]
                return ((state_out, stretch_marks[-1]), total[0].astype(jnp.bfloat16))

            def forward(arg_values, arg_steps, arg_writes, arg_reads):
                start = (jnp.zeros((per_group, GROUPS, HEAD_DIM, STATE), jnp.float32), jnp.array(-1, jnp.int32))
                _, produced = lax.scan(jax.checkpoint(stretch_step), start, (arg_values, arg_steps, arg_writes, arg_reads, stream_marks))
                return produced
            produced, backward = jax.vjp(forward, block_values, block_steps, stream_writes, stream_reads)
            value_grad, step_grad, write_grad, read_grad = backward(block_grad.astype(produced.dtype))
            return (produced.reshape(stretches, STRETCH, quarter * HEAD_DIM), value_grad.reshape(stretches, STRETCH, quarter * HEAD_DIM), step_grad.reshape(stretches, quarter, STRETCH), write_grad.astype(jnp.float32), read_grad.astype(jnp.float32))
        results = lax.map(quarter_pass, jnp.arange(N_TENSOR))
        outputs = jnp.moveaxis(results[0], 0, 2).reshape(N_CTX, OWN, STRETCH, HEADS * HEAD_DIM)
        value_grad = jnp.moveaxis(results[1], 0, 2).reshape(N_CTX, OWN, STRETCH, HEADS * HEAD_DIM)
        step_grad = jnp.moveaxis(results[2], 0, 1).reshape(N_CTX, OWN, HEADS, STRETCH)
        write_grad = lax.optimization_barrier(jnp.sum(results[3], axis=0)).astype(jnp.bfloat16).reshape(N_CTX, OWN, STRETCH, GROUPS * STATE)
        read_grad = lax.optimization_barrier(jnp.sum(results[4], axis=0)).astype(jnp.bfloat16).reshape(N_CTX, OWN, STRETCH, GROUPS * STATE)
        return (outputs, value_grad, step_grad, write_grad, read_grad)
    outputs, value_own, step_own, write_own, read_own = lax.map(stream, jnp.arange(N_DP))
    occupied = routes >= 0
    clipped = jnp.where(occupied, routes, 0)
    target_dp = clipped // OWN
    target_slot = clipped % OWN
    context_ids = jnp.broadcast_to(jnp.arange(N_CTX, dtype=jnp.int32)[None, :, None], routes.shape)

    def settle(operand):
        gathered = operand[target_dp, context_ids, target_slot]
        return jnp.where(occupied[..., None, None], gathered, jnp.zeros((), operand.dtype))
    return (outputs, settle(value_own), settle(step_own), settle(write_own), settle(read_own))
```

```python
import math

import jax
import jax.numpy as jnp
from jax import lax
from jax.experimental import pallas as pl
from jax.experimental.pallas import tpu as pltpu
from jax.sharding import PartitionSpec as P

GROUPS = 8
CHUNK = 128
LOG2E = math.log2(math.e)
F32 = jnp.float32
BF16 = jnp.bfloat16
VMEM_LIMIT = 40 * 1024 * 1024
BLOCKED = -1e30

NN = (((1,), (0,)), ((), ()))
NT = (((1,), (1,)), ((), ()))
TN = (((0,), (0,)), ((), ()))


def dot(a, b, dims):
    return lax.dot_general(a, b, dims, preferred_element_type=F32)


def split_dot(a, b, dims):
    high = b.astype(BF16)
    low = (b - high.astype(F32)).astype(BF16)
    return dot(a, high, dims) + dot(a, low, dims)


def iota(shape, dim):
    return lax.broadcasted_iota(jnp.int32, shape, dim)


def as_mask(condition):
    return jnp.where(condition, 1.0, 0.0).astype(BF16)


def step_columns(steps, k):
    n = CHUNK
    first = jnp.broadcast_to(steps[2 * k : 2 * k + 1], (n, n)).astype(BF16)
    second = jnp.broadcast_to(steps[2 * k + 1 : 2 * k + 2], (n, n)).astype(BF16)
    lower = as_mask(iota((n, n), 0) >= iota((n, n), 1))
    eye = as_mask(iota((n, n), 0) == iota((n, n), 1))
    both = dot(
        jnp.concatenate([lower, eye], axis=0), jnp.concatenate([first, second], axis=0), NT
    )
    halves = jnp.concatenate([first[: n // 2], second[: n // 2]], axis=0)
    total = dot(halves, jnp.ones((n, n), BF16), NT)
    return both[:n, :n], both[:n, n:], both[n:, :n], both[n:, n:], total


def head_rows(k):
    rows, lanes = iota((8, CHUNK), 0), iota((8, CHUNK), 1)
    return as_mask(rows == 2 * k + (lanes >= CHUNK // 2).astype(jnp.int32))


def pick_maps_kernel(own_routes, peer_routes, place, ow, pw, orr, pr, w_out, r_out):
    target = place[0] * 2 + pl.program_id(0)
    mine = (own_routes[0] == target) | (own_routes[1] == target) | (own_routes[2] == target)
    w_out[...] = jnp.where(mine, ow[0], pw[0])
    r_out[...] = jnp.where(mine, orr[0], pr[0])


def slot_of(routes, target):
    return jnp.where(routes[1] == target, 1, jnp.where(routes[2] == target, 2, 0))


def own_slot(s, own_routes, peer_routes, place):
    return slot_of(own_routes, place[0] * 2 + s)


def peer_slot(s, own_routes, peer_routes, place):
    return slot_of(peer_routes, place[0] * 2 + s)


def pick_maps(own_routes, peer_routes, place, write, read, peer_write, peer_read):
    length, state = write.shape[1:]
    own = pl.BlockSpec((1, length, state), lambda s, *r: (own_slot(s, *r), 0, 0))
    peer = pl.BlockSpec((1, length, state), lambda s, *r: (peer_slot(s, *r), 0, 0))
    out = pl.BlockSpec((length, state), lambda s, *r: (s, 0))
    return pl.pallas_call(
        pick_maps_kernel,
        grid_spec=pltpu.PrefetchScalarGridSpec(
            num_scalar_prefetch=3, grid=(2,), in_specs=[own, peer, own, peer], out_specs=[out, out]
        ),
        out_shape=[jax.ShapeDtypeStruct((2 * length, state), BF16)] * 2,
        name="pick_maps",
    )(own_routes, peer_routes, place, write, peer_write, read, peer_read)


def to_groups(block, out):
    half = CHUNK // 2
    for g in range(GROUPS):
        a = block[:, g * half : (g + 1) * half]
        b = block[:, (GROUPS + g) * half : (GROUPS + g + 1) * half]
        out[g] = jnp.concatenate([a, b], axis=1)


def pick_values_kernel(
    own_routes, peer_routes, place, ox, px, os, ps, dy, x_out, s_out, dy_out
):
    target = place[0] * 2 + pl.program_id(0)
    mine = (own_routes[0] == target) | (own_routes[1] == target) | (own_routes[2] == target)
    s_out[0] = jnp.where(mine, os[0].astype(F32), ps[0].astype(F32))
    to_groups(dy[0], dy_out)

    @pl.when(mine)
    def _():
        to_groups(ox[0], x_out)

    @pl.when(jnp.logical_not(mine))
    def _():
        to_groups(px[0], x_out)


def pick_values(own_routes, peer_routes, place, values, peer_values, steps, peer_steps, upstream):
    length, columns = values.shape[1:]
    heads = steps.shape[1]
    own = lambda s, *r: (own_slot(s, *r), 0, 0)
    peer = lambda s, *r: (peer_slot(s, *r), 0, 0)
    plain = lambda s, *r: (s, 0, 0)
    grouped = pl.BlockSpec((GROUPS, length, CHUNK), lambda s, *r: (0, s, 0))
    return pl.pallas_call(
        pick_values_kernel,
        grid_spec=pltpu.PrefetchScalarGridSpec(
            num_scalar_prefetch=3,
            grid=(2,),
            in_specs=[
                pl.BlockSpec((1, length, columns), own),
                pl.BlockSpec((1, length, columns), peer),
                pl.BlockSpec((1, heads, length), own),
                pl.BlockSpec((1, heads, length), peer),
                pl.BlockSpec((1, length, columns), plain),
            ],
            out_specs=[grouped, pl.BlockSpec((1, heads, length), plain), grouped],
        ),
        out_shape=[
            jax.ShapeDtypeStruct((GROUPS, 2 * length, CHUNK), BF16),
            jax.ShapeDtypeStruct((2, heads, length), F32),
            jax.ShapeDtypeStruct((GROUPS, 2 * length, CHUNK), BF16),
        ],
        compiler_params=pltpu.CompilerParams(vmem_limit_bytes=VMEM_LIMIT),
        name="pick_values",
    )(own_routes, peer_routes, place, values, peer_values, steps, peer_steps, upstream)


def local_kernel(
    group, rates, flags, write, read, x_in, dy_in, steps_in, bias, enter, leave,
    y_out, dx_out, dw_out, dr_out, local_out, direct_out, rows_out, send_out,
):
    n, half = CHUNK, CHUNK // 2
    g = group[0]
    rate_a, rate_b = -rates[g] * LOG2E, -rates[GROUPS + g] * LOG2E
    steps = steps_in[0]
    low = iota((n, n), 1) < half
    rate_lanes = jnp.where(low, rate_a, rate_b)
    rate_rows = jnp.where(iota((n, n), 0) < half, rate_a, rate_b)
    upper = as_mask(iota((n, n), 0) <= iota((n, n), 1))
    u_rows = dot(steps.astype(BF16), upper, NN) * jnp.where(
        iota((8, n), 0) % 2 == 0, rate_a, rate_b
    )
    sums = jnp.zeros((8, n), F32)
    locals_, directs, spans = [], [], []
    for k in range(4):
        at = slice(k * n, (k + 1) * n)
        b, c = write[at], read[at]
        x, dy = x_in[0, at], dy_in[0, at]
        dyf = dy.astype(F32)
        cum_a, cum_b, step_a, step_b, total = step_columns(steps, k)
        mask = bias[at]
        fall_a = jnp.exp2(cum_a * rate_a - u_rows[2 * k : 2 * k + 1] + mask)
        fall_b = jnp.exp2(cum_b * rate_b - u_rows[2 * k + 1 : 2 * k + 2] + mask)
        scores = dot(c, b, NT)
        weights = jnp.concatenate([fall_a * scores, fall_b * scores], axis=1).astype(BF16)
        stepped = x.astype(F32) * jnp.where(low, step_a, step_b)
        pair = jnp.concatenate(
            [jnp.where(low, stepped, 0.0), jnp.where(low, 0.0, stepped)], axis=0
        ).astype(BF16)
        inside = dot(weights, pair, NN)
        d_weights = dot(dy, pair, NT)
        d_scores = (d_weights[:, :n] * fall_a + d_weights[:, n:] * fall_b).astype(BF16)
        d_pair = dot(weights, dy, TN)
        d_x = jnp.where(low, d_pair[:n], d_pair[n:])
        y_out[at] = inside
        dx_out[at] = d_x
        dr_out[at] = dot(d_scores, b, NN)
        dw_out[at] = dot(d_scores, c, TN)
        rounded = stepped.astype(BF16).astype(F32)
        sums = sums + split_dot(head_rows(k), dyf * inside - rounded * d_x, NT)
        u = jnp.where(low, cum_a, cum_b) * rate_lanes
        into = jnp.exp2(u + enter[at])
        out_of = jnp.exp2(u[n - 1 : n] - u + leave[at])
        locals_.append(dot((rounded * out_of).astype(BF16), b, TN))
        directs.append(dot((dyf * into).astype(BF16), c, TN))
        spans.append(jnp.exp2(total * rate_rows) * flags[4 + k])
        local_out[at] = locals_[k]
        direct_out[at] = directs[k]
    rows_out[0] = sums
    end, span = locals_[0], spans[0]
    for k in range(1, 4):
        factor = spans[k] * flags[k]
        end = factor * end + locals_[k]
        span = factor * span
    begin = directs[3]
    for k in (2, 1, 0):
        begin = flags[k + 1] * spans[k] * begin + directs[k]
    row = iota((16, n), 0)
    for q in range(2):
        part = slice(q * half, (q + 1) * half)
        send_out[q, :half] = end[part].astype(BF16)
        send_out[q, half:n] = begin[part].astype(BF16)
        one = span[q * half : q * half + 1]
        rest = one - one.astype(BF16).astype(F32)
        meta = jnp.where(row == 0, one, jnp.where(row == 1, rest, jnp.where(row == 2, flags[0], 0.0)))
        send_out[q, n:] = meta.astype(BF16)


def smem():
    return pl.BlockSpec(memory_space=pltpu.SMEM)


def whole(shape):
    return pl.BlockSpec(shape, lambda i, g: (0,) * len(shape))


def by_group(shape):
    return pl.BlockSpec((1,) + shape, lambda i, g: (g[0],) + (0,) * len(shape))


def local_part(group, rates, flags, write, read, x, dy, steps, bias, enter, leave):
    tokens = write.shape[0]
    flat = whole((tokens, CHUNK))
    wide = jax.ShapeDtypeStruct((tokens, CHUNK), F32)
    return pl.pallas_call(
        local_kernel,
        grid_spec=pltpu.PrefetchScalarGridSpec(
            num_scalar_prefetch=1,
            grid=(1,),
            in_specs=[smem(), smem(), flat, flat, by_group((tokens, CHUNK)), by_group((tokens, CHUNK)),
                      by_group((8, CHUNK)), flat, flat, flat],
            out_specs=[flat] * 6 + [whole((1, 8, CHUNK)), whole((2, CHUNK + 16, CHUNK))],
        ),
        out_shape=[wide] * 6
        + [
            jax.ShapeDtypeStruct((1, 8, CHUNK), F32),
            jax.ShapeDtypeStruct((2, CHUNK + 16, CHUNK), BF16),
        ],
        compiler_params=pltpu.CompilerParams(vmem_limit_bytes=VMEM_LIMIT),
        cost_estimate=pl.CostEstimate(flops=300_000_000, bytes_accessed=3_000_000, transcendentals=400_000),
        name="local_part",
    )(group, rates, flags, write, read, x, dy, steps, bias, enter, leave)


def scan_kernel(got, out):
    half = CHUNK // 2
    count = got.shape[0]

    def factors(i):
        meta = got[i, CHUNK:].astype(F32)
        return (meta[0:1] + meta[1:2]), meta[2:3]

    state = jnp.zeros((half, CHUNK), F32)
    for i in range(count):
        span, link = factors(i)
        out[i, :half] = state.astype(BF16)
        state = span * link * state + got[i, :half].astype(F32)
    state = jnp.zeros((half, CHUNK), F32)
    for i in range(count - 1, -1, -1):
        span, link = factors(i)
        out[i, half:] = state.astype(BF16)
        state = link * (span * state + got[i, half:CHUNK].astype(F32))


def scan_states(got):
    return pl.pallas_call(
        scan_kernel,
        out_shape=jax.ShapeDtypeStruct((got.shape[0], CHUNK, CHUNK), BF16),
        compiler_params=pltpu.CompilerParams(vmem_limit_bytes=VMEM_LIMIT),
        name="scan_states",
    )(got)


def final_kernel(
    group, rates, gains, flags, states, write, read, x_in, dy_in, steps_in, enter, leave,
    y_in, dx_in, dw_in, dr_in, local_in, direct_in, rows_in,
    y_out, dx_out, ds_out, dw_out, dr_out,
):
    n, half = CHUNK, CHUNK // 2
    g = group[0]
    rate_a, rate_b = -rates[g] * LOG2E, -rates[GROUPS + g] * LOG2E
    steps = steps_in[0]
    low = iota((n, n), 1) < half
    rate_lanes = jnp.where(low, rate_a, rate_b)
    gain_lanes = jnp.where(low, gains[g], gains[GROUPS + g])
    rate_rows = jnp.where(iota((n, n), 0) < half, rate_a, rate_b)
    columns = [step_columns(steps, k) for k in range(4)]
    spans = [jnp.exp2(columns[k][4] * rate_rows) * flags[4 + k] for k in range(4)]
    state = flags[0] * jnp.concatenate([states[0, :half], states[1, :half]], axis=0).astype(F32)
    used = [state]
    for k in range(3):
        state = flags[k + 1] * (spans[k] * state + local_in[k * n : (k + 1) * n])
        used.append(state)
    after = jnp.concatenate([states[0, half:], states[1, half:]], axis=0).astype(F32)
    wanted = [after]
    for k in (3, 2, 1):
        after = flags[k] * (spans[k] * after + direct_in[k * n : (k + 1) * n])
        wanted.insert(0, after)
    sums = rows_in[0]
    from_before = jnp.zeros((8, n), F32)
    from_all = jnp.zeros((8, n), F32)
    straight = jnp.zeros((8, n), F32)
    for k in range(4):
        at = slice(k * n, (k + 1) * n)
        b, c = write[at], read[at]
        xf, dyf = x_in[0, at].astype(F32), dy_in[0, at].astype(F32)
        cum_a, cum_b, step_a, step_b, _ = columns[k]
        step = jnp.where(low, step_a, step_b)
        u = jnp.where(low, cum_a, cum_b) * rate_lanes
        into = jnp.exp2(u + enter[at])
        out_of = jnp.exp2(u[n - 1 : n] - u + leave[at])
        rounded = (xf * step).astype(BF16).astype(F32)
        scaled = (rounded * out_of).astype(BF16)
        carried = (dyf * into).astype(BF16)
        state_b, after_b = used[k].astype(BF16), wanted[k].astype(BF16)
        cross = dot(c, state_b, NT) * into
        back = dot(b, after_b, NT) * out_of
        d_x = dx_in[at] + back
        y_out[0, at] = (y_in[at] + cross + gain_lanes * xf).astype(BF16)
        dx_out[0, at] = (step * d_x + gain_lanes * dyf).astype(BF16)
        dr_out[at] = (dr_in[at] + dot(carried, state_b, NN)).astype(BF16)
        dw_out[at] = (dw_in[at] + dot(scaled, after_b, NN)).astype(BF16)
        select = head_rows(k)
        sums = sums + split_dot(select, dyf * cross, NT)
        from_before = from_before + split_dot(select, rounded * back, NT)
        from_all = from_all + split_dot(select, spans[k] * wanted[k] * used[k], NN)
        straight = straight + split_dot(select, xf * d_x, NT)
    lower = as_mask(iota((n, n), 0) >= iota((n, n), 1))
    before = as_mask(iota((n, n), 0) < iota((n, n), 1))
    joined = jnp.concatenate([sums, from_before, from_all], axis=1)
    table = jnp.concatenate([lower, before, jnp.ones((n, n), BF16)], axis=0)
    high = joined.astype(BF16)
    rest = joined - high.astype(F32)
    middle = rest.astype(BF16)
    low_part = (rest - middle.astype(F32)).astype(BF16)
    d_rate = dot(high, table, NN) + dot(middle, table, NN) + dot(low_part, table, NN)
    rates8 = jnp.where(iota((8, n), 0) % 2 == 0, rates[g], rates[GROUPS + g])
    ds_out[0] = straight - rates8 * d_rate


def final_part(group, rates, gains, flags, states, write, read, x, dy, steps, enter, leave, parts):
    tokens = write.shape[0]
    flat = whole((tokens, CHUNK))
    y_in, dx_in, dw_in, dr_in, local_in, direct_in, rows_in = parts
    return pl.pallas_call(
        final_kernel,
        grid_spec=pltpu.PrefetchScalarGridSpec(
            num_scalar_prefetch=1,
            grid=(1,),
            in_specs=[smem(), smem(), smem(), whole((2, CHUNK, CHUNK)), flat, flat,
                      by_group((tokens, CHUNK)), by_group((tokens, CHUNK)), by_group((8, CHUNK)),
                      flat, flat] + [flat] * 6 + [whole((1, 8, CHUNK))],
            out_specs=[whole((1, tokens, CHUNK)), whole((1, tokens, CHUNK)), whole((1, 8, CHUNK)), flat, flat],
        ),
        out_shape=[
            jax.ShapeDtypeStruct((1, tokens, CHUNK), BF16),
            jax.ShapeDtypeStruct((1, tokens, CHUNK), BF16),
            jax.ShapeDtypeStruct((1, 8, CHUNK), F32),
            jax.ShapeDtypeStruct((tokens, CHUNK), BF16),
            jax.ShapeDtypeStruct((tokens, CHUNK), BF16),
        ],
        compiler_params=pltpu.CompilerParams(vmem_limit_bytes=VMEM_LIMIT),
        cost_estimate=pl.CostEstimate(flops=200_000_000, bytes_accessed=4_000_000, transcendentals=100_000),
        name="final_part",
    )(group, rates, gains, flags, states, write, read, x, dy, steps, enter, leave,
      y_in, dx_in, dw_in, dr_in, local_in, direct_in, rows_in)


def columns_kernel(order, y_in, dx_in, y_out, dx_out):
    half = CHUNK // 2
    for g in range(GROUPS):
        place = order[g]
        for src, dst in ((y_in, y_out), (dx_in, dx_out)):
            block = src[place]
            dst[0, :, g * half : (g + 1) * half] = block[:, :half]
            dst[0, :, (GROUPS + g) * half : (GROUPS + g + 1) * half] = block[:, half:]


def to_columns(order, y, dx):
    tokens = y.shape[1]
    length = tokens // 2
    columns = GROUPS * CHUNK
    grouped = pl.BlockSpec((GROUPS, length, CHUNK), lambda s, o: (0, s, 0))
    out = pl.BlockSpec((1, length, columns), lambda s, o: (s, 0, 0))
    return pl.pallas_call(
        columns_kernel,
        grid_spec=pltpu.PrefetchScalarGridSpec(
            num_scalar_prefetch=1, grid=(2,), in_specs=[grouped, grouped], out_specs=[out, out]
        ),
        out_shape=[jax.ShapeDtypeStruct((2, length, columns), BF16)] * 2,
        compiler_params=pltpu.CompilerParams(vmem_limit_bytes=VMEM_LIMIT),
        name="to_columns",
    )(order, y, dx)


def settle_kernel(routes, place, *refs):
    count = len(refs) // 3
    target = routes[pl.program_id(0)]
    mine = target // 2 == place[0]
    for i in range(count):
        own, peer, out = refs[2 * i], refs[2 * i + 1], refs[2 * count + i]
        chosen = jnp.where(mine, own[0], peer[0])
        out[0] = jnp.where(target >= 0, chosen, jnp.zeros_like(chosen))


def settle(routes, place, pairs):
    def slot(m, r, p):
        return (jnp.maximum(r[m], 0) % 2, 0, 0)

    in_specs, out_specs, shapes, operands = [], [], [], []
    for own, peer in pairs:
        block = (1,) + own.shape[1:]
        in_specs += [pl.BlockSpec(block, slot), pl.BlockSpec(block, slot)]
        out_specs.append(pl.BlockSpec(block, lambda m, r, p: (m, 0, 0)))
        shapes.append(jax.ShapeDtypeStruct((routes.shape[0],) + own.shape[1:], own.dtype))
        operands += [own, peer]
    return pl.pallas_call(
        settle_kernel,
        grid_spec=pltpu.PrefetchScalarGridSpec(
            num_scalar_prefetch=2, grid=(routes.shape[0],), in_specs=in_specs, out_specs=out_specs
        ),
        out_shape=shapes,
        compiler_params=pltpu.CompilerParams(vmem_limit_bytes=VMEM_LIMIT),
        name="settle",
    )(routes, place, *operands)


def shards(
    values, step_sizes, write_map, read_map, decay_rates, skip_gain, routes, segment_ids, grad_out
):
    values, step_sizes = values[0, 0], step_sizes[0, 0]
    write_map, read_map, grad_out = write_map[0, 0], read_map[0, 0], grad_out[0, 0]
    routes = routes[0, 0]
    ring = lax.axis_size("tensor")
    swap = [(0, 1), (1, 0)]
    right = [(i, (i + 1) % ring) for i in range(ring)]
    left = [(i, (i - 1) % ring) for i in range(ring)]
    me = lax.axis_index("tensor")
    place = lax.axis_index("dp").reshape(1)
    length = values.shape[1]

    def across(operand):
        return lax.ppermute(operand, "dp", swap)

    def go_right(operand):
        return lax.ppermute(operand, "tensor", right)

    def go_left(operand):
        return lax.ppermute(operand, "tensor", left)

    peer_routes = across(routes)
    peer_write, peer_read = across(write_map), across(read_map)
    write, read = pick_maps(routes, peer_routes, place, write_map, read_map, peer_write, peer_read)
    peer_values, peer_steps = across(values), across(step_sizes)

    ids = segment_ids[0].reshape(4, CHUNK)
    last_before = lax.ppermute(ids[3, CHUNK - 1 :], "ctx", [(i, i + 1) for i in range(lax.axis_size("ctx") - 1)])
    begins = jnp.where(
        lax.axis_index("ctx") > 0, (last_before == ids[0, :1]).astype(F32), jnp.zeros((1,), F32)
    )
    flags = jnp.concatenate(
        [
            begins,
            (ids[1:, 0] == ids[:-1, CHUNK - 1]).astype(F32),
            (ids[:, 0] == ids[:, CHUNK - 1]).astype(F32),
        ]
    )
    spots = jnp.arange(CHUNK)
    bias = jnp.where(
        (ids[:, :, None] == ids[:, None, :]) & (spots[:, None] >= spots[None, :]), 0.0, BLOCKED
    ).astype(F32).reshape(4 * CHUNK, CHUNK)

    def edge(column):
        marks = jnp.where(ids == column, 0.0, BLOCKED).astype(F32).reshape(-1, 1)
        return jnp.broadcast_to(marks, (4 * CHUNK, CHUNK))

    enter, leave = edge(ids[:, :1]), edge(ids[:, CHUNK - 1 :])

    x, steps, dy = pick_values(
        routes, peer_routes, place, values, peer_values, step_sizes, peer_steps, grad_out
    )
    steps = steps.reshape(2, 2, GROUPS, 2, CHUNK).transpose(2, 0, 3, 1, 4).reshape(GROUPS, 8, CHUNK)

    pieces = {0: (write, read)}
    w_right = w_left = write
    r_right = r_left = read
    for step in (1, 2, 3):
        w_right, r_left = go_right(w_right), go_left(r_left)
        r_right, w_left = go_right(r_right), go_left(w_left)
        pieces[-step] = (w_right, r_right)
        pieces[step] = (w_left, r_left)
    pieces[4] = (go_right(w_right), go_left(r_left))

    arrival = (0, -1, 1, -2, 2, -3, 3, 4)
    index = {d: ((me + d) % ring).reshape(1).astype(jnp.int32) for d in arrival}
    parts, sends = {}, []
    for d in arrival:
        *kept, sent = local_part(
            index[d], decay_rates, flags, *pieces[d], x, dy, steps, bias, enter, leave
        )
        parts[d] = kept
        sends.append(sent)
    got = lax.all_to_all(jnp.concatenate(sends, axis=0), "ctx", split_axis=0, concat_axis=0, tiled=True)
    states = lax.all_to_all(scan_states(got), "ctx", split_axis=0, concat_axis=0, tiled=True)

    outs = {}

    def finish(d):
        spot = 2 * arrival.index(d)
        outs[d] = final_part(
            index[d], decay_rates, skip_gain, flags, states[spot : spot + 2], *pieces[d],
            x, dy, steps, enter, leave, parts[d],
        )
        return outs[d][3], outs[d][4]

    def add(a, b):
        return (a.astype(F32) + b.astype(F32)).astype(BF16)

    w_right, r_left = finish(4)
    r_right = w_left = None
    for step in (3, 2, 1):
        w_right, r_left = go_right(w_right), go_left(r_left)
        if r_right is not None:
            r_right, w_left = go_right(r_right), go_left(w_left)
        w_up, r_up = finish(step)
        w_down, r_down = finish(-step)
        w_right, r_left = add(w_right, w_up), add(r_left, r_down)
        r_right = r_up if r_right is None else add(r_right, r_up)
        w_left = w_down if w_left is None else add(w_left, w_down)
    w_right, r_left = go_right(w_right), go_left(r_left)
    r_right, w_left = go_right(r_right), go_left(w_left)
    w_here, r_here = finish(0)

    def total(a, b, c):
        summed = a.astype(F32) + b.astype(F32) + c.astype(F32)
        return summed.astype(BF16).reshape(2, length, CHUNK)

    grad_write, grad_read = total(w_right, w_left, w_here), total(r_right, r_left, r_here)

    spots8 = jnp.array([arrival.index(d if d <= 4 else d - 8) for d in range(8)], jnp.int32)
    order = jnp.take(spots8, (jnp.arange(GROUPS) - me) % ring)
    y_all = jnp.concatenate([outs[d][0] for d in arrival], axis=0)
    dx_all = jnp.concatenate([outs[d][1] for d in arrival], axis=0)
    output, grad_values = to_columns(order, y_all, dx_all)
    ds_all = jnp.take(jnp.concatenate([outs[d][2] for d in arrival], axis=0), order, axis=0)
    grad_steps = (
        ds_all.reshape(GROUPS, 2, 2, 2, CHUNK)
        .transpose(1, 3, 0, 2, 4)
        .reshape(2, 2 * GROUPS, length)
        .astype(BF16)
    )
    back_values, back_steps = settle(
        routes, place, [(grad_values, across(grad_values)), (grad_steps, across(grad_steps))]
    )
    back_write, back_read = settle(
        routes, place, [(grad_write, across(grad_write)), (grad_read, across(grad_read))]
    )
    return tuple(
        array[None, None] for array in (output, back_values, back_steps, back_write, back_read)
    )


def solution(mesh):
    placed = (
        P("dp", "ctx", None, None, "tensor"),
        P("dp", "ctx", None, "tensor", None),
        P("dp", "ctx", None, None, "tensor"),
        P("dp", "ctx", None, None, "tensor"),
        P("tensor"),
        P("tensor"),
        P("dp", "ctx", None),
        P("dp", "ctx"),
        P("dp", "ctx", None, None, "tensor"),
    )
    return jax.shard_map(
        shards,
        mesh=mesh,
        in_specs=placed,
        out_specs=(
            P("dp", "ctx", None, None, "tensor"),
            P("dp", "ctx", None, None, "tensor"),
            P("dp", "ctx", None, "tensor", None),
            P("dp", "ctx", None, None, "tensor"),
            P("dp", "ctx", None, None, "tensor"),
        ),
        check_vma=False,
    )
```

```python
import functools
import math

import jax
import jax.numpy as jnp
from jax import lax
from jax.experimental import pallas as pl
from jax.experimental.pallas import tpu as pltpu
from jax.sharding import PartitionSpec as P

GROUPS = 8
CHUNK = 128
LOG2E = math.log2(math.e)
F32 = jnp.float32
BF16 = jnp.bfloat16
VMEM_LIMIT = 16 * 1024 * 1024
BLOCKED = -1e30
SMALL = pl.CostEstimate(flops=1000, bytes_accessed=1000, transcendentals=0)
HBM, VMEM = "hbm", "vmem"

NN = (((1,), (0,)), ((), ()))
NT = (((1,), (1,)), ((), ()))
TN = (((0,), (0,)), ((), ()))


def dot(a, b, dims):
    return lax.dot_general(a, b, dims, preferred_element_type=F32)


def split_dot(a, b, dims):
    high = b.astype(BF16)
    low = (b - high.astype(F32)).astype(BF16)
    return dot(a, high, dims) + dot(a, low, dims)


def iota(shape, dim):
    return lax.broadcasted_iota(jnp.int32, shape, dim)


def as_mask(condition):
    return jnp.where(condition, 1.0, 0.0).astype(BF16)


def step_rows(steps, k):
    n = CHUNK
    first = jnp.broadcast_to(steps[2 * k : 2 * k + 1], (n, n)).astype(BF16)
    second = jnp.broadcast_to(steps[2 * k + 1 : 2 * k + 2], (n, n)).astype(BF16)
    return first, second


def sums_and_steps():
    n = CHUNK
    lower = as_mask(iota((n, n), 0) >= iota((n, n), 1))
    eye = as_mask(iota((n, n), 0) == iota((n, n), 1))
    return jnp.concatenate([lower, eye], axis=0)


def step_columns(steps, k):
    n = CHUNK
    both = dot(sums_and_steps(), jnp.concatenate(step_rows(steps, k), axis=0), NT)
    return both[:n, :n], both[:n, n:], both[n:, :n], both[n:, n:]


def step_halves(steps, k):
    n = CHUNK
    first, second = step_rows(steps, k)
    halves = jnp.concatenate([first[: n // 2], second[: n // 2]], axis=0)
    both = dot(sums_and_steps(), halves, NT)
    return both[:n], both[n:], dot(halves, jnp.ones((n, n), BF16), NT)


def head_rows(k):
    rows, lanes = iota((8, CHUNK), 0), iota((8, CHUNK), 1)
    return as_mask(rows == 2 * k + (lanes >= CHUNK // 2).astype(jnp.int32))


def smem():
    return pl.BlockSpec(memory_space=pltpu.SMEM)


def vmem():
    return pl.BlockSpec(memory_space=pltpu.VMEM)


def hbm():
    return pl.BlockSpec(memory_space=pltpu.HBM)


def in_hbm(*arrays):
    return [pltpu.with_memory_space_constraint(array, pltpu.HBM) for array in arrays]


def hbm_out(shape, dtype):
    return pltpu.HBM(tuple(shape), dtype)


def slot_of(routes, target):
    slot = jnp.where(routes[1] == target, 1, jnp.where(routes[2] == target, 2, 0))
    return slot, (routes[0] == target) | (slot > 0)


def fetch(own_routes, peer_routes, place, s, own, peer, out, sem):
    target = place[0] * 2 + s
    own_slot, mine = slot_of(own_routes, target)
    peer_slot, _ = slot_of(peer_routes, target)

    @pl.when(mine)
    def _():
        pltpu.make_async_copy(own.at[own_slot], out, sem).start()

    @pl.when(jnp.logical_not(mine))
    def _():
        pltpu.make_async_copy(peer.at[peer_slot], out, sem).start()

    return pltpu.make_async_copy(own.at[0], out, sem)


def pick_maps_kernel(own_routes, peer_routes, place, ow, pw, orr, pr, out, sems):
    length = ow.shape[1]
    pending = []
    for s in range(2):
        for i, (own, peer) in enumerate(((ow, pw), (orr, pr))):
            part = out.at[i, s * length : (s + 1) * length]
            pending.append(
                fetch(own_routes, peer_routes, place, s, own, peer, part, sems.at[2 * s + i])
            )
    for copy in pending:
        copy.wait()


def pick_maps(own_routes, peer_routes, place, write, read, peer_write, peer_read):
    length, state = write.shape[1:]
    return pl.pallas_call(
        pick_maps_kernel,
        in_specs=[smem()] * 3 + [hbm()] * 4,
        out_specs=vmem(),
        out_shape=jax.ShapeDtypeStruct((2, 2 * length, state), BF16),
        scratch_shapes=[pltpu.SemaphoreType.DMA((4,))],
        compiler_params=pltpu.CompilerParams(vmem_limit_bytes=VMEM_LIMIT),
        name="pick_maps",
    )(own_routes, peer_routes, place, *in_hbm(write, peer_write, read, peer_read))


def to_groups(block, out):
    half = CHUNK // 2
    for g in range(GROUPS):
        a = block[:, g * half : (g + 1) * half]
        b = block[:, (GROUPS + g) * half : (GROUPS + g + 1) * half]
        out[g] = jnp.concatenate([a, b], axis=1)


def pick_values_kernel(
    own_routes, peer_routes, place, ox, px, os, ps, dy, x_out, s_out, dy_out,
    x_buf, s_buf, dy_buf, sems,
):
    length = ox.shape[1]
    pending = []
    for s in range(2):
        copy = pltpu.make_async_copy(dy.at[s], dy_buf.at[s], sems.at[3 * s])
        copy.start()
        steps = fetch(own_routes, peer_routes, place, s, os, ps, s_buf.at[s], sems.at[3 * s + 1])
        x = fetch(own_routes, peer_routes, place, s, ox, px, x_buf.at[s], sems.at[3 * s + 2])
        pending.append((copy, steps, x))
    for s in range(2):
        for copy in pending[s]:
            copy.wait()
        at = slice(s * length, (s + 1) * length)
        to_groups(dy_buf[s], dy_out.at[:, at])
        to_groups(x_buf[s], x_out.at[:, at])
        steps = s_buf[s].astype(F32)
        for q in range(2):
            for part in range(2):
                s_out[:, (2 * s + part) * 2 + q, :] = steps[
                    q * GROUPS : (q + 1) * GROUPS, part * CHUNK : (part + 1) * CHUNK
                ]


def pick_values(own_routes, peer_routes, place, values, peer_values, steps, peer_steps, upstream):
    length, columns = values.shape[1:]
    heads = steps.shape[1]
    return pl.pallas_call(
        pick_values_kernel,
        in_specs=[smem()] * 3 + [hbm()] * 5,
        out_specs=[vmem()] * 3,
        out_shape=[
            jax.ShapeDtypeStruct((GROUPS, 2 * length, CHUNK), BF16),
            jax.ShapeDtypeStruct((GROUPS, 8, CHUNK), F32),
            jax.ShapeDtypeStruct((GROUPS, 2 * length, CHUNK), BF16),
        ],
        scratch_shapes=[
            pltpu.VMEM((2, length, columns), BF16),
            pltpu.VMEM((2, heads, length), BF16),
            pltpu.VMEM((2, length, columns), BF16),
            pltpu.SemaphoreType.DMA((6,)),
        ],
        compiler_params=pltpu.CompilerParams(vmem_limit_bytes=VMEM_LIMIT),
        cost_estimate=SMALL,
        name="pick_values",
    )(
        own_routes, peer_routes, place,
        *in_hbm(values, peer_values, steps, peer_steps, upstream),
    )


def masks_kernel(ids, ids_rows, bias, enter, leave, flags):
    n = CHUNK
    eye = as_mask(iota((n, n), 0) == iota((n, n), 1))
    causal = iota((n, n), 0) >= iota((n, n), 1)
    for k in range(4):
        at = slice(k * n, (k + 1) * n)
        row = jnp.broadcast_to(ids_rows[:, at].astype(F32), (n, n))
        column = dot(eye, row.astype(BF16), NT)
        bias[at] = jnp.where((row == column) & causal, 0.0, BLOCKED)
        enter[at] = jnp.where(column == column[0:1], 0.0, BLOCKED)
        leave[at] = jnp.where(column == column[n - 1 : n], 0.0, BLOCKED)
        first, last = ids[0, k * n], ids[0, k * n + n - 1]
        linked = (k > 0) & (ids[0, max(k * n - 1, 0)] == first)
        flags[k] = jnp.where(linked, 1.0, 0.0)
        flags[4 + k] = jnp.where(first == last, 1.0, 0.0)
    flags[8] = ids[0, 0].astype(F32)
    flags[9] = ids[0, 4 * n - 1].astype(F32)


def make_masks(ids):
    wide = jax.ShapeDtypeStruct((4 * CHUNK, CHUNK), F32)
    return pl.pallas_call(
        masks_kernel,
        in_specs=[smem(), vmem()],
        out_specs=[vmem()] * 3 + [smem()],
        out_shape=[wide] * 3 + [jax.ShapeDtypeStruct((10,), F32)],
        compiler_params=pltpu.CompilerParams(vmem_limit_bytes=VMEM_LIMIT),
        cost_estimate=SMALL,
        name="make_masks",
    )(ids, ids)


CHUNKS = range(4)


def span_of(k):
    return slice(k * CHUNK, (k + 1) * CHUNK)


class Moves:
    def __init__(self, sems):
        self.sems, self.count = sems, 0

    def start(self, src, dst):
        copy = pltpu.make_async_copy(src, dst, self.sems.at[self.count])
        self.count += 1
        copy.start()
        return copy


def group_of(me, place, d):
    return lax.rem(me[0] + (2 * place[0] - 1) * d + GROUPS, GROUPS)


def head_lanes(per_head, g, axis):
    shape = (CHUNK, CHUNK)
    return jnp.where(iota(shape, axis) < CHUNK // 2, per_head[g], per_head[GROUPS + g])


def entering_group(g, rates, flags, maps, x_in, dy_in, steps, enter, leave, kept, send_out):
    (write, read), n, half = (maps.at[0], maps.at[1]), CHUNK, CHUNK // 2
    rate_lanes = head_lanes(rates, g, 1) * -LOG2E
    rate_rows = head_lanes(rates, g, 0) * -LOG2E
    columns = [step_halves(steps, k) for k in CHUNKS]
    u = [columns[k][0] * rate_lanes for k in CHUNKS]
    into = [jnp.exp2(u[k] + enter[span_of(k)]) for k in CHUNKS]
    out_of = [jnp.exp2(u[k][n - 1 : n] - u[k] + leave[span_of(k)]) for k in CHUNKS]
    rounded = [
        (x_in[g, span_of(k)].astype(F32) * columns[k][1]).astype(BF16).astype(F32) for k in CHUNKS
    ]
    scaled = [(rounded[k] * out_of[k]).astype(BF16) for k in CHUNKS]
    carried = [(dy_in[g, span_of(k)].astype(F32) * into[k]).astype(BF16) for k in CHUNKS]
    spans = [jnp.exp2(columns[k][2] * rate_rows) * flags[4 + k] for k in CHUNKS]
    yield
    locals_ = [dot(scaled[k], write[span_of(k)], TN) for k in CHUNKS]
    directs = [dot(carried[k], read[span_of(k)], TN) for k in CHUNKS]
    for k in CHUNKS:
        kept[0, span_of(k)] = locals_[k].astype(BF16)
        kept[1, span_of(k)] = directs[k].astype(BF16)
    end, span = locals_[0], spans[0]
    for k in range(1, 4):
        factor = spans[k] * flags[k]
        end = factor * end + locals_[k]
        span = factor * span
    begin = directs[3]
    for k in (2, 1, 0):
        begin = flags[k + 1] * spans[k] * begin + directs[k]
    row = iota((16, n), 0)
    for q in range(2):
        part = slice(q * half, (q + 1) * half)
        send_out[q, :half] = end[part].astype(BF16)
        send_out[q, half:n] = begin[part].astype(BF16)
        one = span[q * half : q * half + 1]
        rest = one - one.astype(BF16).astype(F32)
        ids = jnp.where(row == 2, flags[8], jnp.where(row == 3, flags[9], 0.0))
        meta = jnp.where(row == 0, one, jnp.where(row == 1, rest, ids))
        send_out[q, n:] = meta.astype(BF16)
    yield


def entering_kernel(tasks, me, place, rates, flags, *refs):
    count = len(tasks)
    maps_in, (x_in, dy_in, steps_in, enter, leave) = refs[:count], refs[count : count + 5]
    ends_all, sends_all, maps, ends, sends, sems = refs[-6:]
    moves = Moves(sems)
    loads = [moves.start(maps_in[i], maps.at[i]) for i in range(count)]
    stores = []
    for i, (spot, d) in enumerate(tasks):
        g = group_of(me, place, d)
        work = entering_group(
            g, rates, flags, maps.at[i], x_in, dy_in, steps_in[g], enter, leave, ends.at[i], sends.at[i]
        )
        next(work)
        loads[i].wait()
        next(work)
        stores.append(moves.start(ends.at[i], ends_all.at[spot]))
        stores.append(moves.start(sends.at[i], sends_all.at[2 * spot : 2 * spot + 2]))
    for store in stores:
        store.wait()


def call_on(kernel, scalars, arrays, so_far, out_shape, out_specs, scratch, copies, name):
    count = len(scalars) + len(arrays)
    operands = [array if spec is VMEM else in_hbm(array)[0] for array, spec in arrays]
    specs = [vmem() if spec is VMEM else hbm() for _, spec in arrays]
    return pl.pallas_call(
        kernel,
        in_specs=[smem()] * len(scalars) + specs + [hbm()] * len(so_far),
        out_specs=out_specs,
        out_shape=out_shape,
        input_output_aliases={count + i: i for i in range(len(so_far))},
        scratch_shapes=scratch + [pltpu.SemaphoreType.DMA((copies,))],
        compiler_params=pltpu.CompilerParams(vmem_limit_bytes=VMEM_LIMIT),
        cost_estimate=SMALL,
        name=name,
    )(*scalars, *operands, *in_hbm(*so_far))


def entering_part(tasks, me, place, rates, flags, pieces, x, dy, steps, enter, leave, so_far):
    count, tokens = len(tasks), x.shape[1]
    return call_on(
        functools.partial(entering_kernel, tasks),
        [me, place, rates, flags],
        [(pieces[d], HBM) for _, d in tasks] + [(v, VMEM) for v in (x, dy, steps, enter, leave)],
        so_far,
        [
            hbm_out((GROUPS, 2, tokens, CHUNK), BF16),
            hbm_out((2 * GROUPS, CHUNK + 16, CHUNK), BF16),
        ],
        [hbm()] * 2,
        [
            pltpu.VMEM((count, 2, tokens, CHUNK), BF16),
            pltpu.VMEM((count, 2, tokens, CHUNK), BF16),
            pltpu.VMEM((count, 2, CHUNK + 16, CHUNK), BF16),
        ],
        3 * count,
        "entering_part",
    )


def inner_group(g, rates, maps, x_in, dy_in, steps, bias, kept, rows):
    (write, read), n = (maps.at[0], maps.at[1]), CHUNK
    rate_a, rate_b = -rates[g] * LOG2E, -rates[GROUPS + g] * LOG2E
    low = iota((n, n), 1) < n // 2
    upper = as_mask(iota((n, n), 0) <= iota((n, n), 1))
    columns = [step_columns(steps, k) for k in CHUNKS]
    scores = [dot(read[span_of(k)], write[span_of(k)], NT) for k in CHUNKS]
    u_rows = dot(steps.astype(BF16), upper, NN) * jnp.where(
        iota((8, n), 0) % 2 == 0, rate_a, rate_b
    )
    x = [x_in[g, span_of(k)].astype(F32) for k in CHUNKS]
    dy = [dy_in[g, span_of(k)] for k in CHUNKS]
    stepped = [x[k] * jnp.where(low, columns[k][2], columns[k][3]) for k in CHUNKS]
    pair = [
        jnp.concatenate(
            [jnp.where(low, stepped[k], 0.0), jnp.where(low, 0.0, stepped[k])], axis=0
        ).astype(BF16)
        for k in CHUNKS
    ]
    rounded = [stepped[k].astype(BF16).astype(F32) for k in CHUNKS]
    d_weights = [dot(dy[k], pair[k], NT) for k in CHUNKS]
    falls, weights = [], []
    for k in CHUNKS:
        mask = bias[span_of(k)]
        falls.append(
            (
                jnp.exp2(columns[k][0] * rate_a - u_rows[2 * k : 2 * k + 1] + mask),
                jnp.exp2(columns[k][1] * rate_b - u_rows[2 * k + 1 : 2 * k + 2] + mask),
            )
        )
        weights.append(
            jnp.concatenate([falls[k][0] * scores[k], falls[k][1] * scores[k]], axis=1).astype(BF16)
        )
    inside = [dot(weights[k], pair[k], NN) for k in CHUNKS]
    d_pair = [dot(weights[k], dy[k], TN) for k in CHUNKS]
    d_scores = [
        (d_weights[k][:, :n] * falls[k][0] + d_weights[k][:, n:] * falls[k][1]).astype(BF16)
        for k in CHUNKS
    ]
    d_read = [dot(d_scores[k], write[span_of(k)], NN) for k in CHUNKS]
    d_write = [dot(d_scores[k], read[span_of(k)], TN) for k in CHUNKS]
    d_x = [jnp.where(low, d_pair[k][:n], d_pair[k][n:]) for k in CHUNKS]
    sums = [
        split_dot(head_rows(k), dy[k].astype(F32) * inside[k] - rounded[k] * d_x[k], NT)
        for k in CHUNKS
    ]
    rows[...] = (sums[0] + sums[1]) + (sums[2] + sums[3])
    for k in CHUNKS:
        for i, part in enumerate((inside, d_x, d_write, d_read)):
            kept[i, span_of(k)] = part[k].astype(BF16)


def inner_kernel(tasks, me, place, rates, *refs):
    count = len(tasks)
    maps_in, (x_in, dy_in, steps_in, bias) = refs[:count], refs[count : count + 4]
    kept_all, rows_all, maps, kept, rows, sems = refs[-6:]
    moves = Moves(sems)
    loads = [moves.start(maps_in[i], maps.at[i]) for i in range(count)]
    stores = []
    for i, (spot, d) in enumerate(tasks):
        g = group_of(me, place, d)
        loads[i].wait()
        inner_group(g, rates, maps.at[i], x_in, dy_in, steps_in[g], bias, kept.at[i], rows.at[i])
        stores.append(moves.start(kept.at[i], kept_all.at[spot]))
        stores.append(moves.start(rows.at[i], rows_all.at[spot]))
    for store in stores:
        store.wait()


def inner_part(tasks, me, place, rates, pieces, x, dy, steps, bias, so_far):
    count, tokens = len(tasks), x.shape[1]
    return call_on(
        functools.partial(inner_kernel, tasks),
        [me, place, rates],
        [(pieces[d], HBM) for _, d in tasks] + [(v, VMEM) for v in (x, dy, steps, bias)],
        so_far,
        [
            hbm_out((GROUPS, 4, tokens, CHUNK), BF16),
            hbm_out((GROUPS, 8, CHUNK), F32),
        ],
        [hbm()] * 2,
        [
            pltpu.VMEM((count, 2, tokens, CHUNK), BF16),
            pltpu.VMEM((count, 4, tokens, CHUNK), BF16),
            pltpu.VMEM((count, 8, CHUNK), F32),
        ],
        3 * count,
        "inner_part",
    )


def scan_kernel(got, out):
    half = CHUNK // 2
    count = got.shape[0]
    spans, links, last = [], [], None
    for i in range(count):
        meta = got[i, CHUNK:].astype(F32)
        spans.append(meta[0:1] + meta[1:2])
        same = jnp.zeros_like(meta[2:3]) if last is None else jnp.where(meta[2:3] == last, 1.0, 0.0)
        links.append(same)
        last = meta[3:4]
    state = jnp.zeros((half, CHUNK), F32)
    for i in range(count):
        used = links[i] * state
        out[i, :half] = used.astype(BF16)
        state = spans[i] * used + got[i, :half].astype(F32)
    state = jnp.zeros((half, CHUNK), F32)
    for i in range(count - 1, -1, -1):
        out[i, half:] = state.astype(BF16)
        state = links[i] * (spans[i] * state + got[i, half:CHUNK].astype(F32))


def scan_states(got):
    return pl.pallas_call(
        scan_kernel,
        in_specs=[vmem()],
        out_specs=vmem(),
        out_shape=jax.ShapeDtypeStruct((got.shape[0], CHUNK, CHUNK), BF16),
        compiler_params=pltpu.CompilerParams(vmem_limit_bytes=VMEM_LIMIT),
        name="scan_states",
    )(got)


def final_group(
    g, rates, gains, flags, states, maps, x_in, dy_in, steps, enter, leave, kept, rows_in, ends,
    y_out, dx_out, ds_out, d_maps, wait_first, wait_then
):
    (write, read), n, half = (maps.at[0], maps.at[1]), CHUNK, CHUNK // 2
    dw_out, dr_out = d_maps.at[0], d_maps.at[1]
    low = iota((n, n), 1) < half
    rate_lanes = head_lanes(rates, g, 1) * -LOG2E
    gain_lanes = head_lanes(gains, g, 1)
    rate_rows = head_lanes(rates, g, 0) * -LOG2E
    columns = [step_halves(steps, k) for k in CHUNKS]
    spans = [jnp.exp2(columns[k][2] * rate_rows) * flags[4 + k] for k in CHUNKS]
    step = [columns[k][1] for k in CHUNKS]
    u = [columns[k][0] * rate_lanes for k in CHUNKS]
    into = [jnp.exp2(u[k] + enter[span_of(k)]) for k in CHUNKS]
    out_of = [jnp.exp2(u[k][n - 1 : n] - u[k] + leave[span_of(k)]) for k in CHUNKS]
    wait_first()
    state = jnp.concatenate([states[0, :half], states[1, :half]], axis=0).astype(F32)
    used = [state]
    for k in range(3):
        state = flags[k + 1] * (spans[k] * state + ends[0, span_of(k)].astype(F32))
        used.append(state)
    after = jnp.concatenate([states[0, half:], states[1, half:]], axis=0).astype(F32)
    wanted = [after]
    for k in (3, 2, 1):
        after = flags[k] * (spans[k] * after + ends[1, span_of(k)].astype(F32))
        wanted.insert(0, after)
    used16 = [v.astype(BF16) for v in used]
    wanted16 = [v.astype(BF16) for v in wanted]
    cross = [dot(read[span_of(k)], used16[k], NT) for k in CHUNKS]
    back = [dot(write[span_of(k)], wanted16[k], NT) for k in CHUNKS]
    x = [x_in[g, span_of(k)].astype(F32) for k in CHUNKS]
    dy = [dy_in[g, span_of(k)].astype(F32) for k in CHUNKS]
    rounded = [(x[k] * step[k]).astype(BF16).astype(F32) for k in CHUNKS]
    d_read = [dot((dy[k] * into[k]).astype(BF16), used16[k], NN) for k in CHUNKS]
    d_write = [dot((rounded[k] * out_of[k]).astype(BF16), wanted16[k], NN) for k in CHUNKS]
    cross = [cross[k] * into[k] for k in CHUNKS]
    back = [back[k] * out_of[k] for k in CHUNKS]
    wait_then()
    d_x = [kept[1, span_of(k)].astype(F32) + back[k] for k in CHUNKS]
    select = [head_rows(k) for k in CHUNKS]
    from_all = [split_dot(select[k], spans[k] * wanted[k] * used[k], NN) for k in CHUNKS]
    sums = [split_dot(select[k], dy[k] * cross[k], NT) for k in CHUNKS]
    from_before = [split_dot(select[k], rounded[k] * back[k], NT) for k in CHUNKS]
    straight = [split_dot(select[k], x[k] * d_x[k], NT) for k in CHUNKS]
    for k in CHUNKS:
        at = span_of(k)
        y_out[at] = (kept[0, at].astype(F32) + cross[k] + gain_lanes * x[k]).astype(BF16)
        dx_out[at] = (step[k] * d_x[k] + gain_lanes * dy[k]).astype(BF16)
        dr_out[at] = (kept[3, at].astype(F32) + d_read[k]).astype(BF16)
        dw_out[at] = (kept[2, at].astype(F32) + d_write[k]).astype(BF16)
    lower = as_mask(iota((n, n), 0) >= iota((n, n), 1))
    before = as_mask(iota((n, n), 0) < iota((n, n), 1))
    every = lambda v: (v[0] + v[1]) + (v[2] + v[3])
    joined = jnp.concatenate([rows_in[...] + every(sums), every(from_before), every(from_all)], axis=1)
    table = jnp.concatenate([lower, before, jnp.ones((n, n), BF16)], axis=0)
    high = joined.astype(BF16)
    rest = joined - high.astype(F32)
    middle = rest.astype(BF16)
    low_part = (rest - middle.astype(F32)).astype(BF16)
    d_rate = dot(high, table, NN) + dot(middle, table, NN) + dot(low_part, table, NN)
    rates8 = jnp.where(iota((8, n), 0) % 2 == 0, rates[g], rates[GROUPS + g])
    ds_out[...] = every(straight) - rates8 * d_rate


def final_kernel(tasks, me, place, rates, gains, flags, *refs):
    count = len(tasks)
    maps_in = refs[:count]
    states_in, x_in, dy_in, steps_in, enter, leave, kept_in, rows_in, ends_in = refs[count : count + 9]
    y_all, dx_all, ds_all = refs[-11 - count : -8 - count]
    d_maps = refs[-8 - count : -8]
    maps, kept, rows, ends, y, dx, ds, sems = refs[-8:]
    moves = Moves(sems)
    first = [
        (
            moves.start(maps_in[i], maps.at[i]),
            moves.start(ends_in.at[spot], ends.at[i]),
        )
        for i, (spot, _) in enumerate(tasks)
    ]
    then = [
        (
            moves.start(kept_in.at[spot], kept.at[i]),
            moves.start(rows_in.at[spot], rows.at[i]),
        )
        for i, (spot, _) in enumerate(tasks)
    ]

    def wait_for(copies):
        def wait():
            for copy in copies:
                copy.wait()

        return wait

    stores = []
    for i, (spot, d) in enumerate(tasks):
        g = group_of(me, place, d)
        final_group(
            g, rates, gains, flags, states_in.at[2 * spot : 2 * spot + 2], maps.at[i], x_in, dy_in,
            steps_in[g], enter, leave, kept.at[i], rows.at[i], ends.at[i], y.at[i], dx.at[i], ds.at[i],
            d_maps[i], wait_for(first[i]), wait_for(then[i]),
        )
        stores.append(moves.start(y.at[i], y_all.at[g]))
        stores.append(moves.start(dx.at[i], dx_all.at[g]))
        stores.append(moves.start(ds.at[i], ds_all.at[g]))
    for store in stores:
        store.wait()


def final_part(
    tasks, me, place, rates, gains, flags, states, pieces, x, dy, steps, enter, leave, kept, rows, ends, so_far
):
    count, tokens = len(tasks), x.shape[1]
    wide = hbm_out(x.shape, BF16)
    d_maps = jax.ShapeDtypeStruct((2, tokens, CHUNK), BF16)
    outs = call_on(
        functools.partial(final_kernel, tasks),
        [me, place, rates, gains, flags],
        [(pieces[d], HBM) for _, d in tasks]
        + [(v, VMEM) for v in (states, x, dy, steps, enter, leave)]
        + [(v, HBM) for v in (kept, rows, ends)],
        so_far,
        [wide, wide, hbm_out(steps.shape, F32)] + [d_maps] * count,
        [hbm()] * 3 + [vmem()] * count,
        [
            pltpu.VMEM((count, 2, tokens, CHUNK), BF16),
            pltpu.VMEM((count, 4, tokens, CHUNK), BF16),
            pltpu.VMEM((count, 8, CHUNK), F32),
            pltpu.VMEM((count, 2, tokens, CHUNK), BF16),
            pltpu.VMEM((count, tokens, CHUNK), BF16),
            pltpu.VMEM((count, tokens, CHUNK), BF16),
            pltpu.VMEM((count, 8, CHUNK), F32),
        ],
        7 * count,
        "final_part",
    )
    return outs[:3], outs[3:]


def add_kernel(*refs):
    *terms, out = refs
    total = terms[0][...].astype(F32)
    for term in terms[1:]:
        total = total + term[...].astype(F32)
    out[...] = total.astype(BF16)


def add(*terms):
    return pl.pallas_call(
        add_kernel,
        in_specs=[vmem()] * len(terms),
        out_specs=vmem(),
        out_shape=jax.ShapeDtypeStruct(terms[0].shape, BF16),
        compiler_params=pltpu.CompilerParams(vmem_limit_bytes=VMEM_LIMIT),
        cost_estimate=SMALL,
        name="add",
    )(*terms)


def columns_kernel(y_hbm, dx_hbm, ds_in, y_out, dx_out, ds_out, y_in, dx_in, y_buf, sems):
    half = CHUNK // 2
    length = y_buf.shape[1]
    loads, copies = [], []
    for s in range(2):
        at = slice(s * length, (s + 1) * length)
        for src, dst in ((y_hbm, y_in), (dx_hbm, dx_in)):
            loads.append(
                pltpu.make_async_copy(src.at[:, at], dst.at[:, at], sems.at[2 + len(loads)])
            )
            loads[-1].start()
    for s in range(2):
        at = slice(s * length, (s + 1) * length)
        for load in loads[2 * s : 2 * s + 2]:
            load.wait()
        for src, dst in ((y_in, y_buf), (dx_in, dx_out)):
            for g in range(GROUPS):
                block = src[g, at]
                dst[s, :, g * half : (g + 1) * half] = block[:, :half]
                dst[s, :, (GROUPS + g) * half : (GROUPS + g + 1) * half] = block[:, half:]
        copies.append(pltpu.make_async_copy(y_buf.at[s], y_out.at[s], sems.at[s]))
        copies[s].start()
        for q in range(2):
            for part in range(2):
                ds_out[
                    s, q * GROUPS : (q + 1) * GROUPS, part * CHUNK : (part + 1) * CHUNK
                ] = ds_in[:, (2 * s + part) * 2 + q, :].astype(BF16)
    for copy in copies:
        copy.wait()


def to_columns(y, dx, ds):
    length = y.shape[1] // 2
    columns = GROUPS * CHUNK
    wide = jax.ShapeDtypeStruct((2, length, columns), BF16)
    return pl.pallas_call(
        columns_kernel,
        in_specs=[hbm(), hbm(), vmem()],
        out_specs=[hbm(), vmem(), vmem()],
        out_shape=[hbm_out(wide.shape, BF16), wide, jax.ShapeDtypeStruct((2, 2 * GROUPS, length), BF16)],
        scratch_shapes=[pltpu.VMEM(y.shape, BF16)] * 2
        + [pltpu.VMEM((2, length, columns), BF16), pltpu.SemaphoreType.DMA((6,))],
        compiler_params=pltpu.CompilerParams(vmem_limit_bytes=VMEM_LIMIT),
        cost_estimate=SMALL,
        name="to_columns",
    )(*in_hbm(y, dx), ds)


def settle_kernel(count, routes, place, *refs):
    owns, peers, outs = refs[:count], refs[count : 2 * count], refs[2 * count : 3 * count]
    zeros, sems = refs[3 * count : 4 * count], refs[-1]
    for zero in zeros:
        zero[...] = jnp.zeros_like(zero)
    copies = []
    for m in range(3):
        target = routes[m]
        slot = lax.rem(jnp.maximum(target, 0), 2)
        mine = lax.div(target, 2) == place[0]
        for i in range(count):
            out, sem = outs[i].at[m], sems.at[m * count + i]

            @pl.when(target < 0)
            def _(zero=zeros[i], out=out, sem=sem):
                pltpu.make_async_copy(zero, out, sem).start()

            @pl.when((target >= 0) & mine)
            def _(own=owns[i], out=out, sem=sem):
                pltpu.make_async_copy(own.at[slot], out, sem).start()

            @pl.when((target >= 0) & jnp.logical_not(mine))
            def _(peer=peers[i], out=out, sem=sem):
                pltpu.make_async_copy(peer.at[slot], out, sem).start()

            copies.append(pltpu.make_async_copy(zeros[i], out, sem))
    for copy in copies:
        copy.wait()


def settle(routes, place, owns, peers):
    count = len(owns)
    return pl.pallas_call(
        functools.partial(settle_kernel, count),
        in_specs=[smem()] * 2 + [hbm()] * (2 * count),
        out_specs=[hbm()] * count,
        out_shape=[
            hbm_out((routes.shape[0],) + own.shape[1:], own.dtype) for own in owns
        ],
        scratch_shapes=[pltpu.VMEM(own.shape[1:], own.dtype) for own in owns]
        + [pltpu.SemaphoreType.DMA((3 * count,))],
        compiler_params=pltpu.CompilerParams(vmem_limit_bytes=VMEM_LIMIT),
        cost_estimate=SMALL,
        name="settle",
    )(routes, place, *owns, *peers)


def last_sum_kernel(a, b, c, out):
    length = out.shape[1] // 2
    for i in range(2):
        for s in range(2):
            at = slice(s * length, (s + 1) * length)
            total = a[i, at].astype(F32) + b[i, at].astype(F32) + c[i, at].astype(F32)
            out[s, i * length : (i + 1) * length] = total.astype(BF16)


def last_sum(a, b, c):
    return pl.pallas_call(
        last_sum_kernel,
        in_specs=[vmem()] * 3,
        out_specs=vmem(),
        out_shape=jax.ShapeDtypeStruct(a.shape, BF16),
        compiler_params=pltpu.CompilerParams(vmem_limit_bytes=VMEM_LIMIT),
        cost_estimate=SMALL,
        name="last_sum",
    )(a, b, c)


def settle_maps_kernel(routes, place, own, peer, write, read, zero, sems):
    length = write.shape[1]
    zero[...] = jnp.zeros_like(zero)
    copies = []
    for m in range(3):
        target = routes[m]
        slot = lax.rem(jnp.maximum(target, 0), 2)
        mine = lax.div(target, 2) == place[0]
        for i, result in enumerate((write, read)):
            out, sem, at = result.at[m], sems.at[2 * m + i], slice(i * length, (i + 1) * length)

            @pl.when(target < 0)
            def _(out=out, sem=sem):
                pltpu.make_async_copy(zero, out, sem).start()

            @pl.when((target >= 0) & mine)
            def _(out=out, sem=sem, at=at):
                pltpu.make_async_copy(own.at[slot, at], out, sem).start()

            @pl.when((target >= 0) & jnp.logical_not(mine))
            def _(out=out, sem=sem, at=at):
                pltpu.make_async_copy(peer.at[slot, at], out, sem).start()

            copies.append(pltpu.make_async_copy(zero, out, sem))
    for copy in copies:
        copy.wait()


def settle_maps(routes, place, own, peer):
    shape = (own.shape[1] // 2, own.shape[2])
    return pl.pallas_call(
        settle_maps_kernel,
        in_specs=[smem()] * 2 + [vmem()] * 2,
        out_specs=[hbm()] * 2,
        out_shape=[hbm_out((routes.shape[0],) + shape, BF16)] * 2,
        scratch_shapes=[pltpu.VMEM(shape, BF16), pltpu.SemaphoreType.DMA((6,))],
        compiler_params=pltpu.CompilerParams(vmem_limit_bytes=VMEM_LIMIT),
        cost_estimate=SMALL,
        name="settle_maps",
    )(routes, place, own, peer)


def after(operand, other):
    return lax.optimization_barrier((operand, other))[0]


def shards(
    values, step_sizes, write_map, read_map, decay_rates, skip_gain, routes, segment_ids, grad_out
):
    values, step_sizes = values[0, 0], step_sizes[0, 0]
    write_map, read_map, grad_out = write_map[0, 0], read_map[0, 0], grad_out[0, 0]
    routes = routes[0, 0]
    ring, stream = lax.axis_size("tensor"), lax.axis_size("ctx")
    swap = [(0, 1), (1, 0)]
    me = lax.axis_index("tensor").reshape(1)
    place = lax.axis_index("dp").reshape(1)

    def across(operand):
        return lax.ppermute(operand, "dp", swap)

    def turn(way):
        return [
            (core * ring + i, core * ring + (i + (way if core == 0 else -way)) % ring)
            for core in range(2)
            for i in range(ring)
        ]

    def go_first(operand):
        return lax.ppermute(operand, ("dp", "tensor"), turn(1))

    def go_second(operand):
        return lax.ppermute(operand, ("dp", "tensor"), turn(-1))

    peer_routes = across(routes)
    peer_write, peer_read = across(write_map), across(read_map)
    maps = pick_maps(routes, peer_routes, place, write_map, read_map, peer_write, peer_read)
    bias, enter, leave, flags = make_masks(segment_ids)
    peer_values, peer_steps = across(after(values, maps)), across(after(step_sizes, maps))
    x, steps, dy = pick_values(
        routes, peer_routes, place, values, peer_values, step_sizes, peer_steps, grad_out
    )

    arrival = (0, 1, -1, 2, -2, 3, -3, 4)
    spots = {d: i for i, d in enumerate(arrival)}
    pieces, ends = {0: maps}, []

    def entering(*groups):
        nonlocal ends
        ends = entering_part(
            [(spots[d], d) for d in groups], me, place, decay_rates, flags, pieces,
            x, dy, steps, enter, leave, ends,
        )
        return ends[1]

    pieces[1], pieces[-1] = go_first(maps), go_second(maps)
    pieces[2], pieces[-2] = go_first(pieces[1]), go_second(pieces[-1])
    done = entering(0)
    pieces[3], pieces[-3] = go_first(after(pieces[2], done)), go_second(after(pieces[-2], done))
    done = entering(1, -1, 2, -2)
    pieces[4] = go_first(after(pieces[3], done))
    entering(3, -3)
    entering(4)

    inner = []

    def inside(groups, operand):
        nonlocal inner
        inner = inner_part(
            [(spots[d], d) for d in groups], me, place, decay_rates, pieces, operand, dy, steps, bias, inner
        )

    got = lax.all_to_all(ends[1], "ctx", split_axis=0, concat_axis=0, tiled=True)
    inside(arrival[:4], after(x, ends[1]))
    scanned = scan_states(after(got, inner[1]))
    states = lax.all_to_all(scanned, "ctx", split_axis=0, concat_axis=0, tiled=True)
    inside(arrival[4:], after(x, scanned))

    so_far = []

    def final(groups, other=None):
        nonlocal so_far
        operand = x if other is None else after(x, other)
        so_far, d_maps = final_part(
            [(spots[d], d) for d in groups], me, place, decay_rates, skip_gain, flags, states, pieces,
            operand, dy, steps, enter, leave, *inner, ends[0], so_far,
        )
        return d_maps

    (far,) = final((4,))
    far = go_first(far)
    up, down, here = final((-3, 3, 0))
    one, other = add(far, up), down
    one_sent, other_sent = go_first(one), go_second(other)
    up, down = final((-2, 2), (one, other))
    one, other = add(one_sent, up), add(other_sent, down)
    one_sent, other_sent = go_first(one), go_second(other)
    up, down = final((-1, 1), (one, other))
    one, other = add(one_sent, up), add(other_sent, down)
    one_sent, other_sent = go_first(one), go_second(other)
    output, grad_values, grad_steps = to_columns(*after(tuple(so_far), (one, other)))
    peer_values, peer_steps = across(grad_values), across(grad_steps)
    back_values, back_steps = settle(
        routes, place, [grad_values, grad_steps], [peer_values, peer_steps]
    )
    d_maps = last_sum(after(one_sent, back_steps), other_sent, here)
    back_write, back_read = settle_maps(routes, place, d_maps, across(d_maps))
    return tuple(
        array[None, None] for array in (output, back_values, back_steps, back_write, back_read)
    )


def solution(mesh):
    placed = (
        P("dp", "ctx", None, None, "tensor"),
        P("dp", "ctx", None, "tensor", None),
        P("dp", "ctx", None, None, "tensor"),
        P("dp", "ctx", None, None, "tensor"),
        P("tensor"),
        P("tensor"),
        P("dp", "ctx", None),
        P("dp", "ctx"),
        P("dp", "ctx", None, None, "tensor"),
    )
    return jax.shard_map(
        shards,
        mesh=mesh,
        in_specs=placed,
        out_specs=(
            P("dp", "ctx", None, None, "tensor"),
            P("dp", "ctx", None, None, "tensor"),
            P("dp", "ctx", None, "tensor", None),
            P("dp", "ctx", None, None, "tensor"),
            P("dp", "ctx", None, None, "tensor"),
        ),
        check_vma=False,
    )
```

```python
import functools
import math

import jax
import jax.numpy as jnp
from jax import lax
from jax.experimental import pallas as pl
from jax.experimental.pallas import tpu as pltpu
from jax.sharding import PartitionSpec as P

GROUPS = 8
CHUNK = 128
LOG2E = math.log2(math.e)
F32 = jnp.float32
BF16 = jnp.bfloat16
VMEM_LIMIT = 16 * 1024 * 1024
BLOCKED = -1e30
SMALL = pl.CostEstimate(flops=1000, bytes_accessed=1000, transcendentals=0)
HBM, VMEM = "hbm", "vmem"

NN = (((1,), (0,)), ((), ()))
NT = (((1,), (1,)), ((), ()))
TN = (((0,), (0,)), ((), ()))


def dot(a, b, dims):
    return lax.dot_general(a, b, dims, preferred_element_type=F32)


def split_dot(a, b, dims):
    high = b.astype(BF16)
    low = (b - high.astype(F32)).astype(BF16)
    return dot(a, high, dims) + dot(a, low, dims)


def iota(shape, dim):
    return lax.broadcasted_iota(jnp.int32, shape, dim)


def as_mask(condition):
    return jnp.where(condition, 1.0, 0.0).astype(BF16)


def step_rows(steps, k):
    n = CHUNK
    first = jnp.broadcast_to(steps[2 * k : 2 * k + 1], (n, n)).astype(BF16)
    second = jnp.broadcast_to(steps[2 * k + 1 : 2 * k + 2], (n, n)).astype(BF16)
    return first, second


def sums_and_steps():
    n = CHUNK
    lower = as_mask(iota((n, n), 0) >= iota((n, n), 1))
    eye = as_mask(iota((n, n), 0) == iota((n, n), 1))
    return jnp.concatenate([lower, eye], axis=0)


def step_columns(steps, k):
    n = CHUNK
    both = dot(sums_and_steps(), jnp.concatenate(step_rows(steps, k), axis=0), NT)
    return both[:n, :n], both[:n, n:], both[n:, :n], both[n:, n:]


def step_halves(steps, k):
    n = CHUNK
    first, second = step_rows(steps, k)
    halves = jnp.concatenate([first[: n // 2], second[: n // 2]], axis=0)
    both = dot(sums_and_steps(), halves, NT)
    return both[:n], both[n:], dot(halves, jnp.ones((n, n), BF16), NT)


def head_rows(k):
    rows, lanes = iota((8, CHUNK), 0), iota((8, CHUNK), 1)
    return as_mask(rows == 2 * k + (lanes >= CHUNK // 2).astype(jnp.int32))


def smem():
    return pl.BlockSpec(memory_space=pltpu.SMEM)


def vmem():
    return pl.BlockSpec(memory_space=pltpu.VMEM)


def hbm():
    return pl.BlockSpec(memory_space=pltpu.HBM)


def in_hbm(*arrays):
    return [pltpu.with_memory_space_constraint(array, pltpu.HBM) for array in arrays]


def hbm_out(shape, dtype):
    return pltpu.HBM(tuple(shape), dtype)


def slot_of(routes, target):
    slot = jnp.where(routes[1] == target, 1, jnp.where(routes[2] == target, 2, 0))
    return slot, (routes[0] == target) | (slot > 0)


def fetch(own_routes, peer_routes, place, s, own, peer, out, sem):
    target = place[0] * 2 + s
    own_slot, mine = slot_of(own_routes, target)
    peer_slot, _ = slot_of(peer_routes, target)

    @pl.when(mine)
    def _():
        pltpu.make_async_copy(own.at[own_slot], out, sem).start()

    @pl.when(jnp.logical_not(mine))
    def _():
        pltpu.make_async_copy(peer.at[peer_slot], out, sem).start()

    return pltpu.make_async_copy(own.at[0], out, sem)


def pick_maps_kernel(own_routes, peer_routes, place, ow, pw, orr, pr, out, sems):
    length = ow.shape[1]
    pending = []
    for s in range(2):
        for i, (own, peer) in enumerate(((ow, pw), (orr, pr))):
            part = out.at[i, s * length : (s + 1) * length]
            pending.append(
                fetch(own_routes, peer_routes, place, s, own, peer, part, sems.at[2 * s + i])
            )
    for copy in pending:
        copy.wait()


def pick_maps(own_routes, peer_routes, place, write, read, peer_write, peer_read):
    length, state = write.shape[1:]
    return pl.pallas_call(
        pick_maps_kernel,
        in_specs=[smem()] * 3 + [hbm()] * 4,
        out_specs=vmem(),
        out_shape=jax.ShapeDtypeStruct((2, 2 * length, state), BF16),
        scratch_shapes=[pltpu.SemaphoreType.DMA((4,))],
        compiler_params=pltpu.CompilerParams(vmem_limit_bytes=VMEM_LIMIT),
        name="pick_maps",
    )(own_routes, peer_routes, place, *in_hbm(write, peer_write, read, peer_read))


def to_groups(block, out):
    half = CHUNK // 2
    for g in range(GROUPS):
        a = block[:, g * half : (g + 1) * half]
        b = block[:, (GROUPS + g) * half : (GROUPS + g + 1) * half]
        out[g] = jnp.concatenate([a, b], axis=1)


def pick_values_kernel(
    own_routes, peer_routes, place, ox, px, os, ps, dy, x_out, s_out, dy_out,
    x_buf, s_buf, dy_buf, sems,
):
    length = ox.shape[1]
    pending = []
    for s in range(2):
        copy = pltpu.make_async_copy(dy.at[s], dy_buf.at[s], sems.at[3 * s])
        copy.start()
        steps = fetch(own_routes, peer_routes, place, s, os, ps, s_buf.at[s], sems.at[3 * s + 1])
        x = fetch(own_routes, peer_routes, place, s, ox, px, x_buf.at[s], sems.at[3 * s + 2])
        pending.append((copy, steps, x))
    for s in range(2):
        for copy in pending[s]:
            copy.wait()
        at = slice(s * length, (s + 1) * length)
        to_groups(dy_buf[s], dy_out.at[:, at])
        to_groups(x_buf[s], x_out.at[:, at])
        steps = s_buf[s].astype(F32)
        for q in range(2):
            for part in range(2):
                s_out[:, (2 * s + part) * 2 + q, :] = steps[
                    q * GROUPS : (q + 1) * GROUPS, part * CHUNK : (part + 1) * CHUNK
                ]


def pick_values(own_routes, peer_routes, place, values, peer_values, steps, peer_steps, upstream):
    length, columns = values.shape[1:]
    heads = steps.shape[1]
    return pl.pallas_call(
        pick_values_kernel,
        in_specs=[smem()] * 3 + [hbm()] * 5,
        out_specs=[vmem()] * 3,
        out_shape=[
            jax.ShapeDtypeStruct((GROUPS, 2 * length, CHUNK), BF16),
            jax.ShapeDtypeStruct((GROUPS, 8, CHUNK), F32),
            jax.ShapeDtypeStruct((GROUPS, 2 * length, CHUNK), BF16),
        ],
        scratch_shapes=[
            pltpu.VMEM((2, length, columns), BF16),
            pltpu.VMEM((2, heads, length), BF16),
            pltpu.VMEM((2, length, columns), BF16),
            pltpu.SemaphoreType.DMA((6,)),
        ],
        compiler_params=pltpu.CompilerParams(vmem_limit_bytes=VMEM_LIMIT),
        cost_estimate=SMALL,
        name="pick_values",
    )(
        own_routes, peer_routes, place,
        *in_hbm(values, peer_values, steps, peer_steps, upstream),
    )


def masks_kernel(ids, ids_rows, bias, enter, leave, flags):
    n = CHUNK
    eye = as_mask(iota((n, n), 0) == iota((n, n), 1))
    causal = iota((n, n), 0) >= iota((n, n), 1)
    for k in range(4):
        at = slice(k * n, (k + 1) * n)
        row = jnp.broadcast_to(ids_rows[:, at].astype(F32), (n, n))
        column = dot(eye, row.astype(BF16), NT)
        bias[at] = jnp.where((row == column) & causal, 0.0, BLOCKED)
        enter[at] = jnp.where(column == column[0:1], 0.0, BLOCKED)
        leave[at] = jnp.where(column == column[n - 1 : n], 0.0, BLOCKED)
        first, last = ids[0, k * n], ids[0, k * n + n - 1]
        linked = (k > 0) & (ids[0, max(k * n - 1, 0)] == first)
        flags[k] = jnp.where(linked, 1.0, 0.0)
        flags[4 + k] = jnp.where(first == last, 1.0, 0.0)
    flags[8] = ids[0, 0].astype(F32)
    flags[9] = ids[0, 4 * n - 1].astype(F32)


def make_masks(ids):
    wide = jax.ShapeDtypeStruct((4 * CHUNK, CHUNK), F32)
    return pl.pallas_call(
        masks_kernel,
        in_specs=[smem(), vmem()],
        out_specs=[vmem()] * 3 + [smem()],
        out_shape=[wide] * 3 + [jax.ShapeDtypeStruct((10,), F32)],
        compiler_params=pltpu.CompilerParams(vmem_limit_bytes=VMEM_LIMIT),
        cost_estimate=SMALL,
        name="make_masks",
    )(ids, ids)


CHUNKS = range(4)


def span_of(k):
    return slice(k * CHUNK, (k + 1) * CHUNK)


class Moves:
    def __init__(self, sems):
        self.sems, self.count = sems, 0

    def start(self, src, dst):
        copy = pltpu.make_async_copy(src, dst, self.sems.at[self.count])
        self.count += 1
        copy.start()
        return copy


def group_of(me, place, d):
    return lax.rem(me[0] + (2 * place[0] - 1) * d + GROUPS, GROUPS)


def head_lanes(per_head, g, axis):
    shape = (CHUNK, CHUNK)
    return jnp.where(iota(shape, axis) < CHUNK // 2, per_head[g], per_head[GROUPS + g])


def entering_group(g, rates, flags, maps, x_in, dy_in, steps, enter, leave, kept, send_out):
    (write, read), n, half = (maps.at[0], maps.at[1]), CHUNK, CHUNK // 2
    rate_lanes = head_lanes(rates, g, 1) * -LOG2E
    rate_rows = head_lanes(rates, g, 0) * -LOG2E
    columns = [step_halves(steps, k) for k in CHUNKS]
    u = [columns[k][0] * rate_lanes for k in CHUNKS]
    into = [jnp.exp2(u[k] + enter[span_of(k)]) for k in CHUNKS]
    out_of = [jnp.exp2(u[k][n - 1 : n] - u[k] + leave[span_of(k)]) for k in CHUNKS]
    rounded = [
        (x_in[g, span_of(k)].astype(F32) * columns[k][1]).astype(BF16).astype(F32) for k in CHUNKS
    ]
    scaled = [(rounded[k] * out_of[k]).astype(BF16) for k in CHUNKS]
    carried = [(dy_in[g, span_of(k)].astype(F32) * into[k]).astype(BF16) for k in CHUNKS]
    spans = [jnp.exp2(columns[k][2] * rate_rows) * flags[4 + k] for k in CHUNKS]
    yield
    locals_ = [dot(scaled[k], write[span_of(k)], TN) for k in CHUNKS]
    directs = [dot(carried[k], read[span_of(k)], TN) for k in CHUNKS]
    for k in CHUNKS:
        kept[0, span_of(k)] = locals_[k].astype(BF16)
        kept[1, span_of(k)] = directs[k].astype(BF16)
    end, span = locals_[0], spans[0]
    for k in range(1, 4):
        factor = spans[k] * flags[k]
        end = factor * end + locals_[k]
        span = factor * span
    begin = directs[3]
    for k in (2, 1, 0):
        begin = flags[k + 1] * spans[k] * begin + directs[k]
    row = iota((16, n), 0)
    for q in range(2):
        part = slice(q * half, (q + 1) * half)
        send_out[q, :half] = end[part].astype(BF16)
        send_out[q, half:n] = begin[part].astype(BF16)
        one = span[q * half : q * half + 1]
        rest = one - one.astype(BF16).astype(F32)
        ids = jnp.where(row == 2, flags[8], jnp.where(row == 3, flags[9], 0.0))
        meta = jnp.where(row == 0, one, jnp.where(row == 1, rest, ids))
        send_out[q, n:] = meta.astype(BF16)
    yield


def entering_kernel(tasks, me, place, rates, flags, *refs):
    count = len(tasks)
    maps_in, (x_in, dy_in, steps_in, enter, leave) = refs[:count], refs[count : count + 5]
    ends_all, sends_all, maps, ends, sends, sems = refs[-6:]
    moves = Moves(sems)
    loads = [moves.start(maps_in[i], maps.at[i]) for i in range(count)]
    stores = []
    for i, (spot, d) in enumerate(tasks):
        g = group_of(me, place, d)
        work = entering_group(
            g, rates, flags, maps.at[i], x_in, dy_in, steps_in[g], enter, leave, ends.at[i], sends.at[i]
        )
        next(work)
        loads[i].wait()
        next(work)
        stores.append(moves.start(ends.at[i], ends_all.at[spot]))
        stores.append(moves.start(sends.at[i], sends_all.at[2 * spot : 2 * spot + 2]))
    for store in stores:
        store.wait()


def call_on(kernel, scalars, arrays, so_far, out_shape, out_specs, scratch, copies, name):
    count = len(scalars) + len(arrays)
    operands = [array if spec is VMEM else in_hbm(array)[0] for array, spec in arrays]
    specs = [vmem() if spec is VMEM else hbm() for _, spec in arrays]
    return pl.pallas_call(
        kernel,
        in_specs=[smem()] * len(scalars) + specs + [hbm()] * len(so_far),
        out_specs=out_specs,
        out_shape=out_shape,
        input_output_aliases={count + i: i for i in range(len(so_far))},
        scratch_shapes=scratch + [pltpu.SemaphoreType.DMA((copies,))],
        compiler_params=pltpu.CompilerParams(vmem_limit_bytes=VMEM_LIMIT),
        cost_estimate=SMALL,
        name=name,
    )(*scalars, *operands, *in_hbm(*so_far))


def entering_part(tasks, me, place, rates, flags, pieces, x, dy, steps, enter, leave, so_far):
    count, tokens = len(tasks), x.shape[1]
    return call_on(
        functools.partial(entering_kernel, tasks),
        [me, place, rates, flags],
        [(pieces[d], HBM) for _, d in tasks] + [(v, VMEM) for v in (x, dy, steps, enter, leave)],
        so_far,
        [
            hbm_out((GROUPS, 2, tokens, CHUNK), BF16),
            hbm_out((2 * GROUPS, CHUNK + 16, CHUNK), BF16),
        ],
        [hbm()] * 2,
        [
            pltpu.VMEM((count, 2, tokens, CHUNK), BF16),
            pltpu.VMEM((count, 2, tokens, CHUNK), BF16),
            pltpu.VMEM((count, 2, CHUNK + 16, CHUNK), BF16),
        ],
        3 * count,
        "entering_part",
    )


def inner_group(g, rates, maps, x_in, dy_in, steps, bias, kept, rows):
    (write, read), n = (maps.at[0], maps.at[1]), CHUNK
    rate_a, rate_b = -rates[g] * LOG2E, -rates[GROUPS + g] * LOG2E
    low = iota((n, n), 1) < n // 2
    upper = as_mask(iota((n, n), 0) <= iota((n, n), 1))
    columns = [step_columns(steps, k) for k in CHUNKS]
    scores = [dot(read[span_of(k)], write[span_of(k)], NT) for k in CHUNKS]
    u_rows = dot(steps.astype(BF16), upper, NN) * jnp.where(
        iota((8, n), 0) % 2 == 0, rate_a, rate_b
    )
    x = [x_in[g, span_of(k)].astype(F32) for k in CHUNKS]
    dy = [dy_in[g, span_of(k)] for k in CHUNKS]
    stepped = [x[k] * jnp.where(low, columns[k][2], columns[k][3]) for k in CHUNKS]
    pair = [
        jnp.concatenate(
            [jnp.where(low, stepped[k], 0.0), jnp.where(low, 0.0, stepped[k])], axis=0
        ).astype(BF16)
        for k in CHUNKS
    ]
    rounded = [stepped[k].astype(BF16).astype(F32) for k in CHUNKS]
    d_weights = [dot(dy[k], pair[k], NT) for k in CHUNKS]
    falls, weights = [], []
    for k in CHUNKS:
        mask = bias[span_of(k)]
        falls.append(
            (
                jnp.exp2(columns[k][0] * rate_a - u_rows[2 * k : 2 * k + 1] + mask),
                jnp.exp2(columns[k][1] * rate_b - u_rows[2 * k + 1 : 2 * k + 2] + mask),
            )
        )
        weights.append(
            jnp.concatenate([falls[k][0] * scores[k], falls[k][1] * scores[k]], axis=1).astype(BF16)
        )
    inside = [dot(weights[k], pair[k], NN) for k in CHUNKS]
    d_pair = [dot(weights[k], dy[k], TN) for k in CHUNKS]
    d_scores = [
        (d_weights[k][:, :n] * falls[k][0] + d_weights[k][:, n:] * falls[k][1]).astype(BF16)
        for k in CHUNKS
    ]
    d_read = [dot(d_scores[k], write[span_of(k)], NN) for k in CHUNKS]
    d_write = [dot(d_scores[k], read[span_of(k)], TN) for k in CHUNKS]
    d_x = [jnp.where(low, d_pair[k][:n], d_pair[k][n:]) for k in CHUNKS]
    sums = [
        split_dot(head_rows(k), dy[k].astype(F32) * inside[k] - rounded[k] * d_x[k], NT)
        for k in CHUNKS
    ]
    rows[...] = (sums[0] + sums[1]) + (sums[2] + sums[3])
    for k in CHUNKS:
        for i, part in enumerate((inside, d_x, d_write, d_read)):
            kept[i, span_of(k)] = part[k].astype(BF16)


def inner_kernel(tasks, me, place, rates, *refs):
    count = len(tasks)
    maps_in, (x_in, dy_in, steps_in, bias) = refs[:count], refs[count : count + 4]
    kept_all, rows_all, maps, kept, rows, sems = refs[-6:]
    moves = Moves(sems)
    loads = [moves.start(maps_in[i], maps.at[i]) for i in range(count)]
    stores = []
    for i, (spot, d) in enumerate(tasks):
        g = group_of(me, place, d)
        loads[i].wait()
        inner_group(g, rates, maps.at[i], x_in, dy_in, steps_in[g], bias, kept.at[i], rows.at[i])
        stores.append(moves.start(kept.at[i], kept_all.at[spot]))
        stores.append(moves.start(rows.at[i], rows_all.at[spot]))
    for store in stores:
        store.wait()


def inner_part(tasks, me, place, rates, pieces, x, dy, steps, bias, so_far):
    count, tokens = len(tasks), x.shape[1]
    return call_on(
        functools.partial(inner_kernel, tasks),
        [me, place, rates],
        [(pieces[d], HBM) for _, d in tasks] + [(v, VMEM) for v in (x, dy, steps, bias)],
        so_far,
        [
            hbm_out((GROUPS, 4, tokens, CHUNK), BF16),
            hbm_out((GROUPS, 8, CHUNK), F32),
        ],
        [hbm()] * 2,
        [
            pltpu.VMEM((count, 2, tokens, CHUNK), BF16),
            pltpu.VMEM((count, 4, tokens, CHUNK), BF16),
            pltpu.VMEM((count, 8, CHUNK), F32),
        ],
        3 * count,
        "inner_part",
    )


def scan_kernel(got, out):
    half = CHUNK // 2
    count = got.shape[0]
    spans, links, last = [], [], None
    for i in range(count):
        meta = got[i, CHUNK:].astype(F32)
        spans.append(meta[0:1] + meta[1:2])
        same = jnp.zeros_like(meta[2:3]) if last is None else jnp.where(meta[2:3] == last, 1.0, 0.0)
        links.append(same)
        last = meta[3:4]
    state = jnp.zeros((half, CHUNK), F32)
    for i in range(count):
        used = links[i] * state
        out[i, :half] = used.astype(BF16)
        state = spans[i] * used + got[i, :half].astype(F32)
    state = jnp.zeros((half, CHUNK), F32)
    for i in range(count - 1, -1, -1):
        out[i, half:] = state.astype(BF16)
        state = links[i] * (spans[i] * state + got[i, half:CHUNK].astype(F32))


def scan_states(got):
    return pl.pallas_call(
        scan_kernel,
        in_specs=[vmem()],
        out_specs=vmem(),
        out_shape=jax.ShapeDtypeStruct((got.shape[0], CHUNK, CHUNK), BF16),
        compiler_params=pltpu.CompilerParams(vmem_limit_bytes=VMEM_LIMIT),
        name="scan_states",
    )(got)


def final_group(
    g, rates, gains, flags, states, maps, x_in, dy_in, steps, enter, leave, kept, rows_in, ends,
    y_out, dx_out, ds_out, d_maps, wait_first, wait_then
):
    (write, read), n, half = (maps.at[0], maps.at[1]), CHUNK, CHUNK // 2
    dw_out, dr_out = d_maps.at[0], d_maps.at[1]
    low = iota((n, n), 1) < half
    rate_lanes = head_lanes(rates, g, 1) * -LOG2E
    gain_lanes = head_lanes(gains, g, 1)
    rate_rows = head_lanes(rates, g, 0) * -LOG2E
    columns = [step_halves(steps, k) for k in CHUNKS]
    spans = [jnp.exp2(columns[k][2] * rate_rows) * flags[4 + k] for k in CHUNKS]
    step = [columns[k][1] for k in CHUNKS]
    u = [columns[k][0] * rate_lanes for k in CHUNKS]
    into = [jnp.exp2(u[k] + enter[span_of(k)]) for k in CHUNKS]
    out_of = [jnp.exp2(u[k][n - 1 : n] - u[k] + leave[span_of(k)]) for k in CHUNKS]
    wait_first()
    state = jnp.concatenate([states[0, :half], states[1, :half]], axis=0).astype(F32)
    used = [state]
    for k in range(3):
        state = flags[k + 1] * (spans[k] * state + ends[0, span_of(k)].astype(F32))
        used.append(state)
    after = jnp.concatenate([states[0, half:], states[1, half:]], axis=0).astype(F32)
    wanted = [after]
    for k in (3, 2, 1):
        after = flags[k] * (spans[k] * after + ends[1, span_of(k)].astype(F32))
        wanted.insert(0, after)
    used16 = [v.astype(BF16) for v in used]
    wanted16 = [v.astype(BF16) for v in wanted]
    cross = [dot(read[span_of(k)], used16[k], NT) for k in CHUNKS]
    back = [dot(write[span_of(k)], wanted16[k], NT) for k in CHUNKS]
    x = [x_in[g, span_of(k)].astype(F32) for k in CHUNKS]
    dy = [dy_in[g, span_of(k)].astype(F32) for k in CHUNKS]
    rounded = [(x[k] * step[k]).astype(BF16).astype(F32) for k in CHUNKS]
    d_read = [dot((dy[k] * into[k]).astype(BF16), used16[k], NN) for k in CHUNKS]
    d_write = [dot((rounded[k] * out_of[k]).astype(BF16), wanted16[k], NN) for k in CHUNKS]
    cross = [cross[k] * into[k] for k in CHUNKS]
    back = [back[k] * out_of[k] for k in CHUNKS]
    wait_then()
    d_x = [kept[1, span_of(k)].astype(F32) + back[k] for k in CHUNKS]
    select = [head_rows(k) for k in CHUNKS]
    from_all = [split_dot(select[k], spans[k] * wanted[k] * used[k], NN) for k in CHUNKS]
    sums = [split_dot(select[k], dy[k] * cross[k], NT) for k in CHUNKS]
    from_before = [split_dot(select[k], rounded[k] * back[k], NT) for k in CHUNKS]
    straight = [split_dot(select[k], x[k] * d_x[k], NT) for k in CHUNKS]
    for k in CHUNKS:
        at = span_of(k)
        y_out[at] = (kept[0, at].astype(F32) + cross[k] + gain_lanes * x[k]).astype(BF16)
        dx_out[at] = (step[k] * d_x[k] + gain_lanes * dy[k]).astype(BF16)
        dr_out[at] = (kept[3, at].astype(F32) + d_read[k]).astype(BF16)
        dw_out[at] = (kept[2, at].astype(F32) + d_write[k]).astype(BF16)
    lower = as_mask(iota((n, n), 0) >= iota((n, n), 1))
    before = as_mask(iota((n, n), 0) < iota((n, n), 1))
    every = lambda v: (v[0] + v[1]) + (v[2] + v[3])
    joined = jnp.concatenate([rows_in[...] + every(sums), every(from_before), every(from_all)], axis=1)
    table = jnp.concatenate([lower, before, jnp.ones((n, n), BF16)], axis=0)
    high = joined.astype(BF16)
    rest = joined - high.astype(F32)
    middle = rest.astype(BF16)
    low_part = (rest - middle.astype(F32)).astype(BF16)
    d_rate = dot(high, table, NN) + dot(middle, table, NN) + dot(low_part, table, NN)
    rates8 = jnp.where(iota((8, n), 0) % 2 == 0, rates[g], rates[GROUPS + g])
    ds_out[...] = every(straight) - rates8 * d_rate


def final_kernel(tasks, me, place, rates, gains, flags, *refs):
    count = len(tasks)
    maps_in = refs[:count]
    states_in, x_in, dy_in, steps_in, enter, leave, kept_in, rows_in, ends_in = refs[count : count + 9]
    y_all, dx_all, ds_all = refs[-11 - count : -8 - count]
    d_maps = refs[-8 - count : -8]
    maps, kept, rows, ends, y, dx, ds, sems = refs[-8:]
    moves = Moves(sems)
    first = [
        (
            moves.start(maps_in[i], maps.at[i]),
            moves.start(ends_in.at[spot], ends.at[i]),
        )
        for i, (spot, _) in enumerate(tasks)
    ]
    then = [
        (
            moves.start(kept_in.at[spot], kept.at[i]),
            moves.start(rows_in.at[spot], rows.at[i]),
        )
        for i, (spot, _) in enumerate(tasks)
    ]

    def wait_for(copies):
        def wait():
            for copy in copies:
                copy.wait()

        return wait

    stores = []
    for i, (spot, d) in enumerate(tasks):
        g = group_of(me, place, d)
        final_group(
            g, rates, gains, flags, states_in.at[2 * spot : 2 * spot + 2], maps.at[i], x_in, dy_in,
            steps_in[g], enter, leave, kept.at[i], rows.at[i], ends.at[i], y.at[i], dx.at[i], ds.at[i],
            d_maps[i], wait_for(first[i]), wait_for(then[i]),
        )
        stores.append(moves.start(y.at[i], y_all.at[g]))
        stores.append(moves.start(dx.at[i], dx_all.at[g]))
        stores.append(moves.start(ds.at[i], ds_all.at[g]))
    for store in stores:
        store.wait()


def final_part(
    tasks, me, place, rates, gains, flags, states, pieces, x, dy, steps, enter, leave, kept, rows, ends, so_far
):
    count, tokens = len(tasks), x.shape[1]
    wide = hbm_out(x.shape, BF16)
    d_maps = jax.ShapeDtypeStruct((2, tokens, CHUNK), BF16)
    outs = call_on(
        functools.partial(final_kernel, tasks),
        [me, place, rates, gains, flags],
        [(pieces[d], HBM) for _, d in tasks]
        + [(v, VMEM) for v in (states, x, dy, steps, enter, leave)]
        + [(v, HBM) for v in (kept, rows, ends)],
        so_far,
        [wide, wide, hbm_out(steps.shape, F32)] + [d_maps] * count,
        [hbm()] * 3 + [vmem()] * count,
        [
            pltpu.VMEM((count, 2, tokens, CHUNK), BF16),
            pltpu.VMEM((count, 4, tokens, CHUNK), BF16),
            pltpu.VMEM((count, 8, CHUNK), F32),
            pltpu.VMEM((count, 2, tokens, CHUNK), BF16),
            pltpu.VMEM((count, tokens, CHUNK), BF16),
            pltpu.VMEM((count, tokens, CHUNK), BF16),
            pltpu.VMEM((count, 8, CHUNK), F32),
        ],
        7 * count,
        "final_part",
    )
    return outs[:3], outs[3:]


def add_kernel(*refs):
    *terms, out = refs
    total = terms[0][...].astype(F32)
    for term in terms[1:]:
        total = total + term[...].astype(F32)
    out[...] = total.astype(BF16)


def add(*terms):
    return pl.pallas_call(
        add_kernel,
        in_specs=[vmem()] * len(terms),
        out_specs=vmem(),
        out_shape=jax.ShapeDtypeStruct(terms[0].shape, BF16),
        compiler_params=pltpu.CompilerParams(vmem_limit_bytes=VMEM_LIMIT),
        cost_estimate=SMALL,
        name="add",
    )(*terms)


def fetch_halves(src, dst, sems):
    length = src.shape[1] // 2
    loads = []
    for s in range(2):
        at = slice(s * length, (s + 1) * length)
        loads.append(pltpu.make_async_copy(src.at[:, at], dst.at[:, at], sems.at[s]))
        loads[s].start()
    return loads


def spread(groups, s, length, out):
    half = CHUNK // 2
    for g in range(GROUPS):
        block = groups[g, s * length : (s + 1) * length]
        out[s, :, g * half : (g + 1) * half] = block[:, :half]
        out[s, :, (GROUPS + g) * half : (GROUPS + g + 1) * half] = block[:, half:]


def output_columns_kernel(y_hbm, y_out, y_in, y_buf, sems):
    length = y_buf.shape[1]
    loads = fetch_halves(y_hbm, y_in, sems)
    copies = []
    for s in range(2):
        loads[s].wait()
        spread(y_in, s, length, y_buf)
        copies.append(pltpu.make_async_copy(y_buf.at[s], y_out.at[s], sems.at[2 + s]))
        copies[s].start()
    for copy in copies:
        copy.wait()


def output_columns(y):
    shape = (2, y.shape[1] // 2, GROUPS * CHUNK)
    return pl.pallas_call(
        output_columns_kernel,
        in_specs=[hbm()],
        out_specs=hbm(),
        out_shape=hbm_out(shape, BF16),
        scratch_shapes=[
            pltpu.VMEM(y.shape, BF16), pltpu.VMEM(shape, BF16), pltpu.SemaphoreType.DMA((4,))
        ],
        compiler_params=pltpu.CompilerParams(vmem_limit_bytes=VMEM_LIMIT),
        cost_estimate=SMALL,
        name="output_columns",
    )(*in_hbm(y))


def gradient_columns_kernel(dx_hbm, ds_in, dx_out, ds_out, dx_in, sems):
    length = dx_out.shape[1]
    loads = fetch_halves(dx_hbm, dx_in, sems)
    for s in range(2):
        for q in range(2):
            for part in range(2):
                ds_out[
                    s, q * GROUPS : (q + 1) * GROUPS, part * CHUNK : (part + 1) * CHUNK
                ] = ds_in[:, (2 * s + part) * 2 + q, :].astype(BF16)
    for s in range(2):
        loads[s].wait()
        spread(dx_in, s, length, dx_out)


def gradient_columns(dx, ds):
    length = dx.shape[1] // 2
    return pl.pallas_call(
        gradient_columns_kernel,
        in_specs=[hbm(), vmem()],
        out_specs=[vmem()] * 2,
        out_shape=[
            jax.ShapeDtypeStruct((2, length, GROUPS * CHUNK), BF16),
            jax.ShapeDtypeStruct((2, 2 * GROUPS, length), BF16),
        ],
        scratch_shapes=[pltpu.VMEM(dx.shape, BF16), pltpu.SemaphoreType.DMA((2,))],
        compiler_params=pltpu.CompilerParams(vmem_limit_bytes=VMEM_LIMIT),
        cost_estimate=SMALL,
        name="gradient_columns",
    )(*in_hbm(dx), ds)


def settle_kernel(count, routes, place, *refs):
    owns, peers, outs = refs[:count], refs[count : 2 * count], refs[2 * count : 3 * count]
    zeros, sems = refs[3 * count : 4 * count], refs[-1]
    for zero in zeros:
        zero[...] = jnp.zeros_like(zero)
    copies = []
    for m in range(3):
        target = routes[m]
        slot = lax.rem(jnp.maximum(target, 0), 2)
        mine = lax.div(target, 2) == place[0]
        for i in range(count):
            out, sem = outs[i].at[m], sems.at[m * count + i]

            @pl.when(target < 0)
            def _(zero=zeros[i], out=out, sem=sem):
                pltpu.make_async_copy(zero, out, sem).start()

            @pl.when((target >= 0) & mine)
            def _(own=owns[i], out=out, sem=sem):
                pltpu.make_async_copy(own.at[slot], out, sem).start()

            @pl.when((target >= 0) & jnp.logical_not(mine))
            def _(peer=peers[i], out=out, sem=sem):
                pltpu.make_async_copy(peer.at[slot], out, sem).start()

            copies.append(pltpu.make_async_copy(zeros[i], out, sem))
    for copy in copies:
        copy.wait()


def settle(routes, place, owns, peers):
    count = len(owns)
    return pl.pallas_call(
        functools.partial(settle_kernel, count),
        in_specs=[smem()] * 2 + [hbm()] * (2 * count),
        out_specs=[hbm()] * count,
        out_shape=[
            hbm_out((routes.shape[0],) + own.shape[1:], own.dtype) for own in owns
        ],
        scratch_shapes=[pltpu.VMEM(own.shape[1:], own.dtype) for own in owns]
        + [pltpu.SemaphoreType.DMA((3 * count,))],
        compiler_params=pltpu.CompilerParams(vmem_limit_bytes=VMEM_LIMIT),
        cost_estimate=SMALL,
        name="settle",
    )(routes, place, *owns, *peers)


def last_sum_kernel(a, b, c, out):
    length = out.shape[1] // 2
    for i in range(2):
        for s in range(2):
            at = slice(s * length, (s + 1) * length)
            total = a[i, at].astype(F32) + b[i, at].astype(F32) + c[i, at].astype(F32)
            out[s, i * length : (i + 1) * length] = total.astype(BF16)


def last_sum(a, b, c):
    return pl.pallas_call(
        last_sum_kernel,
        in_specs=[vmem()] * 3,
        out_specs=vmem(),
        out_shape=jax.ShapeDtypeStruct(a.shape, BF16),
        compiler_params=pltpu.CompilerParams(vmem_limit_bytes=VMEM_LIMIT),
        cost_estimate=SMALL,
        name="last_sum",
    )(a, b, c)


def settle_maps_kernel(routes, place, own, peer, write, read, zero, sems):
    length = write.shape[1]
    zero[...] = jnp.zeros_like(zero)
    copies = []
    for m in range(3):
        target = routes[m]
        slot = lax.rem(jnp.maximum(target, 0), 2)
        mine = lax.div(target, 2) == place[0]
        for i, result in enumerate((write, read)):
            out, sem, at = result.at[m], sems.at[2 * m + i], slice(i * length, (i + 1) * length)

            @pl.when(target < 0)
            def _(out=out, sem=sem):
                pltpu.make_async_copy(zero, out, sem).start()

            @pl.when((target >= 0) & mine)
            def _(out=out, sem=sem, at=at):
                pltpu.make_async_copy(own.at[slot, at], out, sem).start()

            @pl.when((target >= 0) & jnp.logical_not(mine))
            def _(out=out, sem=sem, at=at):
                pltpu.make_async_copy(peer.at[slot, at], out, sem).start()

            copies.append(pltpu.make_async_copy(zero, out, sem))
    for copy in copies:
        copy.wait()


def settle_maps(routes, place, own, peer):
    shape = (own.shape[1] // 2, own.shape[2])
    return pl.pallas_call(
        settle_maps_kernel,
        in_specs=[smem()] * 2 + [vmem()] * 2,
        out_specs=[hbm()] * 2,
        out_shape=[hbm_out((routes.shape[0],) + shape, BF16)] * 2,
        scratch_shapes=[pltpu.VMEM(shape, BF16), pltpu.SemaphoreType.DMA((6,))],
        compiler_params=pltpu.CompilerParams(vmem_limit_bytes=VMEM_LIMIT),
        cost_estimate=SMALL,
        name="settle_maps",
    )(routes, place, own, peer)


def after(operand, other):
    return lax.optimization_barrier((operand, other))[0]


def shards(
    values, step_sizes, write_map, read_map, decay_rates, skip_gain, routes, segment_ids, grad_out
):
    values, step_sizes = values[0, 0], step_sizes[0, 0]
    write_map, read_map, grad_out = write_map[0, 0], read_map[0, 0], grad_out[0, 0]
    routes = routes[0, 0]
    ring, stream = lax.axis_size("tensor"), lax.axis_size("ctx")
    swap = [(0, 1), (1, 0)]
    me = lax.axis_index("tensor").reshape(1)
    place = lax.axis_index("dp").reshape(1)

    def across(operand):
        return lax.ppermute(operand, "dp", swap)

    def turn(way):
        return [
            (core * ring + i, core * ring + (i + (way if core == 0 else -way)) % ring)
            for core in range(2)
            for i in range(ring)
        ]

    def go_first(operand):
        return lax.ppermute(operand, ("dp", "tensor"), turn(1))

    def go_second(operand):
        return lax.ppermute(operand, ("dp", "tensor"), turn(-1))

    peer_routes = across(routes)
    peer_write, peer_read = across(write_map), across(read_map)
    maps = pick_maps(routes, peer_routes, place, write_map, read_map, peer_write, peer_read)
    bias, enter, leave, flags = make_masks(segment_ids)
    peer_values, peer_steps = across(after(values, maps)), across(after(step_sizes, maps))
    x, steps, dy = pick_values(
        routes, peer_routes, place, values, peer_values, step_sizes, peer_steps, grad_out
    )

    arrival = (0, 1, -1, 2, -2, 3, -3, 4)
    spots = {d: i for i, d in enumerate(arrival)}
    pieces, ends = {0: maps}, []

    def entering(*groups):
        nonlocal ends
        ends = entering_part(
            [(spots[d], d) for d in groups], me, place, decay_rates, flags, pieces,
            x, dy, steps, enter, leave, ends,
        )
        return ends[1]

    pieces[1], pieces[-1] = go_first(maps), go_second(after(maps, bias))
    pieces[2], pieces[-2] = go_first(pieces[1]), go_second(after(pieces[-1], x))
    pieces[3] = go_first(after(pieces[2], entering(0)))
    done = entering(1)
    pieces[-3] = go_second(after(pieces[-2], done))
    pieces[4] = go_first(after(pieces[3], done))
    entering(-1, 2, -2)
    entering(3, -3)
    entering(4)

    inner = []

    def inside(groups, operand):
        nonlocal inner
        inner = inner_part(
            [(spots[d], d) for d in groups], me, place, decay_rates, pieces, operand, dy, steps, bias, inner
        )

    got = lax.all_to_all(ends[1], "ctx", split_axis=0, concat_axis=0, tiled=True)
    inside(arrival[:4], after(x, ends[1]))
    scanned = scan_states(after(got, inner[1]))
    states = lax.all_to_all(scanned, "ctx", split_axis=0, concat_axis=0, tiled=True)
    inside(arrival[4:], after(x, scanned))

    so_far = []

    def final(groups, other=None):
        nonlocal so_far
        operand = x if other is None else after(x, other)
        so_far, d_maps = final_part(
            [(spots[d], d) for d in groups], me, place, decay_rates, skip_gain, flags, states, pieces,
            operand, dy, steps, enter, leave, *inner, ends[0], so_far,
        )
        return d_maps

    (far,) = final((4,))
    far = go_first(far)
    up, down, here = final((-3, 3, 0))
    one, other = add(far, up), down
    one_sent, other_sent = go_first(one), go_second(other)
    up, down = final((-2, 2), (one, other))
    one, other = add(one_sent, up), add(other_sent, down)
    one_sent, other_sent = go_first(one), go_second(other)
    up, down = final((-1, 1), (one, other))
    one, other = add(one_sent, up), add(other_sent, down)
    one_sent, other_sent = go_first(one), go_second(other)
    y_all, dx_all, ds_all = so_far
    grad_values, grad_steps = gradient_columns(*after((dx_all, ds_all), (one, other)))
    output = output_columns(after(y_all, grad_values))
    peer_values, peer_steps = across(grad_values), across(grad_steps)
    back_values, back_steps = settle(
        routes, place, [after(grad_values, output), grad_steps], [peer_values, peer_steps]
    )
    d_maps = last_sum(after(one_sent, back_steps), other_sent, here)
    back_write, back_read = settle_maps(routes, place, d_maps, across(d_maps))
    return tuple(
        array[None, None] for array in (output, back_values, back_steps, back_write, back_read)
    )


def solution(mesh):
    placed = (
        P("dp", "ctx", None, None, "tensor"),
        P("dp", "ctx", None, "tensor", None),
        P("dp", "ctx", None, None, "tensor"),
        P("dp", "ctx", None, None, "tensor"),
        P("tensor"),
        P("tensor"),
        P("dp", "ctx", None),
        P("dp", "ctx"),
        P("dp", "ctx", None, None, "tensor"),
    )
    return jax.shard_map(
        shards,
        mesh=mesh,
        in_specs=placed,
        out_specs=(
            P("dp", "ctx", None, None, "tensor"),
            P("dp", "ctx", None, None, "tensor"),
            P("dp", "ctx", None, "tensor", None),
            P("dp", "ctx", None, None, "tensor"),
            P("dp", "ctx", None, None, "tensor"),
        ),
        check_vma=False,
    )
```

```python
import functools
import math

import jax
import jax.numpy as jnp
from jax import lax
from jax.experimental import pallas as pl
from jax.experimental.pallas import tpu as pltpu
from jax.sharding import PartitionSpec as P

GROUPS = 8
CHUNK = 128
LOG2E = math.log2(math.e)
F32 = jnp.float32
BF16 = jnp.bfloat16
VMEM_LIMIT = 16 * 1024 * 1024
BLOCKED = -1e30
SMALL = pl.CostEstimate(flops=1000, bytes_accessed=1000, transcendentals=0)
HBM, VMEM = "hbm", "vmem"

NN = (((1,), (0,)), ((), ()))
NT = (((1,), (1,)), ((), ()))
TN = (((0,), (0,)), ((), ()))


def dot(a, b, dims):
    return lax.dot_general(a, b, dims, preferred_element_type=F32)


def split_dot(a, b, dims):
    high = b.astype(BF16)
    low = (b - high.astype(F32)).astype(BF16)
    return dot(a, high, dims) + dot(a, low, dims)


def iota(shape, dim):
    return lax.broadcasted_iota(jnp.int32, shape, dim)


def as_mask(condition):
    return jnp.where(condition, 1.0, 0.0).astype(BF16)


def step_rows(steps, k):
    n = CHUNK
    first = jnp.broadcast_to(steps[2 * k : 2 * k + 1], (n, n)).astype(BF16)
    second = jnp.broadcast_to(steps[2 * k + 1 : 2 * k + 2], (n, n)).astype(BF16)
    return first, second


def sums_and_steps():
    n = CHUNK
    lower = as_mask(iota((n, n), 0) >= iota((n, n), 1))
    eye = as_mask(iota((n, n), 0) == iota((n, n), 1))
    return jnp.concatenate([lower, eye], axis=0)


def step_columns(steps, k):
    n = CHUNK
    both = dot(sums_and_steps(), jnp.concatenate(step_rows(steps, k), axis=0), NT)
    return both[:n, :n], both[:n, n:], both[n:, :n], both[n:, n:]


def step_halves(steps, k):
    n = CHUNK
    first, second = step_rows(steps, k)
    halves = jnp.concatenate([first[: n // 2], second[: n // 2]], axis=0)
    both = dot(sums_and_steps(), halves, NT)
    return both[:n], both[n:], dot(halves, jnp.ones((n, n), BF16), NT)


def head_rows(k):
    rows, lanes = iota((8, CHUNK), 0), iota((8, CHUNK), 1)
    return as_mask(rows == 2 * k + (lanes >= CHUNK // 2).astype(jnp.int32))


def smem():
    return pl.BlockSpec(memory_space=pltpu.SMEM)


def vmem():
    return pl.BlockSpec(memory_space=pltpu.VMEM)


def hbm():
    return pl.BlockSpec(memory_space=pltpu.HBM)


def in_hbm(*arrays):
    return [pltpu.with_memory_space_constraint(array, pltpu.HBM) for array in arrays]


def hbm_out(shape, dtype):
    return pltpu.HBM(tuple(shape), dtype)


def slot_of(routes, target):
    slot = jnp.where(routes[1] == target, 1, jnp.where(routes[2] == target, 2, 0))
    return slot, (routes[0] == target) | (slot > 0)


def fetch(own_routes, peer_routes, place, s, own, peer, out, sem):
    target = place[0] * 2 + s
    own_slot, mine = slot_of(own_routes, target)
    peer_slot, _ = slot_of(peer_routes, target)

    @pl.when(mine)
    def _():
        pltpu.make_async_copy(own.at[own_slot], out, sem).start()

    @pl.when(jnp.logical_not(mine))
    def _():
        pltpu.make_async_copy(peer.at[peer_slot], out, sem).start()

    return pltpu.make_async_copy(own.at[0], out, sem)


def pick_maps_kernel(own_routes, peer_routes, place, ow, pw, orr, pr, out, sems):
    length = ow.shape[1]
    pending = []
    for s in range(2):
        for i, (own, peer) in enumerate(((ow, pw), (orr, pr))):
            part = out.at[i, s * length : (s + 1) * length]
            pending.append(
                fetch(own_routes, peer_routes, place, s, own, peer, part, sems.at[2 * s + i])
            )
    for copy in pending:
        copy.wait()


def pick_maps(own_routes, peer_routes, place, write, read, peer_write, peer_read):
    length, state = write.shape[1:]
    return pl.pallas_call(
        pick_maps_kernel,
        in_specs=[smem()] * 3 + [hbm()] * 4,
        out_specs=vmem(),
        out_shape=jax.ShapeDtypeStruct((2, 2 * length, state), BF16),
        scratch_shapes=[pltpu.SemaphoreType.DMA((4,))],
        compiler_params=pltpu.CompilerParams(vmem_limit_bytes=VMEM_LIMIT),
        name="pick_maps",
    )(own_routes, peer_routes, place, *in_hbm(write, peer_write, read, peer_read))


def to_groups(block, out):
    half = CHUNK // 2
    for g in range(GROUPS):
        a = block[:, g * half : (g + 1) * half]
        b = block[:, (GROUPS + g) * half : (GROUPS + g + 1) * half]
        out[g] = jnp.concatenate([a, b], axis=1)


def pick_values_kernel(
    own_routes, peer_routes, place, ox, px, os, ps, dy, x_out, s_out, dy_out,
    x_buf, s_buf, dy_buf, sems,
):
    length = ox.shape[1]
    pending = []
    for s in range(2):
        copy = pltpu.make_async_copy(dy.at[s], dy_buf.at[s], sems.at[3 * s])
        copy.start()
        steps = fetch(own_routes, peer_routes, place, s, os, ps, s_buf.at[s], sems.at[3 * s + 1])
        x = fetch(own_routes, peer_routes, place, s, ox, px, x_buf.at[s], sems.at[3 * s + 2])
        pending.append((copy, steps, x))
    for s in range(2):
        for copy in pending[s]:
            copy.wait()
        at = slice(s * length, (s + 1) * length)
        to_groups(dy_buf[s], dy_out.at[:, at])
        to_groups(x_buf[s], x_out.at[:, at])
        steps = s_buf[s].astype(F32)
        for q in range(2):
            for part in range(2):
                s_out[:, (2 * s + part) * 2 + q, :] = steps[
                    q * GROUPS : (q + 1) * GROUPS, part * CHUNK : (part + 1) * CHUNK
                ]


def pick_values(own_routes, peer_routes, place, values, peer_values, steps, peer_steps, upstream):
    length, columns = values.shape[1:]
    heads = steps.shape[1]
    return pl.pallas_call(
        pick_values_kernel,
        in_specs=[smem()] * 3 + [hbm()] * 5,
        out_specs=[vmem()] * 3,
        out_shape=[
            jax.ShapeDtypeStruct((GROUPS, 2 * length, CHUNK), BF16),
            jax.ShapeDtypeStruct((GROUPS, 8, CHUNK), F32),
            jax.ShapeDtypeStruct((GROUPS, 2 * length, CHUNK), BF16),
        ],
        scratch_shapes=[
            pltpu.VMEM((2, length, columns), BF16),
            pltpu.VMEM((2, heads, length), BF16),
            pltpu.VMEM((2, length, columns), BF16),
            pltpu.SemaphoreType.DMA((6,)),
        ],
        compiler_params=pltpu.CompilerParams(vmem_limit_bytes=VMEM_LIMIT),
        cost_estimate=SMALL,
        name="pick_values",
    )(
        own_routes, peer_routes, place,
        *in_hbm(values, peer_values, steps, peer_steps, upstream),
    )


def masks_kernel(ids, ids_rows, bias, enter, leave, flags):
    n = CHUNK
    eye = as_mask(iota((n, n), 0) == iota((n, n), 1))
    causal = iota((n, n), 0) >= iota((n, n), 1)
    for k in range(4):
        at = slice(k * n, (k + 1) * n)
        row = jnp.broadcast_to(ids_rows[:, at].astype(F32), (n, n))
        column = dot(eye, row.astype(BF16), NT)
        bias[at] = jnp.where((row == column) & causal, 0.0, BLOCKED)
        enter[at] = jnp.where(column == column[0:1], 0.0, BLOCKED)
        leave[at] = jnp.where(column == column[n - 1 : n], 0.0, BLOCKED)
        first, last = ids[0, k * n], ids[0, k * n + n - 1]
        linked = (k > 0) & (ids[0, max(k * n - 1, 0)] == first)
        flags[k] = jnp.where(linked, 1.0, 0.0)
        flags[4 + k] = jnp.where(first == last, 1.0, 0.0)
    flags[8] = ids[0, 0].astype(F32)
    flags[9] = ids[0, 4 * n - 1].astype(F32)


def make_masks(ids):
    wide = jax.ShapeDtypeStruct((4 * CHUNK, CHUNK), F32)
    return pl.pallas_call(
        masks_kernel,
        in_specs=[smem(), vmem()],
        out_specs=[vmem()] * 3 + [smem()],
        out_shape=[wide] * 3 + [jax.ShapeDtypeStruct((10,), F32)],
        compiler_params=pltpu.CompilerParams(vmem_limit_bytes=VMEM_LIMIT),
        cost_estimate=SMALL,
        name="make_masks",
    )(ids, ids)


CHUNKS = range(4)


def span_of(k):
    return slice(k * CHUNK, (k + 1) * CHUNK)


class Moves:
    def __init__(self, sems):
        self.sems, self.count = sems, 0

    def start(self, src, dst):
        copy = pltpu.make_async_copy(src, dst, self.sems.at[self.count])
        self.count += 1
        copy.start()
        return copy


def group_of(me, place, d):
    return lax.rem(me[0] + (2 * place[0] - 1) * d + GROUPS, GROUPS)


def head_lanes(per_head, g, axis):
    shape = (CHUNK, CHUNK)
    return jnp.where(iota(shape, axis) < CHUNK // 2, per_head[g], per_head[GROUPS + g])


def entering_group(g, rates, flags, maps, x_in, dy_in, steps, enter, leave, kept, send_out):
    (write, read), n, half = (maps.at[0], maps.at[1]), CHUNK, CHUNK // 2
    rate_lanes = head_lanes(rates, g, 1) * -LOG2E
    rate_rows = head_lanes(rates, g, 0) * -LOG2E
    columns = [step_halves(steps, k) for k in CHUNKS]
    u = [columns[k][0] * rate_lanes for k in CHUNKS]
    into = [jnp.exp2(u[k] + enter[span_of(k)]) for k in CHUNKS]
    out_of = [jnp.exp2(u[k][n - 1 : n] - u[k] + leave[span_of(k)]) for k in CHUNKS]
    rounded = [
        (x_in[g, span_of(k)].astype(F32) * columns[k][1]).astype(BF16).astype(F32) for k in CHUNKS
    ]
    scaled = [(rounded[k] * out_of[k]).astype(BF16) for k in CHUNKS]
    carried = [(dy_in[g, span_of(k)].astype(F32) * into[k]).astype(BF16) for k in CHUNKS]
    spans = [jnp.exp2(columns[k][2] * rate_rows) * flags[4 + k] for k in CHUNKS]
    yield
    locals_ = [dot(scaled[k], write[span_of(k)], TN) for k in CHUNKS]
    directs = [dot(carried[k], read[span_of(k)], TN) for k in CHUNKS]
    for k in CHUNKS:
        kept[0, span_of(k)] = locals_[k].astype(BF16)
        kept[1, span_of(k)] = directs[k].astype(BF16)
    end, span = locals_[0], spans[0]
    for k in range(1, 4):
        factor = spans[k] * flags[k]
        end = factor * end + locals_[k]
        span = factor * span
    begin = directs[3]
    for k in (2, 1, 0):
        begin = flags[k + 1] * spans[k] * begin + directs[k]
    row = iota((16, n), 0)
    for q in range(2):
        part = slice(q * half, (q + 1) * half)
        send_out[q, :half] = end[part].astype(BF16)
        send_out[q, half:n] = begin[part].astype(BF16)
        one = span[q * half : q * half + 1]
        rest = one - one.astype(BF16).astype(F32)
        ids = jnp.where(row == 2, flags[8], jnp.where(row == 3, flags[9], 0.0))
        meta = jnp.where(row == 0, one, jnp.where(row == 1, rest, ids))
        send_out[q, n:] = meta.astype(BF16)
    yield


def entering_kernel(tasks, me, place, rates, flags, *refs):
    count = len(tasks)
    maps_in, (x_in, dy_in, steps_in, enter, leave) = refs[:count], refs[count : count + 5]
    ends_all, sends_all, maps, ends, sends, sems = refs[-6:]
    moves = Moves(sems)
    loads = [moves.start(maps_in[i], maps.at[i]) for i in range(count)]
    stores = []
    for i, (spot, d) in enumerate(tasks):
        g = group_of(me, place, d)
        work = entering_group(
            g, rates, flags, maps.at[i], x_in, dy_in, steps_in[g], enter, leave, ends.at[i], sends.at[i]
        )
        next(work)
        loads[i].wait()
        next(work)
        stores.append(moves.start(ends.at[i], ends_all.at[spot]))
        stores.append(moves.start(sends.at[i], sends_all.at[2 * spot : 2 * spot + 2]))
    for store in stores:
        store.wait()


def call_on(kernel, scalars, arrays, so_far, out_shape, out_specs, scratch, copies, name):
    count = len(scalars) + len(arrays)
    operands = [array if spec is VMEM else in_hbm(array)[0] for array, spec in arrays]
    specs = [vmem() if spec is VMEM else hbm() for _, spec in arrays]
    return pl.pallas_call(
        kernel,
        in_specs=[smem()] * len(scalars) + specs + [hbm()] * len(so_far),
        out_specs=out_specs,
        out_shape=out_shape,
        input_output_aliases={count + i: i for i in range(len(so_far))},
        scratch_shapes=scratch + [pltpu.SemaphoreType.DMA((copies,))],
        compiler_params=pltpu.CompilerParams(vmem_limit_bytes=VMEM_LIMIT),
        cost_estimate=SMALL,
        name=name,
    )(*scalars, *operands, *in_hbm(*so_far))


def entering_part(tasks, me, place, rates, flags, pieces, x, dy, steps, enter, leave, so_far):
    count, tokens = len(tasks), x.shape[1]
    return call_on(
        functools.partial(entering_kernel, tasks),
        [me, place, rates, flags],
        [(pieces[d], HBM) for _, d in tasks] + [(v, VMEM) for v in (x, dy, steps, enter, leave)],
        so_far,
        [
            hbm_out((GROUPS, 2, tokens, CHUNK), BF16),
            hbm_out((2 * GROUPS, CHUNK + 16, CHUNK), BF16),
        ],
        [hbm()] * 2,
        [
            pltpu.VMEM((count, 2, tokens, CHUNK), BF16),
            pltpu.VMEM((count, 2, tokens, CHUNK), BF16),
            pltpu.VMEM((count, 2, CHUNK + 16, CHUNK), BF16),
        ],
        3 * count,
        "entering_part",
    )


def inner_group(g, rates, maps, x_in, dy_in, steps, bias, kept, rows):
    (write, read), n = (maps.at[0], maps.at[1]), CHUNK
    rate_a, rate_b = -rates[g] * LOG2E, -rates[GROUPS + g] * LOG2E
    low = iota((n, n), 1) < n // 2
    upper = as_mask(iota((n, n), 0) <= iota((n, n), 1))
    columns = [step_columns(steps, k) for k in CHUNKS]
    scores = [dot(read[span_of(k)], write[span_of(k)], NT) for k in CHUNKS]
    u_rows = dot(steps.astype(BF16), upper, NN) * jnp.where(
        iota((8, n), 0) % 2 == 0, rate_a, rate_b
    )
    x = [x_in[g, span_of(k)].astype(F32) for k in CHUNKS]
    dy = [dy_in[g, span_of(k)] for k in CHUNKS]
    stepped = [x[k] * jnp.where(low, columns[k][2], columns[k][3]) for k in CHUNKS]
    pair = [
        jnp.concatenate(
            [jnp.where(low, stepped[k], 0.0), jnp.where(low, 0.0, stepped[k])], axis=0
        ).astype(BF16)
        for k in CHUNKS
    ]
    rounded = [stepped[k].astype(BF16).astype(F32) for k in CHUNKS]
    d_weights = [dot(dy[k], pair[k], NT) for k in CHUNKS]
    falls, weights = [], []
    for k in CHUNKS:
        mask = bias[span_of(k)]
        falls.append(
            (
                jnp.exp2(columns[k][0] * rate_a - u_rows[2 * k : 2 * k + 1] + mask),
                jnp.exp2(columns[k][1] * rate_b - u_rows[2 * k + 1 : 2 * k + 2] + mask),
            )
        )
        weights.append(
            jnp.concatenate([falls[k][0] * scores[k], falls[k][1] * scores[k]], axis=1).astype(BF16)
        )
    inside = [dot(weights[k], pair[k], NN) for k in CHUNKS]
    d_pair = [dot(weights[k], dy[k], TN) for k in CHUNKS]
    d_scores = [
        (d_weights[k][:, :n] * falls[k][0] + d_weights[k][:, n:] * falls[k][1]).astype(BF16)
        for k in CHUNKS
    ]
    d_read = [dot(d_scores[k], write[span_of(k)], NN) for k in CHUNKS]
    d_write = [dot(d_scores[k], read[span_of(k)], TN) for k in CHUNKS]
    d_x = [jnp.where(low, d_pair[k][:n], d_pair[k][n:]) for k in CHUNKS]
    sums = [
        split_dot(head_rows(k), dy[k].astype(F32) * inside[k] - rounded[k] * d_x[k], NT)
        for k in CHUNKS
    ]
    rows[...] = (sums[0] + sums[1]) + (sums[2] + sums[3])
    for k in CHUNKS:
        for i, part in enumerate((inside, d_x, d_write, d_read)):
            kept[i, span_of(k)] = part[k].astype(BF16)


def inner_kernel(tasks, me, place, rates, *refs):
    count = len(tasks)
    maps_in, (x_in, dy_in, steps_in, bias) = refs[:count], refs[count : count + 4]
    kept_all, rows_all, maps, kept, rows, sems = refs[-6:]
    moves = Moves(sems)
    loads = [moves.start(maps_in[i], maps.at[i]) for i in range(count)]
    stores = []
    for i, (spot, d) in enumerate(tasks):
        g = group_of(me, place, d)
        loads[i].wait()
        inner_group(g, rates, maps.at[i], x_in, dy_in, steps_in[g], bias, kept.at[i], rows.at[i])
        stores.append(moves.start(kept.at[i], kept_all.at[spot]))
        stores.append(moves.start(rows.at[i], rows_all.at[spot]))
    for store in stores:
        store.wait()


def inner_part(tasks, me, place, rates, pieces, x, dy, steps, bias, so_far):
    count, tokens = len(tasks), x.shape[1]
    return call_on(
        functools.partial(inner_kernel, tasks),
        [me, place, rates],
        [(pieces[d], HBM) for _, d in tasks] + [(v, VMEM) for v in (x, dy, steps, bias)],
        so_far,
        [
            hbm_out((GROUPS, 4, tokens, CHUNK), BF16),
            hbm_out((GROUPS, 8, CHUNK), F32),
        ],
        [hbm()] * 2,
        [
            pltpu.VMEM((count, 2, tokens, CHUNK), BF16),
            pltpu.VMEM((count, 4, tokens, CHUNK), BF16),
            pltpu.VMEM((count, 8, CHUNK), F32),
        ],
        3 * count,
        "inner_part",
    )


def scan_kernel(got, out):
    half = CHUNK // 2
    count = got.shape[0]
    spans, links, last = [], [], None
    for i in range(count):
        meta = got[i, CHUNK:].astype(F32)
        spans.append(meta[0:1] + meta[1:2])
        same = jnp.zeros_like(meta[2:3]) if last is None else jnp.where(meta[2:3] == last, 1.0, 0.0)
        links.append(same)
        last = meta[3:4]
    state = jnp.zeros((half, CHUNK), F32)
    for i in range(count):
        used = links[i] * state
        out[i, :half] = used.astype(BF16)
        state = spans[i] * used + got[i, :half].astype(F32)
    state = jnp.zeros((half, CHUNK), F32)
    for i in range(count - 1, -1, -1):
        out[i, half:] = state.astype(BF16)
        state = links[i] * (spans[i] * state + got[i, half:CHUNK].astype(F32))


def scan_states(got):
    return pl.pallas_call(
        scan_kernel,
        in_specs=[vmem()],
        out_specs=vmem(),
        out_shape=jax.ShapeDtypeStruct((got.shape[0], CHUNK, CHUNK), BF16),
        compiler_params=pltpu.CompilerParams(vmem_limit_bytes=VMEM_LIMIT),
        name="scan_states",
    )(got)


def final_group(
    g, rates, gains, flags, states, maps, x_in, dy_in, steps, enter, leave, kept, rows_in, ends,
    y_out, dx_out, ds_out, d_maps, wait_first, wait_then
):
    (write, read), n, half = (maps.at[0], maps.at[1]), CHUNK, CHUNK // 2
    dw_out, dr_out = d_maps.at[0], d_maps.at[1]
    low = iota((n, n), 1) < half
    rate_lanes = head_lanes(rates, g, 1) * -LOG2E
    gain_lanes = head_lanes(gains, g, 1)
    rate_rows = head_lanes(rates, g, 0) * -LOG2E
    columns = [step_halves(steps, k) for k in CHUNKS]
    spans = [jnp.exp2(columns[k][2] * rate_rows) * flags[4 + k] for k in CHUNKS]
    step = [columns[k][1] for k in CHUNKS]
    u = [columns[k][0] * rate_lanes for k in CHUNKS]
    into = [jnp.exp2(u[k] + enter[span_of(k)]) for k in CHUNKS]
    out_of = [jnp.exp2(u[k][n - 1 : n] - u[k] + leave[span_of(k)]) for k in CHUNKS]
    wait_first()
    state = jnp.concatenate([states[0, :half], states[1, :half]], axis=0).astype(F32)
    used = [state]
    for k in range(3):
        state = flags[k + 1] * (spans[k] * state + ends[0, span_of(k)].astype(F32))
        used.append(state)
    after = jnp.concatenate([states[0, half:], states[1, half:]], axis=0).astype(F32)
    wanted = [after]
    for k in (3, 2, 1):
        after = flags[k] * (spans[k] * after + ends[1, span_of(k)].astype(F32))
        wanted.insert(0, after)
    used16 = [v.astype(BF16) for v in used]
    wanted16 = [v.astype(BF16) for v in wanted]
    cross = [dot(read[span_of(k)], used16[k], NT) for k in CHUNKS]
    back = [dot(write[span_of(k)], wanted16[k], NT) for k in CHUNKS]
    x = [x_in[g, span_of(k)].astype(F32) for k in CHUNKS]
    dy = [dy_in[g, span_of(k)].astype(F32) for k in CHUNKS]
    rounded = [(x[k] * step[k]).astype(BF16).astype(F32) for k in CHUNKS]
    d_read = [dot((dy[k] * into[k]).astype(BF16), used16[k], NN) for k in CHUNKS]
    d_write = [dot((rounded[k] * out_of[k]).astype(BF16), wanted16[k], NN) for k in CHUNKS]
    cross = [cross[k] * into[k] for k in CHUNKS]
    back = [back[k] * out_of[k] for k in CHUNKS]
    wait_then()
    d_x = [kept[1, span_of(k)].astype(F32) + back[k] for k in CHUNKS]
    select = [head_rows(k) for k in CHUNKS]
    from_all = [split_dot(select[k], spans[k] * wanted[k] * used[k], NN) for k in CHUNKS]
    sums = [split_dot(select[k], dy[k] * cross[k], NT) for k in CHUNKS]
    from_before = [split_dot(select[k], rounded[k] * back[k], NT) for k in CHUNKS]
    straight = [split_dot(select[k], x[k] * d_x[k], NT) for k in CHUNKS]
    for k in CHUNKS:
        at = span_of(k)
        y_out[at] = (kept[0, at].astype(F32) + cross[k] + gain_lanes * x[k]).astype(BF16)
        dx_out[at] = (step[k] * d_x[k] + gain_lanes * dy[k]).astype(BF16)
        dr_out[at] = (kept[3, at].astype(F32) + d_read[k]).astype(BF16)
        dw_out[at] = (kept[2, at].astype(F32) + d_write[k]).astype(BF16)
    lower = as_mask(iota((n, n), 0) >= iota((n, n), 1))
    before = as_mask(iota((n, n), 0) < iota((n, n), 1))
    every = lambda v: (v[0] + v[1]) + (v[2] + v[3])
    joined = jnp.concatenate([rows_in[...] + every(sums), every(from_before), every(from_all)], axis=1)
    table = jnp.concatenate([lower, before, jnp.ones((n, n), BF16)], axis=0)
    high = joined.astype(BF16)
    rest = joined - high.astype(F32)
    middle = rest.astype(BF16)
    low_part = (rest - middle.astype(F32)).astype(BF16)
    d_rate = dot(high, table, NN) + dot(middle, table, NN) + dot(low_part, table, NN)
    rates8 = jnp.where(iota((8, n), 0) % 2 == 0, rates[g], rates[GROUPS + g])
    ds_out[...] = every(straight) - rates8 * d_rate


def final_kernel(tasks, me, place, rates, gains, flags, *refs):
    count = len(tasks)
    maps_in = refs[:count]
    states_in, x_in, dy_in, steps_in, enter, leave, kept_in, rows_in, ends_in = refs[count : count + 9]
    y_all, dx_all, ds_all = refs[-11 - count : -8 - count]
    d_maps = refs[-8 - count : -8]
    maps, kept, rows, ends, y, dx, ds, sems = refs[-8:]
    moves = Moves(sems)
    first = [
        (
            moves.start(maps_in[i], maps.at[i]),
            moves.start(ends_in.at[spot], ends.at[i]),
        )
        for i, (spot, _) in enumerate(tasks)
    ]
    then = [
        (
            moves.start(kept_in.at[spot], kept.at[i]),
            moves.start(rows_in.at[spot], rows.at[i]),
        )
        for i, (spot, _) in enumerate(tasks)
    ]

    def wait_for(copies):
        def wait():
            for copy in copies:
                copy.wait()

        return wait

    stores = []
    for i, (spot, d) in enumerate(tasks):
        g = group_of(me, place, d)
        final_group(
            g, rates, gains, flags, states_in.at[2 * spot : 2 * spot + 2], maps.at[i], x_in, dy_in,
            steps_in[g], enter, leave, kept.at[i], rows.at[i], ends.at[i], y.at[i], dx.at[i], ds.at[i],
            d_maps[i], wait_for(first[i]), wait_for(then[i]),
        )
        stores.append(moves.start(y.at[i], y_all.at[g]))
        stores.append(moves.start(dx.at[i], dx_all.at[g]))
        stores.append(moves.start(ds.at[i], ds_all.at[g]))
    for store in stores:
        store.wait()


def final_part(
    tasks, me, place, rates, gains, flags, states, pieces, x, dy, steps, enter, leave, kept, rows, ends, so_far
):
    count, tokens = len(tasks), x.shape[1]
    wide = hbm_out(x.shape, BF16)
    d_maps = jax.ShapeDtypeStruct((2, tokens, CHUNK), BF16)
    outs = call_on(
        functools.partial(final_kernel, tasks),
        [me, place, rates, gains, flags],
        [(pieces[d], HBM) for _, d in tasks]
        + [(v, VMEM) for v in (states, x, dy, steps, enter, leave)]
        + [(v, HBM) for v in (kept, rows, ends)],
        so_far,
        [wide, wide, hbm_out(steps.shape, F32)] + [d_maps] * count,
        [hbm()] * 3 + [vmem()] * count,
        [
            pltpu.VMEM((count, 2, tokens, CHUNK), BF16),
            pltpu.VMEM((count, 4, tokens, CHUNK), BF16),
            pltpu.VMEM((count, 8, CHUNK), F32),
            pltpu.VMEM((count, 2, tokens, CHUNK), BF16),
            pltpu.VMEM((count, tokens, CHUNK), BF16),
            pltpu.VMEM((count, tokens, CHUNK), BF16),
            pltpu.VMEM((count, 8, CHUNK), F32),
        ],
        7 * count,
        "final_part",
    )
    return outs[:3], outs[3:]


def add_kernel(*refs):
    *terms, out = refs
    total = terms[0][...].astype(F32)
    for term in terms[1:]:
        total = total + term[...].astype(F32)
    out[...] = total.astype(BF16)


def add(*terms):
    return pl.pallas_call(
        add_kernel,
        in_specs=[vmem()] * len(terms),
        out_specs=vmem(),
        out_shape=jax.ShapeDtypeStruct(terms[0].shape, BF16),
        compiler_params=pltpu.CompilerParams(vmem_limit_bytes=VMEM_LIMIT),
        cost_estimate=SMALL,
        name="add",
    )(*terms)


def fetch_halves(src, dst, sems):
    length = src.shape[1] // 2
    loads = []
    for s in range(2):
        at = slice(s * length, (s + 1) * length)
        loads.append(pltpu.make_async_copy(src.at[:, at], dst.at[:, at], sems.at[s]))
        loads[s].start()
    return loads


def spread(groups, s, length, out):
    half = CHUNK // 2
    for g in range(GROUPS):
        block = groups[g, s * length : (s + 1) * length]
        out[s, :, g * half : (g + 1) * half] = block[:, :half]
        out[s, :, (GROUPS + g) * half : (GROUPS + g + 1) * half] = block[:, half:]


def output_columns_kernel(y_hbm, y_out, y_in, y_buf, sems):
    length = y_buf.shape[1]
    loads = fetch_halves(y_hbm, y_in, sems)
    copies = []
    for s in range(2):
        loads[s].wait()
        spread(y_in, s, length, y_buf)
        copies.append(pltpu.make_async_copy(y_buf.at[s], y_out.at[s], sems.at[2 + s]))
        copies[s].start()
    for copy in copies:
        copy.wait()


def output_columns(y):
    shape = (2, y.shape[1] // 2, GROUPS * CHUNK)
    return pl.pallas_call(
        output_columns_kernel,
        in_specs=[hbm()],
        out_specs=hbm(),
        out_shape=hbm_out(shape, BF16),
        scratch_shapes=[
            pltpu.VMEM(y.shape, BF16), pltpu.VMEM(shape, BF16), pltpu.SemaphoreType.DMA((4,))
        ],
        compiler_params=pltpu.CompilerParams(vmem_limit_bytes=VMEM_LIMIT),
        cost_estimate=SMALL,
        name="output_columns",
    )(*in_hbm(y))


def gradient_columns_kernel(dx_hbm, ds_in, dx_out, ds_out, dx_in, sems):
    length = dx_out.shape[1]
    loads = fetch_halves(dx_hbm, dx_in, sems)
    for s in range(2):
        for q in range(2):
            for part in range(2):
                ds_out[
                    s, q * GROUPS : (q + 1) * GROUPS, part * CHUNK : (part + 1) * CHUNK
                ] = ds_in[:, (2 * s + part) * 2 + q, :].astype(BF16)
    for s in range(2):
        loads[s].wait()
        spread(dx_in, s, length, dx_out)


def gradient_columns(dx, ds):
    length = dx.shape[1] // 2
    return pl.pallas_call(
        gradient_columns_kernel,
        in_specs=[hbm(), vmem()],
        out_specs=[vmem()] * 2,
        out_shape=[
            jax.ShapeDtypeStruct((2, length, GROUPS * CHUNK), BF16),
            jax.ShapeDtypeStruct((2, 2 * GROUPS, length), BF16),
        ],
        scratch_shapes=[pltpu.VMEM(dx.shape, BF16), pltpu.SemaphoreType.DMA((2,))],
        compiler_params=pltpu.CompilerParams(vmem_limit_bytes=VMEM_LIMIT),
        cost_estimate=SMALL,
        name="gradient_columns",
    )(*in_hbm(dx), ds)


def settle_kernel(count, routes, place, *refs):
    owns, peers, outs = refs[:count], refs[count : 2 * count], refs[2 * count : 3 * count]
    zeros, sems = refs[3 * count : 4 * count], refs[-1]
    for zero in zeros:
        zero[...] = jnp.zeros_like(zero)
    copies = []
    for m in range(3):
        target = routes[m]
        slot = lax.rem(jnp.maximum(target, 0), 2)
        mine = lax.div(target, 2) == place[0]
        for i in range(count):
            out, sem = outs[i].at[m], sems.at[m * count + i]

            @pl.when(target < 0)
            def _(zero=zeros[i], out=out, sem=sem):
                pltpu.make_async_copy(zero, out, sem).start()

            @pl.when((target >= 0) & mine)
            def _(own=owns[i], out=out, sem=sem):
                pltpu.make_async_copy(own.at[slot], out, sem).start()

            @pl.when((target >= 0) & jnp.logical_not(mine))
            def _(peer=peers[i], out=out, sem=sem):
                pltpu.make_async_copy(peer.at[slot], out, sem).start()

            copies.append(pltpu.make_async_copy(zeros[i], out, sem))
    for copy in copies:
        copy.wait()


def settle(routes, place, owns, peers):
    count = len(owns)
    return pl.pallas_call(
        functools.partial(settle_kernel, count),
        in_specs=[smem()] * 2 + [hbm()] * (2 * count),
        out_specs=[hbm()] * count,
        out_shape=[
            hbm_out((routes.shape[0],) + own.shape[1:], own.dtype) for own in owns
        ],
        scratch_shapes=[pltpu.VMEM(own.shape[1:], own.dtype) for own in owns]
        + [pltpu.SemaphoreType.DMA((3 * count,))],
        compiler_params=pltpu.CompilerParams(vmem_limit_bytes=VMEM_LIMIT),
        cost_estimate=SMALL,
        name="settle",
    )(routes, place, *owns, *peers)


def last_sum_kernel(a, b, c, out):
    length = out.shape[1] // 2
    for i in range(2):
        for s in range(2):
            at = slice(s * length, (s + 1) * length)
            total = a[i, at].astype(F32) + b[i, at].astype(F32) + c[i, at].astype(F32)
            out[s, i * length : (i + 1) * length] = total.astype(BF16)


def last_sum(a, b, c):
    return pl.pallas_call(
        last_sum_kernel,
        in_specs=[vmem()] * 3,
        out_specs=vmem(),
        out_shape=jax.ShapeDtypeStruct(a.shape, BF16),
        compiler_params=pltpu.CompilerParams(vmem_limit_bytes=VMEM_LIMIT),
        cost_estimate=SMALL,
        name="last_sum",
    )(a, b, c)


def settle_maps_kernel(routes, place, own, peer, write, read, zero, sems):
    length = write.shape[1]
    zero[...] = jnp.zeros_like(zero)
    copies = []
    for m in range(3):
        target = routes[m]
        slot = lax.rem(jnp.maximum(target, 0), 2)
        mine = lax.div(target, 2) == place[0]
        for i, result in enumerate((write, read)):
            out, sem, at = result.at[m], sems.at[2 * m + i], slice(i * length, (i + 1) * length)

            @pl.when(target < 0)
            def _(out=out, sem=sem):
                pltpu.make_async_copy(zero, out, sem).start()

            @pl.when((target >= 0) & mine)
            def _(out=out, sem=sem, at=at):
                pltpu.make_async_copy(own.at[slot, at], out, sem).start()

            @pl.when((target >= 0) & jnp.logical_not(mine))
            def _(out=out, sem=sem, at=at):
                pltpu.make_async_copy(peer.at[slot, at], out, sem).start()

            copies.append(pltpu.make_async_copy(zero, out, sem))
    for copy in copies:
        copy.wait()


def settle_maps(routes, place, own, peer):
    shape = (own.shape[1] // 2, own.shape[2])
    return pl.pallas_call(
        settle_maps_kernel,
        in_specs=[smem()] * 2 + [vmem()] * 2,
        out_specs=[hbm()] * 2,
        out_shape=[hbm_out((routes.shape[0],) + shape, BF16)] * 2,
        scratch_shapes=[pltpu.VMEM(shape, BF16), pltpu.SemaphoreType.DMA((6,))],
        compiler_params=pltpu.CompilerParams(vmem_limit_bytes=VMEM_LIMIT),
        cost_estimate=SMALL,
        name="settle_maps",
    )(routes, place, own, peer)


def after(operand, other):
    return lax.optimization_barrier((operand, other))[0]


def shards(
    values, step_sizes, write_map, read_map, decay_rates, skip_gain, routes, segment_ids, grad_out
):
    values, step_sizes = values[0, 0], step_sizes[0, 0]
    write_map, read_map, grad_out = write_map[0, 0], read_map[0, 0], grad_out[0, 0]
    routes = routes[0, 0]
    ring, stream = lax.axis_size("tensor"), lax.axis_size("ctx")
    swap = [(0, 1), (1, 0)]
    me = lax.axis_index("tensor").reshape(1)
    place = lax.axis_index("dp").reshape(1)

    def across(operand):
        return lax.ppermute(operand, "dp", swap)

    def turn(way):
        return [
            (core * ring + i, core * ring + (i + (way if core == 0 else -way)) % ring)
            for core in range(2)
            for i in range(ring)
        ]

    def go_first(operand):
        return lax.ppermute(operand, ("dp", "tensor"), turn(1))

    def go_second(operand):
        return lax.ppermute(operand, ("dp", "tensor"), turn(-1))

    peer_routes = across(routes)
    peer_write, peer_read = across(write_map), across(read_map)
    maps = pick_maps(routes, peer_routes, place, write_map, read_map, peer_write, peer_read)
    bias, enter, leave, flags = make_masks(segment_ids)
    peer_values, peer_steps = across(after(values, maps)), across(after(step_sizes, maps))
    x, steps, dy = pick_values(
        routes, peer_routes, place, values, peer_values, step_sizes, peer_steps, grad_out
    )

    arrival = (0, 1, -1, 2, -2, 3, -3, 4)
    spots = {d: i for i, d in enumerate(arrival)}
    pieces, ends = {0: maps}, []

    def entering(*groups):
        nonlocal ends
        ends = entering_part(
            [(spots[d], d) for d in groups], me, place, decay_rates, flags, pieces,
            x, dy, steps, enter, leave, ends,
        )
        return ends[1]

    pieces[1], pieces[-1] = go_first(maps), go_second(after(maps, bias))
    pieces[2], pieces[-2] = go_first(pieces[1]), go_second(after(pieces[-1], x))
    pieces[3] = go_first(after(pieces[2], entering(0)))
    done = entering(1)
    pieces[-3] = go_second(after(pieces[-2], done))
    pieces[4] = go_first(after(pieces[3], done))
    entering(-1, 2, -2)
    entering(3, -3)
    entering(4)

    inner = []

    def inside(groups, operand):
        nonlocal inner
        inner = inner_part(
            [(spots[d], d) for d in groups], me, place, decay_rates, pieces, operand, dy, steps, bias, inner
        )

    got = lax.all_to_all(ends[1], "ctx", split_axis=0, concat_axis=0, tiled=True)
    inside(arrival[:4], after(x, ends[1]))
    scanned = scan_states(after(got, inner[1]))
    states = lax.all_to_all(scanned, "ctx", split_axis=0, concat_axis=0, tiled=True)
    inside(arrival[4:], after(x, scanned))

    so_far = []

    def final(groups, other=None):
        nonlocal so_far
        operand = x if other is None else after(x, other)
        so_far, d_maps = final_part(
            [(spots[d], d) for d in groups], me, place, decay_rates, skip_gain, flags, states, pieces,
            operand, dy, steps, enter, leave, *inner, ends[0], so_far,
        )
        return d_maps

    (far,) = final((4,))
    far = go_first(far)
    up, down, here = final((-3, 3, 0))
    one, other = add(far, up), down
    one_sent, other_sent = go_first(one), go_second(other)
    up, down = final((-2, 2), (one, other))
    one, other = add(one_sent, up), add(other_sent, down)
    one_sent, other_sent = go_first(one), go_second(other)
    up, down = final((-1, 1), (one, other))
    one, other = add(one_sent, up), add(other_sent, down)
    one_sent, other_sent = go_first(one), go_second(other)
    y_all, dx_all, ds_all = so_far
    output = output_columns(after(y_all, (one, other)))
    grad_values, grad_steps = gradient_columns(*after((dx_all, ds_all), (one_sent, output)))
    peer_values, peer_steps = across(grad_values), across(grad_steps)
    back_values, back_steps = settle(
        routes, place, [grad_values, grad_steps], [peer_values, peer_steps]
    )
    d_maps = last_sum(after(one_sent, back_steps), other_sent, here)
    back_write, back_read = settle_maps(routes, place, d_maps, across(d_maps))
    return tuple(
        array[None, None] for array in (output, back_values, back_steps, back_write, back_read)
    )


def solution(mesh):
    placed = (
        P("dp", "ctx", None, None, "tensor"),
        P("dp", "ctx", None, "tensor", None),
        P("dp", "ctx", None, None, "tensor"),
        P("dp", "ctx", None, None, "tensor"),
        P("tensor"),
        P("tensor"),
        P("dp", "ctx", None),
        P("dp", "ctx"),
        P("dp", "ctx", None, None, "tensor"),
    )
    return jax.shard_map(
        shards,
        mesh=mesh,
        in_specs=placed,
        out_specs=(
            P("dp", "ctx", None, None, "tensor"),
            P("dp", "ctx", None, None, "tensor"),
            P("dp", "ctx", None, "tensor", None),
            P("dp", "ctx", None, None, "tensor"),
            P("dp", "ctx", None, None, "tensor"),
        ),
        check_vma=False,
    )
```

```python
import functools
import math

import jax
import jax.numpy as jnp
from jax import lax
from jax.experimental import pallas as pl
from jax.experimental.pallas import tpu as pltpu
from jax.sharding import PartitionSpec as P

GROUPS = 8
CHUNK = 128
LOG2E = math.log2(math.e)
F32 = jnp.float32
BF16 = jnp.bfloat16
VMEM_LIMIT = 16 * 1024 * 1024
BLOCKED = -1e30
SMALL = pl.CostEstimate(flops=1000, bytes_accessed=1000, transcendentals=0)
HBM, VMEM = "hbm", "vmem"

NN = (((1,), (0,)), ((), ()))
NT = (((1,), (1,)), ((), ()))
TN = (((0,), (0,)), ((), ()))


def dot(a, b, dims):
    return lax.dot_general(a, b, dims, preferred_element_type=F32)


def split_dot(a, b, dims):
    high = b.astype(BF16)
    low = (b - high.astype(F32)).astype(BF16)
    return dot(a, high, dims) + dot(a, low, dims)


def iota(shape, dim):
    return lax.broadcasted_iota(jnp.int32, shape, dim)


def as_mask(condition):
    return jnp.where(condition, 1.0, 0.0).astype(BF16)


def step_rows(steps, k):
    n = CHUNK
    first = jnp.broadcast_to(steps[2 * k : 2 * k + 1], (n, n)).astype(BF16)
    second = jnp.broadcast_to(steps[2 * k + 1 : 2 * k + 2], (n, n)).astype(BF16)
    return first, second


def sums_and_steps():
    n = CHUNK
    lower = as_mask(iota((n, n), 0) >= iota((n, n), 1))
    eye = as_mask(iota((n, n), 0) == iota((n, n), 1))
    return jnp.concatenate([lower, eye], axis=0)


def step_columns(steps, k):
    n = CHUNK
    both = dot(sums_and_steps(), jnp.concatenate(step_rows(steps, k), axis=0), NT)
    return both[:n, :n], both[:n, n:], both[n:, :n], both[n:, n:]


def step_halves(steps, k):
    n = CHUNK
    first, second = step_rows(steps, k)
    halves = jnp.concatenate([first[: n // 2], second[: n // 2]], axis=0)
    both = dot(sums_and_steps(), halves, NT)
    return both[:n], both[n:], dot(halves, jnp.ones((n, n), BF16), NT)


def head_rows(k):
    rows, lanes = iota((8, CHUNK), 0), iota((8, CHUNK), 1)
    return as_mask(rows == 2 * k + (lanes >= CHUNK // 2).astype(jnp.int32))


def smem():
    return pl.BlockSpec(memory_space=pltpu.SMEM)


def vmem():
    return pl.BlockSpec(memory_space=pltpu.VMEM)


def hbm():
    return pl.BlockSpec(memory_space=pltpu.HBM)


def in_hbm(*arrays):
    return [pltpu.with_memory_space_constraint(array, pltpu.HBM) for array in arrays]


def hbm_out(shape, dtype):
    return pltpu.HBM(tuple(shape), dtype)


def slot_of(routes, target):
    slot = jnp.where(routes[1] == target, 1, jnp.where(routes[2] == target, 2, 0))
    return slot, (routes[0] == target) | (slot > 0)


def fetch(own_routes, peer_routes, place, s, own, peer, out, sem):
    target = place[0] * 2 + s
    own_slot, mine = slot_of(own_routes, target)
    peer_slot, _ = slot_of(peer_routes, target)

    @pl.when(mine)
    def _():
        pltpu.make_async_copy(own.at[own_slot], out, sem).start()

    @pl.when(jnp.logical_not(mine))
    def _():
        pltpu.make_async_copy(peer.at[peer_slot], out, sem).start()

    return pltpu.make_async_copy(own.at[0], out, sem)


def pick_maps_kernel(own_routes, peer_routes, place, ow, pw, orr, pr, out, sems):
    length = ow.shape[1]
    pending = []
    for s in range(2):
        for i, (own, peer) in enumerate(((ow, pw), (orr, pr))):
            part = out.at[i, s * length : (s + 1) * length]
            pending.append(
                fetch(own_routes, peer_routes, place, s, own, peer, part, sems.at[2 * s + i])
            )
    for copy in pending:
        copy.wait()


def pick_maps(own_routes, peer_routes, place, write, read, peer_write, peer_read):
    length, state = write.shape[1:]
    return pl.pallas_call(
        pick_maps_kernel,
        in_specs=[smem()] * 3 + [hbm()] * 4,
        out_specs=vmem(),
        out_shape=jax.ShapeDtypeStruct((2, 2 * length, state), BF16),
        scratch_shapes=[pltpu.SemaphoreType.DMA((4,))],
        compiler_params=pltpu.CompilerParams(vmem_limit_bytes=VMEM_LIMIT),
        name="pick_maps",
    )(own_routes, peer_routes, place, *in_hbm(write, peer_write, read, peer_read))


def to_groups(block, out):
    half = CHUNK // 2
    for g in range(GROUPS):
        a = block[:, g * half : (g + 1) * half]
        b = block[:, (GROUPS + g) * half : (GROUPS + g + 1) * half]
        out[g] = jnp.concatenate([a, b], axis=1)


def pick_values_kernel(
    own_routes, peer_routes, place, ox, px, os, ps, dy, x_out, s_out, dy_out,
    x_buf, s_buf, dy_buf, sems,
):
    length = ox.shape[1]
    pending = []
    for s in range(2):
        copy = pltpu.make_async_copy(dy.at[s], dy_buf.at[s], sems.at[3 * s])
        copy.start()
        steps = fetch(own_routes, peer_routes, place, s, os, ps, s_buf.at[s], sems.at[3 * s + 1])
        x = fetch(own_routes, peer_routes, place, s, ox, px, x_buf.at[s], sems.at[3 * s + 2])
        pending.append((copy, steps, x))
    for s in range(2):
        for copy in pending[s]:
            copy.wait()
        at = slice(s * length, (s + 1) * length)
        to_groups(dy_buf[s], dy_out.at[:, at])
        to_groups(x_buf[s], x_out.at[:, at])
        steps = s_buf[s].astype(F32)
        for q in range(2):
            for part in range(2):
                s_out[:, (2 * s + part) * 2 + q, :] = steps[
                    q * GROUPS : (q + 1) * GROUPS, part * CHUNK : (part + 1) * CHUNK
                ]


def pick_values(own_routes, peer_routes, place, values, peer_values, steps, peer_steps, upstream):
    length, columns = values.shape[1:]
    heads = steps.shape[1]
    return pl.pallas_call(
        pick_values_kernel,
        in_specs=[smem()] * 3 + [hbm()] * 5,
        out_specs=[vmem()] * 3,
        out_shape=[
            jax.ShapeDtypeStruct((GROUPS, 2 * length, CHUNK), BF16),
            jax.ShapeDtypeStruct((GROUPS, 8, CHUNK), F32),
            jax.ShapeDtypeStruct((GROUPS, 2 * length, CHUNK), BF16),
        ],
        scratch_shapes=[
            pltpu.VMEM((2, length, columns), BF16),
            pltpu.VMEM((2, heads, length), BF16),
            pltpu.VMEM((2, length, columns), BF16),
            pltpu.SemaphoreType.DMA((6,)),
        ],
        compiler_params=pltpu.CompilerParams(vmem_limit_bytes=VMEM_LIMIT),
        cost_estimate=SMALL,
        name="pick_values",
    )(
        own_routes, peer_routes, place,
        *in_hbm(values, peer_values, steps, peer_steps, upstream),
    )


def masks_kernel(ids, ids_rows, bias, enter, leave, flags):
    n = CHUNK
    eye = as_mask(iota((n, n), 0) == iota((n, n), 1))
    causal = iota((n, n), 0) >= iota((n, n), 1)
    for k in range(4):
        at = slice(k * n, (k + 1) * n)
        row = jnp.broadcast_to(ids_rows[:, at].astype(F32), (n, n))
        column = dot(eye, row.astype(BF16), NT)
        bias[at] = jnp.where((row == column) & causal, 0.0, BLOCKED)
        enter[at] = jnp.where(column == column[0:1], 0.0, BLOCKED)
        leave[at] = jnp.where(column == column[n - 1 : n], 0.0, BLOCKED)
        first, last = ids[0, k * n], ids[0, k * n + n - 1]
        linked = (k > 0) & (ids[0, max(k * n - 1, 0)] == first)
        flags[k] = jnp.where(linked, 1.0, 0.0)
        flags[4 + k] = jnp.where(first == last, 1.0, 0.0)
    flags[8] = ids[0, 0].astype(F32)
    flags[9] = ids[0, 4 * n - 1].astype(F32)


def make_masks(ids):
    wide = jax.ShapeDtypeStruct((4 * CHUNK, CHUNK), F32)
    return pl.pallas_call(
        masks_kernel,
        in_specs=[smem(), vmem()],
        out_specs=[vmem()] * 3 + [smem()],
        out_shape=[wide] * 3 + [jax.ShapeDtypeStruct((10,), F32)],
        compiler_params=pltpu.CompilerParams(vmem_limit_bytes=VMEM_LIMIT),
        cost_estimate=SMALL,
        name="make_masks",
    )(ids, ids)


CHUNKS = range(4)


def span_of(k):
    return slice(k * CHUNK, (k + 1) * CHUNK)


class Moves:
    def __init__(self, sems):
        self.sems, self.count = sems, 0

    def start(self, src, dst):
        copy = pltpu.make_async_copy(src, dst, self.sems.at[self.count])
        self.count += 1
        copy.start()
        return copy


def group_of(me, place, d):
    return lax.rem(me[0] + (2 * place[0] - 1) * d + GROUPS, GROUPS)


def head_lanes(per_head, g, axis):
    shape = (CHUNK, CHUNK)
    return jnp.where(iota(shape, axis) < CHUNK // 2, per_head[g], per_head[GROUPS + g])


def entering_group(g, rates, flags, maps, x_in, dy_in, steps, enter, leave, kept, send_out):
    (write, read), n, half = (maps.at[0], maps.at[1]), CHUNK, CHUNK // 2
    rate_lanes = head_lanes(rates, g, 1) * -LOG2E
    rate_rows = head_lanes(rates, g, 0) * -LOG2E
    columns = [step_halves(steps, k) for k in CHUNKS]
    u = [columns[k][0] * rate_lanes for k in CHUNKS]
    into = [jnp.exp2(u[k] + enter[span_of(k)]) for k in CHUNKS]
    out_of = [jnp.exp2(u[k][n - 1 : n] - u[k] + leave[span_of(k)]) for k in CHUNKS]
    rounded = [
        (x_in[g, span_of(k)].astype(F32) * columns[k][1]).astype(BF16).astype(F32) for k in CHUNKS
    ]
    scaled = [(rounded[k] * out_of[k]).astype(BF16) for k in CHUNKS]
    carried = [(dy_in[g, span_of(k)].astype(F32) * into[k]).astype(BF16) for k in CHUNKS]
    spans = [jnp.exp2(columns[k][2] * rate_rows) * flags[4 + k] for k in CHUNKS]
    yield
    locals_ = [dot(scaled[k], write[span_of(k)], TN) for k in CHUNKS]
    directs = [dot(carried[k], read[span_of(k)], TN) for k in CHUNKS]
    for k in CHUNKS:
        kept[0, span_of(k)] = locals_[k].astype(BF16)
        kept[1, span_of(k)] = directs[k].astype(BF16)
    end, span = locals_[0], spans[0]
    for k in range(1, 4):
        factor = spans[k] * flags[k]
        end = factor * end + locals_[k]
        span = factor * span
    begin = directs[3]
    for k in (2, 1, 0):
        begin = flags[k + 1] * spans[k] * begin + directs[k]
    row = iota((16, n), 0)
    for q in range(2):
        part = slice(q * half, (q + 1) * half)
        send_out[q, :half] = end[part].astype(BF16)
        send_out[q, half:n] = begin[part].astype(BF16)
        one = span[q * half : q * half + 1]
        rest = one - one.astype(BF16).astype(F32)
        ids = jnp.where(row == 2, flags[8], jnp.where(row == 3, flags[9], 0.0))
        meta = jnp.where(row == 0, one, jnp.where(row == 1, rest, ids))
        send_out[q, n:] = meta.astype(BF16)
    yield


def entering_kernel(tasks, me, place, rates, flags, *refs):
    count = len(tasks)
    maps_in, (x_in, dy_in, steps_in, enter, leave) = refs[:count], refs[count : count + 5]
    ends_all, sends_all, maps, ends, sends, sems = refs[-6:]
    moves = Moves(sems)
    loads = [moves.start(maps_in[i], maps.at[i]) for i in range(count)]
    stores = []
    for i, (spot, d) in enumerate(tasks):
        g = group_of(me, place, d)
        work = entering_group(
            g, rates, flags, maps.at[i], x_in, dy_in, steps_in[g], enter, leave, ends.at[i], sends.at[i]
        )
        next(work)
        loads[i].wait()
        next(work)
        stores.append(moves.start(ends.at[i], ends_all.at[spot]))
        stores.append(moves.start(sends.at[i], sends_all.at[2 * spot : 2 * spot + 2]))
    for store in stores:
        store.wait()


def call_on(kernel, scalars, arrays, so_far, out_shape, out_specs, scratch, copies, name):
    count = len(scalars) + len(arrays)
    operands = [array if spec is VMEM else in_hbm(array)[0] for array, spec in arrays]
    specs = [vmem() if spec is VMEM else hbm() for _, spec in arrays]
    return pl.pallas_call(
        kernel,
        in_specs=[smem()] * len(scalars) + specs + [hbm()] * len(so_far),
        out_specs=out_specs,
        out_shape=out_shape,
        input_output_aliases={count + i: i for i in range(len(so_far))},
        scratch_shapes=scratch + [pltpu.SemaphoreType.DMA((copies,))],
        compiler_params=pltpu.CompilerParams(vmem_limit_bytes=VMEM_LIMIT),
        cost_estimate=SMALL,
        name=name,
    )(*scalars, *operands, *in_hbm(*so_far))


def entering_part(tasks, me, place, rates, flags, pieces, x, dy, steps, enter, leave, so_far):
    count, tokens = len(tasks), x.shape[1]
    return call_on(
        functools.partial(entering_kernel, tasks),
        [me, place, rates, flags],
        [(pieces[d], HBM) for _, d in tasks] + [(v, VMEM) for v in (x, dy, steps, enter, leave)],
        so_far,
        [
            hbm_out((GROUPS, 2, tokens, CHUNK), BF16),
            hbm_out((2 * GROUPS, CHUNK + 16, CHUNK), BF16),
        ],
        [hbm()] * 2,
        [
            pltpu.VMEM((count, 2, tokens, CHUNK), BF16),
            pltpu.VMEM((count, 2, tokens, CHUNK), BF16),
            pltpu.VMEM((count, 2, CHUNK + 16, CHUNK), BF16),
        ],
        3 * count,
        "entering_part",
    )


def inner_group(g, rates, maps, x_in, dy_in, steps, bias, kept, rows):
    (write, read), n = (maps.at[0], maps.at[1]), CHUNK
    rate_a, rate_b = -rates[g] * LOG2E, -rates[GROUPS + g] * LOG2E
    low = iota((n, n), 1) < n // 2
    upper = as_mask(iota((n, n), 0) <= iota((n, n), 1))
    columns = [step_columns(steps, k) for k in CHUNKS]
    scores = [dot(read[span_of(k)], write[span_of(k)], NT) for k in CHUNKS]
    u_rows = dot(steps.astype(BF16), upper, NN) * jnp.where(
        iota((8, n), 0) % 2 == 0, rate_a, rate_b
    )
    x = [x_in[g, span_of(k)].astype(F32) for k in CHUNKS]
    dy = [dy_in[g, span_of(k)] for k in CHUNKS]
    stepped = [x[k] * jnp.where(low, columns[k][2], columns[k][3]) for k in CHUNKS]
    pair = [
        jnp.concatenate(
            [jnp.where(low, stepped[k], 0.0), jnp.where(low, 0.0, stepped[k])], axis=0
        ).astype(BF16)
        for k in CHUNKS
    ]
    rounded = [stepped[k].astype(BF16).astype(F32) for k in CHUNKS]
    d_weights = [dot(dy[k], pair[k], NT) for k in CHUNKS]
    falls, weights = [], []
    for k in CHUNKS:
        mask = bias[span_of(k)]
        falls.append(
            (
                jnp.exp2(columns[k][0] * rate_a - u_rows[2 * k : 2 * k + 1] + mask),
                jnp.exp2(columns[k][1] * rate_b - u_rows[2 * k + 1 : 2 * k + 2] + mask),
            )
        )
        weights.append(
            jnp.concatenate([falls[k][0] * scores[k], falls[k][1] * scores[k]], axis=1).astype(BF16)
        )
    inside = [dot(weights[k], pair[k], NN) for k in CHUNKS]
    d_pair = [dot(weights[k], dy[k], TN) for k in CHUNKS]
    d_scores = [
        (d_weights[k][:, :n] * falls[k][0] + d_weights[k][:, n:] * falls[k][1]).astype(BF16)
        for k in CHUNKS
    ]
    d_read = [dot(d_scores[k], write[span_of(k)], NN) for k in CHUNKS]
    d_write = [dot(d_scores[k], read[span_of(k)], TN) for k in CHUNKS]
    d_x = [jnp.where(low, d_pair[k][:n], d_pair[k][n:]) for k in CHUNKS]
    sums = [
        split_dot(head_rows(k), dy[k].astype(F32) * inside[k] - rounded[k] * d_x[k], NT)
        for k in CHUNKS
    ]
    rows[...] = (sums[0] + sums[1]) + (sums[2] + sums[3])
    for k in CHUNKS:
        for i, part in enumerate((inside, d_x, d_write, d_read)):
            kept[i, span_of(k)] = part[k].astype(BF16)


def inner_kernel(tasks, me, place, rates, *refs):
    count = len(tasks)
    maps_in, (x_in, dy_in, steps_in, bias) = refs[:count], refs[count : count + 4]
    kept_all, rows_all, maps, kept, rows, sems = refs[-6:]
    moves = Moves(sems)
    loads = [moves.start(maps_in[i], maps.at[i]) for i in range(count)]
    stores = []
    for i, (spot, d) in enumerate(tasks):
        g = group_of(me, place, d)
        loads[i].wait()
        inner_group(g, rates, maps.at[i], x_in, dy_in, steps_in[g], bias, kept.at[i], rows.at[i])
        stores.append(moves.start(kept.at[i], kept_all.at[spot]))
        stores.append(moves.start(rows.at[i], rows_all.at[spot]))
    for store in stores:
        store.wait()


def inner_part(tasks, me, place, rates, pieces, x, dy, steps, bias, so_far):
    count, tokens = len(tasks), x.shape[1]
    return call_on(
        functools.partial(inner_kernel, tasks),
        [me, place, rates],
        [(pieces[d], HBM) for _, d in tasks] + [(v, VMEM) for v in (x, dy, steps, bias)],
        so_far,
        [
            hbm_out((GROUPS, 4, tokens, CHUNK), BF16),
            hbm_out((GROUPS, 8, CHUNK), F32),
        ],
        [hbm()] * 2,
        [
            pltpu.VMEM((count, 2, tokens, CHUNK), BF16),
            pltpu.VMEM((count, 4, tokens, CHUNK), BF16),
            pltpu.VMEM((count, 8, CHUNK), F32),
        ],
        3 * count,
        "inner_part",
    )


def scan_kernel(got, out):
    half = CHUNK // 2
    count = got.shape[0]
    spans, links, last = [], [], None
    for i in range(count):
        meta = got[i, CHUNK:].astype(F32)
        spans.append(meta[0:1] + meta[1:2])
        same = jnp.zeros_like(meta[2:3]) if last is None else jnp.where(meta[2:3] == last, 1.0, 0.0)
        links.append(same)
        last = meta[3:4]
    state = jnp.zeros((half, CHUNK), F32)
    for i in range(count):
        used = links[i] * state
        out[i, :half] = used.astype(BF16)
        state = spans[i] * used + got[i, :half].astype(F32)
    state = jnp.zeros((half, CHUNK), F32)
    for i in range(count - 1, -1, -1):
        out[i, half:] = state.astype(BF16)
        state = links[i] * (spans[i] * state + got[i, half:CHUNK].astype(F32))


def scan_states(got):
    return pl.pallas_call(
        scan_kernel,
        in_specs=[vmem()],
        out_specs=vmem(),
        out_shape=jax.ShapeDtypeStruct((got.shape[0], CHUNK, CHUNK), BF16),
        compiler_params=pltpu.CompilerParams(vmem_limit_bytes=VMEM_LIMIT),
        name="scan_states",
    )(got)


def final_group(
    g, rates, gains, flags, states, maps, x_in, dy_in, steps, enter, leave, kept, rows_in, ends,
    y_out, dx_out, ds_out, d_maps, wait_first, wait_then
):
    (write, read), n, half = (maps.at[0], maps.at[1]), CHUNK, CHUNK // 2
    dw_out, dr_out = d_maps.at[0], d_maps.at[1]
    low = iota((n, n), 1) < half
    rate_lanes = head_lanes(rates, g, 1) * -LOG2E
    gain_lanes = head_lanes(gains, g, 1)
    rate_rows = head_lanes(rates, g, 0) * -LOG2E
    columns = [step_halves(steps, k) for k in CHUNKS]
    spans = [jnp.exp2(columns[k][2] * rate_rows) * flags[4 + k] for k in CHUNKS]
    step = [columns[k][1] for k in CHUNKS]
    u = [columns[k][0] * rate_lanes for k in CHUNKS]
    into = [jnp.exp2(u[k] + enter[span_of(k)]) for k in CHUNKS]
    out_of = [jnp.exp2(u[k][n - 1 : n] - u[k] + leave[span_of(k)]) for k in CHUNKS]
    wait_first()
    state = jnp.concatenate([states[0, :half], states[1, :half]], axis=0).astype(F32)
    used = [state]
    for k in range(3):
        state = flags[k + 1] * (spans[k] * state + ends[0, span_of(k)].astype(F32))
        used.append(state)
    after = jnp.concatenate([states[0, half:], states[1, half:]], axis=0).astype(F32)
    wanted = [after]
    for k in (3, 2, 1):
        after = flags[k] * (spans[k] * after + ends[1, span_of(k)].astype(F32))
        wanted.insert(0, after)
    used16 = [v.astype(BF16) for v in used]
    wanted16 = [v.astype(BF16) for v in wanted]
    cross = [dot(read[span_of(k)], used16[k], NT) for k in CHUNKS]
    back = [dot(write[span_of(k)], wanted16[k], NT) for k in CHUNKS]
    x = [x_in[g, span_of(k)].astype(F32) for k in CHUNKS]
    dy = [dy_in[g, span_of(k)].astype(F32) for k in CHUNKS]
    rounded = [(x[k] * step[k]).astype(BF16).astype(F32) for k in CHUNKS]
    d_read = [dot((dy[k] * into[k]).astype(BF16), used16[k], NN) for k in CHUNKS]
    d_write = [dot((rounded[k] * out_of[k]).astype(BF16), wanted16[k], NN) for k in CHUNKS]
    cross = [cross[k] * into[k] for k in CHUNKS]
    back = [back[k] * out_of[k] for k in CHUNKS]
    wait_then()
    d_x = [kept[1, span_of(k)].astype(F32) + back[k] for k in CHUNKS]
    select = [head_rows(k) for k in CHUNKS]
    from_all = [split_dot(select[k], spans[k] * wanted[k] * used[k], NN) for k in CHUNKS]
    sums = [split_dot(select[k], dy[k] * cross[k], NT) for k in CHUNKS]
    from_before = [split_dot(select[k], rounded[k] * back[k], NT) for k in CHUNKS]
    straight = [split_dot(select[k], x[k] * d_x[k], NT) for k in CHUNKS]
    for k in CHUNKS:
        at = span_of(k)
        y_out[at] = (kept[0, at].astype(F32) + cross[k] + gain_lanes * x[k]).astype(BF16)
        dx_out[at] = (step[k] * d_x[k] + gain_lanes * dy[k]).astype(BF16)
        dr_out[at] = (kept[3, at].astype(F32) + d_read[k]).astype(BF16)
        dw_out[at] = (kept[2, at].astype(F32) + d_write[k]).astype(BF16)
    lower = as_mask(iota((n, n), 0) >= iota((n, n), 1))
    before = as_mask(iota((n, n), 0) < iota((n, n), 1))
    every = lambda v: (v[0] + v[1]) + (v[2] + v[3])
    joined = jnp.concatenate([rows_in[...] + every(sums), every(from_before), every(from_all)], axis=1)
    table = jnp.concatenate([lower, before, jnp.ones((n, n), BF16)], axis=0)
    high = joined.astype(BF16)
    rest = joined - high.astype(F32)
    middle = rest.astype(BF16)
    low_part = (rest - middle.astype(F32)).astype(BF16)
    d_rate = dot(high, table, NN) + dot(middle, table, NN) + dot(low_part, table, NN)
    rates8 = jnp.where(iota((8, n), 0) % 2 == 0, rates[g], rates[GROUPS + g])
    ds_out[...] = every(straight) - rates8 * d_rate


def final_kernel(tasks, me, place, rates, gains, flags, *refs):
    count = len(tasks)
    maps_in = refs[:count]
    states_in, x_in, dy_in, steps_in, enter, leave, kept_in, rows_in, ends_in = refs[count : count + 9]
    y_all, dx_all, ds_all = refs[-11 - count : -8 - count]
    d_maps = refs[-8 - count : -8]
    maps, kept, rows, ends, y, dx, ds, sems = refs[-8:]
    moves = Moves(sems)
    first = [
        (
            moves.start(maps_in[i], maps.at[i]),
            moves.start(ends_in.at[spot], ends.at[i]),
        )
        for i, (spot, _) in enumerate(tasks)
    ]
    then = [
        (
            moves.start(kept_in.at[spot], kept.at[i]),
            moves.start(rows_in.at[spot], rows.at[i]),
        )
        for i, (spot, _) in enumerate(tasks)
    ]

    def wait_for(copies):
        def wait():
            for copy in copies:
                copy.wait()

        return wait

    stores = []
    for i, (spot, d) in enumerate(tasks):
        g = group_of(me, place, d)
        final_group(
            g, rates, gains, flags, states_in.at[2 * spot : 2 * spot + 2], maps.at[i], x_in, dy_in,
            steps_in[g], enter, leave, kept.at[i], rows.at[i], ends.at[i], y.at[i], dx.at[i], ds.at[i],
            d_maps[i], wait_for(first[i]), wait_for(then[i]),
        )
        stores.append(moves.start(y.at[i], y_all.at[g]))
        stores.append(moves.start(dx.at[i], dx_all.at[g]))
        stores.append(moves.start(ds.at[i], ds_all.at[g]))
    for store in stores:
        store.wait()


def final_part(
    tasks, me, place, rates, gains, flags, states, pieces, x, dy, steps, enter, leave, kept, rows, ends, so_far
):
    count, tokens = len(tasks), x.shape[1]
    wide = hbm_out(x.shape, BF16)
    d_maps = jax.ShapeDtypeStruct((2, tokens, CHUNK), BF16)
    outs = call_on(
        functools.partial(final_kernel, tasks),
        [me, place, rates, gains, flags],
        [(pieces[d], HBM) for _, d in tasks]
        + [(v, VMEM) for v in (states, x, dy, steps, enter, leave)]
        + [(v, HBM) for v in (kept, rows, ends)],
        so_far,
        [wide, wide, hbm_out(steps.shape, F32)] + [d_maps] * count,
        [hbm()] * 3 + [vmem()] * count,
        [
            pltpu.VMEM((count, 2, tokens, CHUNK), BF16),
            pltpu.VMEM((count, 4, tokens, CHUNK), BF16),
            pltpu.VMEM((count, 8, CHUNK), F32),
            pltpu.VMEM((count, 2, tokens, CHUNK), BF16),
            pltpu.VMEM((count, tokens, CHUNK), BF16),
            pltpu.VMEM((count, tokens, CHUNK), BF16),
            pltpu.VMEM((count, 8, CHUNK), F32),
        ],
        7 * count,
        "final_part",
    )
    return outs[:3], outs[3:]


def add_kernel(*refs):
    *terms, out = refs
    total = terms[0][...].astype(F32)
    for term in terms[1:]:
        total = total + term[...].astype(F32)
    out[...] = total.astype(BF16)


def add(*terms):
    return pl.pallas_call(
        add_kernel,
        in_specs=[vmem()] * len(terms),
        out_specs=vmem(),
        out_shape=jax.ShapeDtypeStruct(terms[0].shape, BF16),
        compiler_params=pltpu.CompilerParams(vmem_limit_bytes=VMEM_LIMIT),
        cost_estimate=SMALL,
        name="add",
    )(*terms)


def fetch_halves(src, dst, sems):
    length = src.shape[1] // 2
    loads = []
    for s in range(2):
        at = slice(s * length, (s + 1) * length)
        loads.append(pltpu.make_async_copy(src.at[:, at], dst.at[:, at], sems.at[s]))
        loads[s].start()
    return loads


def spread(groups, s, length, out):
    half = CHUNK // 2
    for g in range(GROUPS):
        block = groups[g, s * length : (s + 1) * length]
        out[s, :, g * half : (g + 1) * half] = block[:, :half]
        out[s, :, (GROUPS + g) * half : (GROUPS + g + 1) * half] = block[:, half:]


def output_columns_kernel(y_hbm, y_out, y_in, y_buf, sems):
    length = y_buf.shape[1]
    loads = fetch_halves(y_hbm, y_in, sems)
    copies = []
    for s in range(2):
        loads[s].wait()
        spread(y_in, s, length, y_buf)
        copies.append(pltpu.make_async_copy(y_buf.at[s], y_out.at[s], sems.at[2 + s]))
        copies[s].start()
    for copy in copies:
        copy.wait()


def output_columns(y):
    shape = (2, y.shape[1] // 2, GROUPS * CHUNK)
    return pl.pallas_call(
        output_columns_kernel,
        in_specs=[hbm()],
        out_specs=hbm(),
        out_shape=hbm_out(shape, BF16),
        scratch_shapes=[
            pltpu.VMEM(y.shape, BF16), pltpu.VMEM(shape, BF16), pltpu.SemaphoreType.DMA((4,))
        ],
        compiler_params=pltpu.CompilerParams(vmem_limit_bytes=VMEM_LIMIT),
        cost_estimate=SMALL,
        name="output_columns",
    )(*in_hbm(y))


def gradient_columns_kernel(dx_hbm, ds_in, dx_out, ds_out, dx_in, sems):
    length = dx_out.shape[1]
    loads = fetch_halves(dx_hbm, dx_in, sems)
    for s in range(2):
        for q in range(2):
            for part in range(2):
                ds_out[
                    s, q * GROUPS : (q + 1) * GROUPS, part * CHUNK : (part + 1) * CHUNK
                ] = ds_in[:, (2 * s + part) * 2 + q, :].astype(BF16)
    for s in range(2):
        loads[s].wait()
        spread(dx_in, s, length, dx_out)


def gradient_columns(dx, ds):
    length = dx.shape[1] // 2
    return pl.pallas_call(
        gradient_columns_kernel,
        in_specs=[hbm(), vmem()],
        out_specs=[vmem()] * 2,
        out_shape=[
            jax.ShapeDtypeStruct((2, length, GROUPS * CHUNK), BF16),
            jax.ShapeDtypeStruct((2, 2 * GROUPS, length), BF16),
        ],
        scratch_shapes=[pltpu.VMEM(dx.shape, BF16), pltpu.SemaphoreType.DMA((2,))],
        compiler_params=pltpu.CompilerParams(vmem_limit_bytes=VMEM_LIMIT),
        cost_estimate=SMALL,
        name="gradient_columns",
    )(*in_hbm(dx), ds)


def settle_kernel(count, routes, place, *refs):
    owns, peers, outs = refs[:count], refs[count : 2 * count], refs[2 * count : 3 * count]
    zeros, sems = refs[3 * count : 4 * count], refs[-1]
    for zero in zeros:
        zero[...] = jnp.zeros_like(zero)
    copies = []
    for m in range(3):
        target = routes[m]
        slot = lax.rem(jnp.maximum(target, 0), 2)
        mine = lax.div(target, 2) == place[0]
        for i in range(count):
            out, sem = outs[i].at[m], sems.at[m * count + i]

            @pl.when(target < 0)
            def _(zero=zeros[i], out=out, sem=sem):
                pltpu.make_async_copy(zero, out, sem).start()

            @pl.when((target >= 0) & mine)
            def _(own=owns[i], out=out, sem=sem):
                pltpu.make_async_copy(own.at[slot], out, sem).start()

            @pl.when((target >= 0) & jnp.logical_not(mine))
            def _(peer=peers[i], out=out, sem=sem):
                pltpu.make_async_copy(peer.at[slot], out, sem).start()

            copies.append(pltpu.make_async_copy(zeros[i], out, sem))
    for copy in copies:
        copy.wait()


def settle(routes, place, owns, peers):
    count = len(owns)
    return pl.pallas_call(
        functools.partial(settle_kernel, count),
        in_specs=[smem()] * 2 + [hbm()] * (2 * count),
        out_specs=[hbm()] * count,
        out_shape=[
            hbm_out((routes.shape[0],) + own.shape[1:], own.dtype) for own in owns
        ],
        scratch_shapes=[pltpu.VMEM(own.shape[1:], own.dtype) for own in owns]
        + [pltpu.SemaphoreType.DMA((3 * count,))],
        compiler_params=pltpu.CompilerParams(vmem_limit_bytes=VMEM_LIMIT),
        cost_estimate=SMALL,
        name="settle",
    )(routes, place, *owns, *peers)


def last_sum_kernel(a, b, c, out):
    length = out.shape[1] // 2
    for i in range(2):
        for s in range(2):
            at = slice(s * length, (s + 1) * length)
            total = a[i, at].astype(F32) + b[i, at].astype(F32) + c[i, at].astype(F32)
            out[s, i * length : (i + 1) * length] = total.astype(BF16)


def last_sum(a, b, c):
    return pl.pallas_call(
        last_sum_kernel,
        in_specs=[vmem()] * 3,
        out_specs=vmem(),
        out_shape=jax.ShapeDtypeStruct(a.shape, BF16),
        compiler_params=pltpu.CompilerParams(vmem_limit_bytes=VMEM_LIMIT),
        cost_estimate=SMALL,
        name="last_sum",
    )(a, b, c)


def settle_maps_kernel(routes, place, own, peer, write, read, zero, sems):
    length = write.shape[1]
    zero[...] = jnp.zeros_like(zero)
    copies = []
    for m in range(3):
        target = routes[m]
        slot = lax.rem(jnp.maximum(target, 0), 2)
        mine = lax.div(target, 2) == place[0]
        for i, result in enumerate((write, read)):
            out, sem, at = result.at[m], sems.at[2 * m + i], slice(i * length, (i + 1) * length)

            @pl.when(target < 0)
            def _(out=out, sem=sem):
                pltpu.make_async_copy(zero, out, sem).start()

            @pl.when((target >= 0) & mine)
            def _(out=out, sem=sem, at=at):
                pltpu.make_async_copy(own.at[slot, at], out, sem).start()

            @pl.when((target >= 0) & jnp.logical_not(mine))
            def _(out=out, sem=sem, at=at):
                pltpu.make_async_copy(peer.at[slot, at], out, sem).start()

            copies.append(pltpu.make_async_copy(zero, out, sem))
    for copy in copies:
        copy.wait()


def settle_maps(routes, place, own, peer):
    shape = (own.shape[1] // 2, own.shape[2])
    return pl.pallas_call(
        settle_maps_kernel,
        in_specs=[smem()] * 2 + [vmem()] * 2,
        out_specs=[hbm()] * 2,
        out_shape=[hbm_out((routes.shape[0],) + shape, BF16)] * 2,
        scratch_shapes=[pltpu.VMEM(shape, BF16), pltpu.SemaphoreType.DMA((6,))],
        compiler_params=pltpu.CompilerParams(vmem_limit_bytes=VMEM_LIMIT),
        cost_estimate=SMALL,
        name="settle_maps",
    )(routes, place, own, peer)


def after(operand, other):
    return lax.optimization_barrier((operand, other))[0]


def shards(
    values, step_sizes, write_map, read_map, decay_rates, skip_gain, routes, segment_ids, grad_out
):
    values, step_sizes = values[0, 0], step_sizes[0, 0]
    write_map, read_map, grad_out = write_map[0, 0], read_map[0, 0], grad_out[0, 0]
    routes = routes[0, 0]
    ring, stream = lax.axis_size("tensor"), lax.axis_size("ctx")
    swap = [(0, 1), (1, 0)]
    me = lax.axis_index("tensor").reshape(1)
    place = lax.axis_index("dp").reshape(1)

    def across(operand):
        return lax.ppermute(operand, "dp", swap)

    def turn(way):
        return [
            (core * ring + i, core * ring + (i + (way if core == 0 else -way)) % ring)
            for core in range(2)
            for i in range(ring)
        ]

    def go_first(operand):
        return lax.ppermute(operand, ("dp", "tensor"), turn(1))

    def go_second(operand):
        return lax.ppermute(operand, ("dp", "tensor"), turn(-1))

    peer_routes = across(routes)
    peer_write, peer_read = across(write_map), across(read_map)
    maps = pick_maps(routes, peer_routes, place, write_map, read_map, peer_write, peer_read)
    bias, enter, leave, flags = make_masks(segment_ids)
    peer_values, peer_steps = across(after(values, maps)), across(after(step_sizes, maps))
    x, steps, dy = pick_values(
        routes, peer_routes, place, values, peer_values, step_sizes, peer_steps, grad_out
    )

    arrival = (0, 1, -1, 2, -2, 3, -3, 4)
    spots = {d: i for i, d in enumerate(arrival)}
    pieces, ends = {0: maps}, []

    def entering(*groups):
        nonlocal ends
        ends = entering_part(
            [(spots[d], d) for d in groups], me, place, decay_rates, flags, pieces,
            x, dy, steps, enter, leave, ends,
        )
        return ends[1]

    pieces[1], pieces[-1] = go_first(maps), go_second(after(maps, bias))
    pieces[2], pieces[-2] = go_first(pieces[1]), go_second(after(pieces[-1], x))
    pieces[3] = go_first(after(pieces[2], entering(0)))
    done = entering(1)
    pieces[-3] = go_second(after(pieces[-2], done))
    pieces[4] = go_first(after(pieces[3], done))
    entering(-1, 2, -2)
    entering(3, -3)
    entering(4)

    inner = []

    def inside(groups, operand):
        nonlocal inner
        inner = inner_part(
            [(spots[d], d) for d in groups], me, place, decay_rates, pieces, operand, dy, steps, bias, inner
        )

    got = lax.all_to_all(ends[1], "ctx", split_axis=0, concat_axis=0, tiled=True)
    inside(arrival[:4], after(x, ends[1]))
    scanned = scan_states(after(got, inner[1]))
    states = lax.all_to_all(scanned, "ctx", split_axis=0, concat_axis=0, tiled=True)
    inside(arrival[4:], after(x, scanned))

    so_far = []

    def final(groups, other=None):
        nonlocal so_far
        operand = x if other is None else after(x, other)
        so_far, d_maps = final_part(
            [(spots[d], d) for d in groups], me, place, decay_rates, skip_gain, flags, states, pieces,
            operand, dy, steps, enter, leave, *inner, ends[0], so_far,
        )
        return d_maps

    (far,) = final((4,))
    far = go_first(far)
    up, down, here = final((-3, 3, 0))
    one, other = add(far, up), down
    one_sent, other_sent = go_first(one), go_second(other)
    up, down = final((-2, 2), (one, other))
    one, other = add(one_sent, up), add(other_sent, down)
    one_sent, other_sent = go_first(one), go_second(other)
    up, down = final((-1, 1), (one, other))
    one, other = add(one_sent, up), add(other_sent, down)
    one_sent, other_sent = go_first(one), go_second(other)
    y_all, dx_all, ds_all = so_far
    output = output_columns(after(y_all, (one, other)))
    grad_values, grad_steps = gradient_columns(
        *after((dx_all, ds_all), (one_sent, other_sent, output))
    )
    peer_values, peer_steps = across(grad_values), across(grad_steps)
    back_values, back_steps = settle(
        routes, place, [grad_values, grad_steps], [peer_values, peer_steps]
    )
    d_maps = last_sum(one_sent, other_sent, here)
    back_write, back_read = settle_maps(routes, place, d_maps, across(d_maps))
    return tuple(
        array[None, None] for array in (output, back_values, back_steps, back_write, back_read)
    )


def solution(mesh):
    placed = (
        P("dp", "ctx", None, None, "tensor"),
        P("dp", "ctx", None, "tensor", None),
        P("dp", "ctx", None, None, "tensor"),
        P("dp", "ctx", None, None, "tensor"),
        P("tensor"),
        P("tensor"),
        P("dp", "ctx", None),
        P("dp", "ctx"),
        P("dp", "ctx", None, None, "tensor"),
    )
    return jax.shard_map(
        shards,
        mesh=mesh,
        in_specs=placed,
        out_specs=(
            P("dp", "ctx", None, None, "tensor"),
            P("dp", "ctx", None, None, "tensor"),
            P("dp", "ctx", None, "tensor", None),
            P("dp", "ctx", None, None, "tensor"),
            P("dp", "ctx", None, None, "tensor"),
        ),
        check_vma=False,
    )
```
